32 devices in a mesh: seq: 8 (over z, x), head: 4 (over y, core).
Axes of the slice: x: 2, y: 2, z: 4, core: 2. Of those that a mesh axis runs over, the one named last changes fastest.
Arguments:
- inputs: bfloat16 [8, 2048, 768], P(None, 'seq'), may hold values from -6 to 6
- lengths: int32 [8], replicated, may hold values from 512 to 2048, as said below
- norm_gain: float32 [768], replicated, may hold values from 0.5 to 1.5
- in_proj: float32 [768, 3352], P(None, 'head'), may hold values from -0.21875 to 0.21875
- conv_weight: float32 [4, 1792], P(None, 'head'), may hold values from -3 to 3
- conv_bias: float32 [1792], P('head'), may hold values from -1.75 to 1.75
- head_params: float32 [3, 24], P(None, 'head'), may hold values from -9.2 to 1.5, as said below
- gate_gain: float32 [1536], P('head'), may hold values from 0.5 to 1.5
- out_proj: float32 [1536, 768], P('head'), may hold values from -0.15625 to 0.15625
- cotangent: bfloat16 [8, 2048, 768], P(None, 'seq'), may hold values from -6 to 6
- norm_gain_mom: float32 [768], replicated, may hold values from -384 to 384
- in_proj_mom: float32 [768, 3352], P('seq', 'head'), may hold values from -192 to 192
- conv_weight_mom: float32 [4, 1792], P(None, 'head'), may hold values from -384 to 384
- conv_bias_mom: float32 [1792], P('head'), may hold values from -384 to 384
- head_params_mom: float32 [3, 24], P(None, 'head'), may hold values from -384 to 384
- gate_gain_mom: float32 [1536], P('head'), may hold values from -384 to 384
- out_proj_mom: float32 [1536, 768], P('head', 'seq'), may hold values from -640 to 640
Outputs:
- output: bfloat16 [8, 2048, 768], P(None, 'seq')
- input_grad: float32 [8, 2048, 768], P(None, 'seq')
- norm_gain_grad: float32 [768], replicated
- in_proj_grad: float32 [768, 3352], P('seq', 'head')
- conv_weight_grad: float32 [4, 1792], P(None, 'head')
- conv_bias_grad: float32 [1792], P('head')
- head_params_grad: float32 [3, 24], P(None, 'head')
- gate_gain_grad: float32 [1536], P('head')
- out_proj_grad: float32 [1536, 768], P('head', 'seq')
- norm_gain_mom_new: float32 [768], replicated
- in_proj_mom_new: float32 [768, 3352], P('seq', 'head')
- conv_weight_mom_new: float32 [4, 1792], P(None, 'head')
- conv_bias_mom_new: float32 [1792], P('head')
- head_params_mom_new: float32 [3, 24], P(None, 'head')
- gate_gain_mom_new: float32 [1536], P('head')
- out_proj_mom_new: float32 [1536, 768], P('head', 'seq')
- norm_gain_new: float32 [768], replicated
- in_proj_new: float32 [768, 3352], P('seq', 'head')
- conv_weight_new: float32 [4, 1792], P(None, 'head')
- conv_bias_new: float32 [1792], P('head')
- head_params_new: float32 [3, 24], P(None, 'head')
- gate_gain_new: float32 [1536], P('head')
- out_proj_new: float32 [1536, 768], P('head', 'seq')
- rms: float32 [], replicated
The draws below stay inside these ranges and needn't reach their ends.
Inputs may be any that keep to these rules, and one draw needn't show every extreme that they name: `lengths`: each length lies between 512 and 2048; one sequence, which one drawn from the seed, fills all 2048 slots. `head_params`: row 0 holds dt biases, row 1 logarithms of decay rates, row 2 skip weights.
All inputs are finite; a program needn't handle non-finite values.
Results may differ from the reference program's by a relative error of at most 0.0083.
The reference program's roundings to bfloat16 on the way count: a program that leaves them out, or rounds other values in their place, can miss the bound.
Values may be sent and summed in bfloat16 or wider, within the bound.
No kernel may reach another device: no remote copies, remote signals or barrier semaphores. Data moves between devices by JAX's collectives and lax.ppermute only.
A program may use at most 448 MiB of HBM per device.

```python
import jax
import jax.numpy as jnp
from jax import lax

D = 768
HEADS = 24
HDIM = 64
NSTATE = 128
KCONV = 4
NS_STEPS = 5
SEQS = 8
INNER = 1536
PROJ = 3352
CONVCH = 1792
HG = 6
GCOLS = 838
CCH = 448
SEQ_LEN = 2048
N_HEAD = 4


def draw_lengths(key, part):
    key = jax.random.fold_in(key, 11)
    first_key, second_key = jax.random.split(key)
    drawn = jax.random.randint(first_key, (SEQS,), SEQ_LEN // 4, SEQ_LEN + 1)
    chosen = jax.random.randint(second_key, (), 0, SEQS)
    return jnp.where(jnp.arange(SEQS) == chosen, SEQ_LEN, drawn).astype(jnp.int32)


def draw_head_params(key, part):
    key = jax.random.fold_in(key, 23)
    bias_key, rate_key, skip_key = jax.random.split(key, 3)
    bias_row = jax.random.uniform(bias_key, (HEADS,), jnp.float32, -4.0, -2.0)
    rate_row = jax.random.uniform(rate_key, (HEADS,), jnp.float32, -9.2, 0.0)
    skip_row = jax.random.uniform(skip_key, (HEADS,), jnp.float32, 0.5, 1.5)
    return jnp.stack([bias_row, rate_row, skip_row]).astype(jnp.float32)


def levels(rng, shape, shards, least, largest):
    def one(position, shards_of):
        steps = jax.random.uniform(jax.random.fold_in(jax.random.fold_in(rng, 6), position), (shards_of,), jnp.float32, least / len(shards), largest / len(shards))
        return jnp.repeat(jnp.exp(steps), shape[position] // shards_of).reshape((-1,) + (1,) * (len(shape) - position - 1))

    level = one(*shards[0])
    for cut in shards[1:]:
        level = level * one(*cut)
    return level


def centred(stream_key, shape, width, bound, cuts=(), kind=jnp.bfloat16):
    gain = levels(stream_key, shape, cuts, -0.22, 0.18) if cuts else 1.0
    values = jax.random.normal(stream_key, shape, jnp.float32) * width * gain
    return jnp.minimum(jnp.maximum(values, -bound), bound).astype(kind)


def setup_inputs(seed: int = 0) -> dict:
    streams_of = jax.random.split(jax.random.key(seed), 18)
    return {
        "inputs": centred(streams_of[0], (SEQS, SEQ_LEN, D), 1.0, 6.0, ((1, 8),)),
        "lengths": draw_lengths(jax.random.fold_in(streams_of[17], 71), 0),
        "norm_gain": jnp.clip(1.0 + 0.1 * jax.random.normal(streams_of[2], (D,), jnp.float32), 0.5, 1.5),
        "in_proj": centred(streams_of[3], (D, PROJ), D ** -0.5, 0.21875, ((1, 4),), jnp.float32),
        "conv_weight": centred(streams_of[4], (KCONV, CONVCH), 0.5, 3.0, ((1, 4),), jnp.float32),
        "conv_bias": centred(streams_of[5], (CONVCH,), 0.3, 1.75, ((0, 4),), jnp.float32),
        "head_params": draw_head_params(jax.random.fold_in(streams_of[17], 71), 0),
        "gate_gain": jnp.clip(1.0 + 0.1 * jax.random.normal(streams_of[7], (INNER,), jnp.float32), 0.5, 1.5),
        "out_proj": centred(streams_of[8], (INNER, D), INNER ** -0.5, 0.15625, ((0, 4),), jnp.float32),
        "cotangent": centred(streams_of[9], (SEQS, SEQ_LEN, D), 1.0, 6.0, ((1, 8),)),
        "norm_gain_mom": centred(streams_of[10], (D,), (0.5 * (SEQS * SEQ_LEN) ** 0.5), 384.0, (), jnp.float32),
        "in_proj_mom": centred(streams_of[11], (D, PROJ), (0.25 * (SEQS * SEQ_LEN) ** 0.5), 192.0, ((0, 8), (1, 4)), jnp.float32),
        "conv_weight_mom": centred(streams_of[12], (KCONV, CONVCH), (0.5 * (SEQS * SEQ_LEN) ** 0.5), 384.0, ((1, 4),), jnp.float32),
        "conv_bias_mom": centred(streams_of[13], (CONVCH,), (0.5 * (SEQS * SEQ_LEN) ** 0.5), 384.0, ((0, 4),), jnp.float32),
        "head_params_mom": centred(streams_of[14], (3, HEADS), (0.5 * (SEQS * SEQ_LEN) ** 0.5), 384.0, ((1, 4),), jnp.float32),
        "gate_gain_mom": centred(streams_of[15], (INNER,), (0.5 * (SEQS * SEQ_LEN) ** 0.5), 384.0, ((0, 4),), jnp.float32),
        "out_proj_mom": centred(streams_of[16], (INNER, D), (0.8 * (SEQS * SEQ_LEN) ** 0.5), 640.0, ((0, 4), (1, 8)), jnp.float32),
    }


@jax.custom_vjp
def low(v):
    return lax.optimization_barrier(v.astype(jnp.bfloat16)).astype(jnp.float32)

@jax.custom_vjp
def low_back(v):
    return v

def low_keep(v):
    return (low(v), None)

def low_pass(kept, grad):
    return (grad,)

def back_keep(v):
    return (v, None)

def back_low(kept, grad):
    return (low(grad),)
low.defvjp(low_keep, low_pass)
low_back.defvjp(back_keep, back_low)
EPSILON = 1e-05
COEF_A = 3.4445
COEF_B = -4.775
COEF_C = 2.0315
MUON_RATE = 0.2
SMALL_RATE = 0.2
PRECISE = lax.Precision.HIGHEST

def silu(values):
    return values * jax.nn.sigmoid(values)

def stretch_update(carry, pieces):
    state, decay_rate = carry
    x_block, step_block, b_block, c_block = pieces
    cumulative = jnp.cumsum(step_block * decay_rate, axis=1)
    extent = step_block.shape[1]
    row_index = lax.broadcasted_iota(jnp.int32, (extent, extent), 0)
    col_index = lax.broadcasted_iota(jnp.int32, (extent, extent), 1)
    causal = (row_index >= col_index)[None, :, :, None]
    gaps = cumulative[:, :, None, :] - cumulative[:, None, :, :]
    kernel = jnp.exp(jnp.where(causal, gaps, -1e+30))
    scores = jnp.einsum('btn,bsn->bts', c_block, b_block, precision=PRECISE)
    mixing = kernel * scores[..., None] * step_block[:, None, :, :]
    inner = jnp.einsum('btsh,bshp->bthp', mixing, x_block, precision=PRECISE)
    carried = jnp.einsum('btn,bhpn->bthp', c_block, state, precision=PRECISE) * jnp.exp(cumulative)[..., None]
    tail_weight = jnp.exp(cumulative[:, -1:, :] - cumulative) * step_block
    fresh = jnp.einsum('bsh,bshp,bsn->bhpn', tail_weight, x_block, b_block, precision=PRECISE)
    state = jnp.exp(cumulative[:, -1, :])[:, :, None, None] * state + fresh
    return ((state, decay_rate), inner + carried)

def state_scan(x_part, step_sizes, b_matrix, c_matrix, decay_rate):
    batch_seqs, extent = (step_sizes.shape[0], step_sizes.shape[1])
    block_size = min(extent, 256)
    block_count = extent // block_size

    def split_blocks(values):
        shaped = values.reshape((batch_seqs, block_count, block_size) + values.shape[2:])
        return jnp.moveaxis(shaped, 1, 0)
    start = jnp.zeros((batch_seqs, x_part.shape[2], x_part.shape[3], b_matrix.shape[2]), jnp.float32)
    carry_out, outputs = lax.scan(jax.checkpoint(stretch_update), (start, decay_rate), (split_blocks(x_part), split_blocks(step_sizes), split_blocks(b_matrix), split_blocks(c_matrix)))
    return jnp.moveaxis(outputs, 0, 1).reshape(x_part.shape)

def forward(data, norm_gain, in_proj, conv_weight, conv_bias, head_params, gate_gain, out_proj, valid_mask):
    batch_seqs, extent = (data.shape[0], data.shape[1])
    head_span = HG * HDIM
    normed = data * lax.rsqrt(lax.optimization_barrier(jnp.mean(data * data, axis=-1, keepdims=True)) + EPSILON)
    lowered = low(normed * norm_gain)
    projected = low_back(jnp.einsum('bld,dk->blk', lowered, low(in_proj), precision=PRECISE))
    groups = projected.reshape(batch_seqs, extent, N_HEAD, GCOLS)
    z_part = groups[..., :head_span].reshape(batch_seqs, extent, INNER)
    conv_in = low(groups[..., head_span:head_span + CCH]).reshape(batch_seqs, extent, CONVCH)
    raw_steps = groups[..., head_span + CCH:].reshape(batch_seqs, extent, HEADS)
    padded = jnp.pad(conv_in, ((0, 0), (KCONV - 1, 0), (0, 0)))
    conv_out = conv_bias + jnp.zeros_like(conv_in)
    for offset in range(KCONV):
        conv_out = conv_out + conv_weight[offset] * padded[:, offset:offset + extent]
    conv_out = low_back(conv_out)
    activated = silu(conv_out).reshape(batch_seqs, extent, N_HEAD, CCH)
    x_heads = activated[..., :head_span].reshape(batch_seqs, extent, HEADS, HDIM)
    bc_values = low(activated[..., head_span:]).reshape(batch_seqs, extent, 2 * NSTATE)
    b_matrix = bc_values[..., :NSTATE]
    c_matrix = bc_values[..., NSTATE:]
    step_sizes = jax.nn.softplus(raw_steps + head_params[0])
    decay_rate = -jnp.exp(head_params[1])
    mixed = state_scan(x_heads, step_sizes, b_matrix, c_matrix, decay_rate) + head_params[2][:, None] * x_heads
    gated = mixed.reshape(batch_seqs, extent, INNER) * silu(z_part)
    norm_scale = lax.rsqrt(lax.optimization_barrier(jnp.mean(gated * gated, axis=-1, keepdims=True)) + EPSILON)
    summed = low_back(jnp.einsum('blk,kd->bld', low(gated * gate_gain), low(out_proj), precision=PRECISE))
    return valid_mask * (data + norm_scale * summed)

def orthogonal(matrix):
    ortho = matrix / (jnp.sqrt(jnp.sum(matrix * matrix)) + 1e-07)
    for iteration in range(NS_STEPS):
        gram = jnp.dot(ortho, ortho.T, precision=PRECISE)
        poly = COEF_B * gram + COEF_C * jnp.dot(gram, gram, precision=PRECISE)
        ortho = COEF_A * ortho + jnp.dot(poly, ortho, precision=PRECISE)
    return ortho

def reference(inputs, lengths, norm_gain, in_proj, conv_weight, conv_bias, head_params, gate_gain, out_proj, cotangent, norm_gain_mom, in_proj_mom, conv_weight_mom, conv_bias_mom, head_params_mom, gate_gain_mom, out_proj_mom):
    positions = lax.broadcasted_iota(jnp.int32, (SEQS, SEQ_LEN), 1)
    valid_mask = (positions < lengths[:, None]).astype(jnp.float32)[..., None]
    data = inputs.astype(jnp.float32)

    def closed(data_in, gain_a, in_w, conv_w, conv_b, head_p, gain_b, out_w):
        return forward(data_in, gain_a, in_w, conv_w, conv_b, head_p, gain_b, out_w, valid_mask)
    result, pullback = jax.vjp(closed, data, norm_gain, in_proj, conv_weight, conv_bias, head_params, gate_gain, out_proj)
    grads = pullback(cotangent.astype(jnp.float32))
    output = result.astype(jnp.bfloat16)
    rms = jnp.sqrt(jnp.sum(result * result) / (jnp.sum(lengths).astype(jnp.float32) * D))
    weights = (norm_gain, in_proj, conv_weight, conv_bias, head_params, gate_gain, out_proj)
    moments = (norm_gain_mom, in_proj_mom, conv_weight_mom, conv_bias_mom, head_params_mom, gate_gain_mom, out_proj_mom)
    weight_grads = grads[1:]
    moments_new = tuple((0.5 * old + grad for old, grad in zip(moments, weight_grads)))
    divisor = (SEQS * SEQ_LEN) ** 0.5
    fresh = [old - SMALL_RATE * mom / divisor for old, mom in zip(weights, moments_new)]
    fresh[1] = in_proj - MUON_RATE * 0.2 * max(D, PROJ) ** 0.5 * orthogonal(moments_new[1])
    fresh[6] = out_proj - MUON_RATE * 0.2 * max(INNER, D) ** 0.5 * orthogonal(moments_new[6].T).T
    return (output, grads[0], weight_grads[0], weight_grads[1], weight_grads[2], weight_grads[3], weight_grads[4], weight_grads[5], weight_grads[6], moments_new[0], moments_new[1], moments_new[2], moments_new[3], moments_new[4], moments_new[5], moments_new[6], fresh[0], fresh[1], fresh[2], fresh[3], fresh[4], fresh[5], fresh[6], rms)
```

```python
import math

import jax
import jax.numpy as jnp
from jax import lax
from jax.sharding import PartitionSpec as P

NS_STEPS = 5
EPSILON = 1e-05
COEF_A = 3.4445
COEF_B = -4.775
COEF_C = 2.0315
MUON_RATE = 0.2
SMALL_RATE = 0.2
PRECISE = lax.Precision.HIGHEST
BF = jnp.bfloat16
F32 = jnp.float32


def silu(values):
    return values * jax.nn.sigmoid(values)


def silu_slope(values):
    sigmoid_value = jax.nn.sigmoid(values)
    return sigmoid_value * (1.0 + values * (1.0 - sigmoid_value))


def flip(value, axis, bit):
    count = lax.axis_size(axis)
    return lax.ppermute(value, axis, [(i, i ^ bit) for i in range(count)])


def sum_over(value, axis):
    bit = 1
    while bit < lax.axis_size(axis):
        value = jax.tree.map(lambda part: part + flip(part, axis, bit), value)
        bit *= 2
    return value


def pick(stacked, index, axis):
    return lax.dynamic_index_in_dim(stacked, index, axis, keepdims=False)


def gather_head(piece, axis):
    place = lax.axis_index("head")
    across = flip(piece, "head", 2)
    beside = flip(piece, "head", 1)
    corner = flip(across, "head", 1)
    low, high = place % 2, place // 2
    near = jnp.where(low == 0, jnp.stack([piece, beside], axis), jnp.stack([beside, piece], axis))
    far = jnp.where(low == 0, jnp.stack([across, corner], axis), jnp.stack([corner, across], axis))
    return jnp.where(
        high == 0, jnp.concatenate([near, far], axis), jnp.concatenate([far, near], axis)
    )


def scatter_head(parts, axis, wire):
    place = lax.axis_index("head")
    low, high = place % 2, place // 2
    shape = parts.shape
    parts = parts.reshape(shape[:axis] + (2, 2) + shape[axis + 1 :])
    half = pick(parts, low, axis + 1) + flip(pick(parts, 1 - low, axis + 1), "head", 1)
    sent = flip(pick(half, 1 - high, axis).astype(wire), "head", 2)
    return pick(half, high, axis) + sent.astype(F32)


def spread(blocks, members):
    count = lax.axis_size("seq")
    runs = [list(range(i, i + members)) for i in range(0, count, members)]
    return lax.all_to_all(
        blocks, "seq", 0, 0, tiled=True, axis_index_groups=runs if len(runs) > 1 else None
    )


def stretch_update(carry, pieces):
    state, decay_rate = carry
    x_block, step_block, b_block, c_block = pieces
    cumulative = jnp.cumsum(step_block * decay_rate, axis=1)
    extent = step_block.shape[1]
    row_index = lax.broadcasted_iota(jnp.int32, (extent, extent), 0)
    col_index = lax.broadcasted_iota(jnp.int32, (extent, extent), 1)
    causal = (row_index >= col_index)[None, :, :, None]
    gaps = cumulative[:, :, None, :] - cumulative[:, None, :, :]
    kernel = jnp.exp(jnp.where(causal, gaps, -1e30))
    scores = jnp.einsum("btn,bsn->bts", c_block, b_block, precision=PRECISE)
    mixing = kernel * scores[..., None] * step_block[:, None, :, :]
    inner = jnp.einsum("btsh,bshp->bthp", mixing, x_block, precision=PRECISE)
    carried = (
        jnp.einsum("btn,bhpn->bthp", c_block, state, precision=PRECISE)
        * jnp.exp(cumulative)[..., None]
    )
    tail_weight = jnp.exp(cumulative[:, -1:, :] - cumulative) * step_block
    fresh = jnp.einsum("bsh,bshp,bsn->bhpn", tail_weight, x_block, b_block, precision=PRECISE)
    state = jnp.exp(cumulative[:, -1, :])[:, :, None, None] * state + fresh
    return ((state, decay_rate), inner + carried)


def local_scan(x_part, step_sizes, b_matrix, c_matrix, decay_rate, skip_weight, start):
    batch_seqs, extent = (step_sizes.shape[0], step_sizes.shape[1])
    block_size = min(extent, 256)
    block_count = extent // block_size

    def split_blocks(values):
        shaped = values.reshape((batch_seqs, block_count, block_size) + values.shape[2:])
        return jnp.moveaxis(shaped, 1, 0)

    carry_out, outputs = lax.scan(
        jax.checkpoint(stretch_update),
        (start, decay_rate),
        (
            split_blocks(x_part),
            split_blocks(step_sizes),
            split_blocks(b_matrix),
            split_blocks(c_matrix),
        ),
    )
    mixed = jnp.moveaxis(outputs, 0, 1).reshape(x_part.shape) + skip_weight[:, None] * x_part
    return mixed, carry_out[0]


def entering(growth, state, members, backward):
    count = lax.axis_size("seq")
    runs = count // members
    mine = lax.axis_index("seq") // members
    step = -members if backward else members
    pairs = [(i, i + step) for i in range(count) if 0 <= i + step < count]
    total = jnp.zeros_like(state)
    for _ in range(runs - 1):
        total = lax.ppermute(growth * total + state, "seq", pairs)
    return total


def orthogonal_rows(matrix, row_start, row_count):
    gram = jnp.dot(matrix, matrix.T, precision=PRECISE)
    gram = sum_over(gram, "head")
    size = jnp.trace(gram)
    factor = 1.0 / (jnp.sqrt(size) + 1e-07)
    gram = gram * (factor * factor)
    eye = jnp.eye(gram.shape[0], dtype=F32)
    polys = []
    for iteration in range(NS_STEPS):
        square = jnp.dot(gram, gram, precision=PRECISE)
        poly = COEF_A * eye + COEF_B * gram + COEF_C * square
        polys.append(poly)
        if iteration + 1 < NS_STEPS:
            image = COEF_A * gram + COEF_B * square
            image = image + COEF_C * jnp.dot(square, gram, precision=PRECISE)
            gram = jnp.dot(image, poly, precision=PRECISE)
    rows = lax.dynamic_slice_in_dim(polys[-1], row_start, row_count, 0)
    for poly in polys[-2::-1]:
        rows = jnp.dot(rows, poly, precision=PRECISE)
    return jnp.dot(rows, matrix, precision=PRECISE) * factor


def per_device(
    inputs,
    lengths,
    norm_gain,
    in_proj,
    conv_weight,
    conv_bias,
    head_params,
    gate_gain,
    out_proj,
    cotangent,
    norm_gain_mom,
    in_proj_mom,
    conv_weight_mom,
    conv_bias_mom,
    head_params_mom,
    gate_gain_mom,
    out_proj_mom,
):
    members, extent, model_width = inputs.shape
    seq_count = lax.axis_size("seq")
    head_count = lax.axis_size("head")
    seq_place = lax.axis_index("seq")
    head_place = lax.axis_index("head")
    heads_here = head_params.shape[1]
    head_span = gate_gain.shape[0]
    head_size = head_span // heads_here
    channels = conv_bias.shape[0]
    state_size = (channels - head_span) * head_count // 2
    inner_all = head_span * head_count
    group_cols = in_proj.shape[1]
    proj_all = group_cols * head_count
    tap_count = conv_weight.shape[0]
    share = model_width // seq_count
    tokens = members * extent
    quarter = extent // head_count
    runs = seq_count // members

    def to_sequence(blocks):
        piece = lax.dynamic_slice_in_dim(blocks, head_place * quarter, quarter, 1)
        piece = spread(piece, members)
        return piece, gather_head(piece, 1).reshape(tokens, -1)

    def from_sequence(piece):
        return gather_head(spread(piece.astype(BF), members), 1).reshape(inputs.shape)

    def own(per_token):
        return pick(per_token.reshape((members, head_count, quarter, -1)), head_place, 1)

    data_piece, data = to_sequence(inputs)
    cot_piece, cot = to_sequence(cotangent)
    data_piece, data = data_piece.astype(F32), data.astype(F32)
    run_place = seq_place // members
    positions = run_place * tokens + lax.broadcasted_iota(jnp.int32, (tokens, 1), 0)
    valid_mask = (positions < lengths[seq_place % members]).astype(F32)
    root_scale = lax.rsqrt(jnp.mean(data * data, axis=-1, keepdims=True) + EPSILON)
    normed = data * root_scale
    lowered = (normed * norm_gain).astype(BF)
    in_low = in_proj.astype(BF)
    projected = jnp.dot(lowered, in_low, preferred_element_type=F32)
    z_part = projected[:, :head_span]
    conv_in = projected[:, head_span : head_span + channels].astype(BF)
    raw_steps = projected[:, head_span + channels :]
    halo = tap_count - 1

    def from_run(edge, step):
        if runs == 1:
            return jnp.zeros_like(edge)
        pairs = [(i, i + step) for i in range(seq_count) if 0 <= i + step < seq_count]
        return lax.ppermute(edge, "seq", pairs)

    padded = jnp.concatenate([from_run(conv_in[tokens - halo :], members), conv_in], axis=0)
    conv_out = conv_bias + jnp.zeros(conv_in.shape, F32)
    for offset in range(tap_count):
        conv_out = conv_out + conv_weight[offset] * padded[offset : offset + tokens]
    activated = silu(conv_out)
    x_heads = activated[:, :head_span].reshape(1, tokens, heads_here, head_size)
    bc_local = activated[:, head_span:].astype(BF)
    bc_full = gather_head(bc_local.T, 0).reshape(2 * state_size, tokens).T.astype(F32)
    b_matrix = bc_full[None, :, :state_size]
    c_matrix = bc_full[None, :, state_size:]
    pre_steps = raw_steps + head_params[0]
    step_sizes = jax.nn.softplus(pre_steps)
    decay_rate = -jnp.exp(head_params[1])
    growth = jnp.exp(jnp.sum(step_sizes, axis=0) * decay_rate)[None, :, None, None]
    start = jnp.zeros((1, heads_here, head_size, state_size), F32)
    scan_args = (x_heads, step_sizes[None], b_matrix, c_matrix, decay_rate, head_params[2])
    if runs > 1:
        start = entering(growth, local_scan(*scan_args, start)[1], members, False)
    (mixed, state_end), pullback = jax.vjp(local_scan, *scan_args, start)
    mixed_flat = mixed.reshape(tokens, head_span)
    gate_value = silu(z_part)
    gated = mixed_flat * gate_value
    squares = jnp.sum(gated * gated, axis=-1)
    gated_low = (gated * gate_gain).astype(BF)
    out_low = out_proj.astype(BF)
    partial_out = jnp.dot(gated_low, out_low, preferred_element_type=F32)
    back_grad = cot.astype(F32) * valid_mask
    partial_scale = jnp.sum(back_grad * partial_out, axis=-1)
    square_sum, grad_scale = sum_over(jnp.stack([squares, partial_scale]), "head")
    norm_scale = lax.rsqrt(square_sum / inner_all + EPSILON)[:, None]
    grad_scale = grad_scale[:, None]
    summed = scatter_head(partial_out.reshape(members, head_count, quarter, -1), 1, BF)
    result = own(valid_mask) * (data_piece + own(norm_scale) * summed)
    output = from_sequence(result)
    result_squares = jnp.sum(result * result)
    grad_summed = (norm_scale * back_grad).astype(BF)
    grad_low = jnp.dot(grad_summed, out_low.T, preferred_element_type=F32)
    grad_gated = (
        grad_low * gate_gain - grad_scale * norm_scale * norm_scale * norm_scale * gated / inner_all
    )
    gate_gain_grad = jnp.sum(grad_low * gated, axis=0)
    grad_mixed = (grad_gated * gate_value).reshape(x_heads.shape)
    grad_z = grad_gated * mixed_flat * silu_slope(z_part)
    state_back = jnp.zeros_like(state_end)
    if runs > 1:
        state_back = entering(growth, pullback((grad_mixed, state_back))[6], members, True)
    grad_x, grad_steps, grad_b, grad_c, grad_rate, grad_skip, _ = pullback((grad_mixed, state_back))
    grad_bc = jnp.concatenate([grad_b[0], grad_c[0]], axis=-1).T
    grad_bc_local = scatter_head(grad_bc.reshape(head_count, -1, tokens), 0, F32).T
    grad_pre = grad_steps[0] * jax.nn.sigmoid(pre_steps)
    head_params_grad = jnp.stack([jnp.sum(grad_pre, axis=0), grad_rate * decay_rate, grad_skip])
    grad_activated = jnp.concatenate([grad_x.reshape(tokens, head_span), grad_bc_local], axis=-1)
    grad_conv = (grad_activated * silu_slope(conv_out)).astype(BF)
    trailing = jnp.concatenate([grad_conv, from_run(grad_conv[:halo], -members)], axis=0)
    grad_conv_wide = grad_conv.astype(F32)
    grad_conv_in = jnp.zeros(conv_in.shape, F32)
    tap_grads = []
    for offset in range(tap_count):
        lead = tap_count - 1 - offset
        grad_conv_in = grad_conv_in + conv_weight[offset] * trailing[lead : lead + tokens]
        tap_grads.append(jnp.sum(grad_conv_wide * padded[offset : offset + tokens], axis=0))
    conv_weight_grad = jnp.stack(tap_grads)
    conv_bias_grad = jnp.sum(grad_conv_wide, axis=0)
    grad_projected = jnp.concatenate([grad_z, grad_conv_in, grad_pre], axis=-1).astype(BF)
    partial_in = jnp.dot(grad_projected, in_low.T, preferred_element_type=F32)
    grad_lowered = scatter_head(partial_in.reshape(members, head_count, quarter, -1), 1, BF)
    root_piece = own(root_scale)
    normed_piece = data_piece * root_piece
    norm_gain_grad = jnp.sum(grad_lowered * normed_piece, axis=(0, 1))
    grad_normed = grad_lowered * norm_gain
    input_grad = own(back_grad) + root_piece * (
        grad_normed - normed_piece * jnp.mean(grad_normed * normed_piece, axis=-1, keepdims=True)
    )
    input_grad = from_sequence(input_grad).astype(F32)
    term_in = jnp.dot(lowered.T, grad_projected, preferred_element_type=F32)
    term_out = jnp.dot(grad_summed.T, gated_low, preferred_element_type=F32)
    out_grad_rows = lax.psum_scatter(term_out, "seq", scatter_dimension=0, tiled=True)
    in_proj_grad = lax.psum_scatter(term_in, "seq", scatter_dimension=0, tiled=True)
    norm_gain_grad, result_squares = sum_over((norm_gain_grad, result_squares), "head")
    (
        norm_gain_grad,
        conv_weight_grad,
        conv_bias_grad,
        head_params_grad,
        gate_gain_grad,
        squares_all,
    ) = sum_over(
        (
            norm_gain_grad,
            conv_weight_grad,
            conv_bias_grad,
            head_params_grad,
            gate_gain_grad,
            result_squares,
        ),
        "seq",
    )
    rms = jnp.sqrt(squares_all / (jnp.sum(lengths).astype(F32) * model_width))
    in_proj_mom_new = 0.5 * in_proj_mom + in_proj_grad
    out_rows_mom = 0.5 * out_proj_mom.T + out_grad_rows
    full_out = lax.all_gather(out_rows_mom, "seq", axis=0, tiled=True)
    full_in = lax.all_gather(in_proj_mom_new, "seq", axis=0, tiled=True)
    rows_out = orthogonal_rows(full_out, seq_place * share, share)
    rows_in = orthogonal_rows(full_in, seq_place * share, share)
    in_old_rows = lax.dynamic_slice_in_dim(in_proj, seq_place * share, share, 0)
    in_proj_new = in_old_rows - MUON_RATE * 0.2 * math.sqrt(max(model_width, proj_all)) * rows_in
    out_old_cols = lax.dynamic_slice_in_dim(out_proj, seq_place * share, share, 1)
    out_proj_new = (
        out_old_cols - MUON_RATE * 0.2 * math.sqrt(max(inner_all, model_width)) * rows_out.T
    )
    divisor = math.sqrt(members * extent * seq_count)
    norm_gain_mom_new = 0.5 * norm_gain_mom + norm_gain_grad
    conv_weight_mom_new = 0.5 * conv_weight_mom + conv_weight_grad
    conv_bias_mom_new = 0.5 * conv_bias_mom + conv_bias_grad
    head_params_mom_new = 0.5 * head_params_mom + head_params_grad
    gate_gain_mom_new = 0.5 * gate_gain_mom + gate_gain_grad
    norm_gain_new = norm_gain - SMALL_RATE * norm_gain_mom_new / divisor
    conv_weight_new = conv_weight - SMALL_RATE * conv_weight_mom_new / divisor
    conv_bias_new = conv_bias - SMALL_RATE * conv_bias_mom_new / divisor
    head_params_new = head_params - SMALL_RATE * head_params_mom_new / divisor
    gate_gain_new = gate_gain - SMALL_RATE * gate_gain_mom_new / divisor
    return (
        output,
        input_grad,
        norm_gain_grad,
        in_proj_grad,
        conv_weight_grad,
        conv_bias_grad,
        head_params_grad,
        gate_gain_grad,
        out_grad_rows.T,
        norm_gain_mom_new,
        in_proj_mom_new,
        conv_weight_mom_new,
        conv_bias_mom_new,
        head_params_mom_new,
        gate_gain_mom_new,
        out_rows_mom.T,
        norm_gain_new,
        in_proj_new,
        conv_weight_new,
        conv_bias_new,
        head_params_new,
        gate_gain_new,
        out_proj_new,
        rms,
    )


def solution(mesh):
    return jax.shard_map(
        per_device,
        mesh=mesh,
        in_specs=(
            P(None, "seq", None),
            P(),
            P(),
            P(None, "head"),
            P(None, "head"),
            P("head"),
            P(None, "head"),
            P("head"),
            P("head", None),
            P(None, "seq", None),
            P(),
            P("seq", "head"),
            P(None, "head"),
            P("head"),
            P(None, "head"),
            P("head"),
            P("head", "seq"),
        ),
        out_specs=(
            P(None, "seq", None),
            P(None, "seq", None),
            P(),
            P("seq", "head"),
            P(None, "head"),
            P("head"),
            P(None, "head"),
            P("head"),
            P("head", "seq"),
            P(),
            P("seq", "head"),
            P(None, "head"),
            P("head"),
            P(None, "head"),
            P("head"),
            P("head", "seq"),
            P(),
            P("seq", "head"),
            P(None, "head"),
            P("head"),
            P(None, "head"),
            P("head"),
            P("head", "seq"),
            P(),
        ),
        check_vma=False,
    )
```

```python
import functools
import math

import jax
import jax.numpy as jnp
from jax import lax
from jax.experimental import pallas as pl
from jax.experimental.pallas import tpu as pltpu
from jax.sharding import PartitionSpec as P

NS_STEPS = 5
EPSILON = 1e-05
COEF_A = 3.4445
COEF_B = -4.775
COEF_C = 2.0315
MUON_RATE = 0.2
SMALL_RATE = 0.2
PRECISE = lax.Precision.HIGHEST
BF = jnp.bfloat16
F32 = jnp.float32


def silu(values):
    return values * jax.nn.sigmoid(values)


def silu_slope(values):
    sigmoid_value = jax.nn.sigmoid(values)
    return sigmoid_value * (1.0 + values * (1.0 - sigmoid_value))


def flip(value, axis, bit):
    count = lax.axis_size(axis)
    return lax.ppermute(value, axis, [(i, i ^ bit) for i in range(count)])


def sum_over(value, axis):
    bit = 1
    while bit < lax.axis_size(axis):
        value = jax.tree.map(lambda part: part + flip(part, axis, bit), value)
        bit *= 2
    return value


def pick(stacked, index, axis):
    return lax.dynamic_index_in_dim(stacked, index, axis, keepdims=False)


def gather_head(piece, axis):
    place = lax.axis_index("head")
    across = flip(piece, "head", 2)
    beside = flip(piece, "head", 1)
    corner = flip(across, "head", 1)
    low, high = place % 2, place // 2
    near = jnp.where(low == 0, jnp.stack([piece, beside], axis), jnp.stack([beside, piece], axis))
    far = jnp.where(low == 0, jnp.stack([across, corner], axis), jnp.stack([corner, across], axis))
    return jnp.where(
        high == 0, jnp.concatenate([near, far], axis), jnp.concatenate([far, near], axis)
    )


def scatter_head(parts, axis, wire):
    place = lax.axis_index("head")
    low, high = place % 2, place // 2
    shape = parts.shape
    parts = parts.reshape(shape[:axis] + (2, 2) + shape[axis + 1 :])
    half = pick(parts, low, axis + 1) + flip(pick(parts, 1 - low, axis + 1), "head", 1)
    sent = flip(pick(half, 1 - high, axis).astype(wire), "head", 2)
    return pick(half, high, axis) + sent.astype(F32)


def spread(blocks, members):
    count = lax.axis_size("seq")
    runs = [list(range(i, i + members)) for i in range(0, count, members)]
    return lax.all_to_all(
        blocks, "seq", 0, 0, tiled=True, axis_index_groups=runs if len(runs) > 1 else None
    )


def entering(growth, state, members, backward):
    count = lax.axis_size("seq")
    runs = count // members
    mine = lax.axis_index("seq") // members
    step = -members if backward else members
    pairs = [(i, i + step) for i in range(count) if 0 <= i + step < count]
    total = jnp.zeros_like(state)
    for _ in range(runs - 1):
        total = lax.ppermute(growth * total + state, "seq", pairs)
    return total


CHUNK = 128
LANES = 128
SUBLANES = 8
VMEM_BYTES = 56 * 1024 * 1024


def split(values, terms):
    pieces = []
    for _ in range(terms):
        pieces.append(values.astype(BF))
        values = values - pieces[-1].astype(F32)
    return pieces


def product(left, right, dims=((1,), (0,))):
    total = None
    for i, a in enumerate(left):
        for j, b in enumerate(right):
            if i + j < max(len(left), len(right)):
                part = lax.dot_general(a, b, (dims, ((), ())), preferred_element_type=F32)
                total = part if total is None else total + part
    return total


ROWS_OF_BOTH = ((1,), (1,))


def columns(rows):
    count, extent = rows.shape
    return jnp.concatenate([rows, jnp.zeros((LANES - count, extent), F32)], axis=0).T


def lane_pair(left, right, half):
    lane = lax.broadcasted_iota(jnp.int32, (CHUNK, LANES), 1)
    return jnp.where(lane < half, left, right)


def apart(pair, half):
    lane = lax.broadcasted_iota(jnp.int32, pair.shape, 1)
    zero = jnp.zeros_like(pair)
    return jnp.concatenate([jnp.where(lane < half, pair, zero), jnp.where(lane < half, zero, pair)], 0)


def head_sums(values, half):
    lane = lax.broadcasted_iota(jnp.int32, values.shape, 1)
    first = jnp.sum(jnp.where(lane < half, values, 0.0), axis=1, keepdims=True)
    return first, jnp.sum(values, axis=1, keepdims=True) - first


def forward_kernel(
    half, terms, place_ref, conv_ref, z_ref, c_ref, bt_ref, rows_ref, skip_ref, gain_ref,
    out_low_ref, cot_ref, start_ref,
    mixed_ref, states_ref, end_ref, gated_ref, partial_ref, sums_ref, state_ref,
):
    step = pl.program_id(0)
    block = conv_ref.shape[0]
    span = conv_ref.shape[1]
    pairs = span // LANES

    @pl.when(step == 0)
    def _():
        state_ref[...] = start_ref[...]

    causal = lax.broadcasted_iota(jnp.int32, (CHUNK, CHUNK), 0) >= lax.broadcasted_iota(
        jnp.int32, (CHUNK, CHUNK), 1
    )
    for sub in range(block // CHUNK):
        here = slice(sub * CHUNK, (sub + 1) * CHUNK)
        rows = rows_ref[:, here]
        cols = columns(rows)
        c_block, bt_block = c_ref[here], bt_ref[:, here]
        scores = product([c_block], [bt_block])
        states_ref[sub] = state_ref[...]
        state_parts = split(state_ref[...], terms)
        carried = product([c_block], state_parts)
        weighted, grown = [], []
        for pair in range(pairs):
            lanes = slice(pair * LANES, (pair + 1) * LANES)
            first, second = 2 * pair, 2 * pair + 1
            x = silu(conv_ref[here, lanes])

            def pair_cols(table, offset):
                return lane_pair(
                    table[:, offset + first : offset + first + 1],
                    table[:, offset + second : offset + second + 1],
                    half,
                )

            cum = pair_cols(cols, SUBLANES)
            scaled = x * pair_cols(cols, 0)
            last = cum[CHUNK - 1 : CHUNK]
            growth = jnp.exp(cum)
            weighted.append(scaled * jnp.exp(last - cum))
            grown.append(growth[CHUNK - 1 : CHUNK])
            mixing = []
            for head in (first, second):
                gap = cols[:, SUBLANES + head : SUBLANES + head + 1] - rows[SUBLANES + head : SUBLANES + head + 1]
                mixing.append(jnp.exp(jnp.where(causal, gap, -1e30)) * scores)
            inner = product(
                split(jnp.concatenate(mixing, axis=1), terms), split(apart(scaled, half), terms)
            )
            mixed_ref[here, lanes] = inner + carried[:, lanes] * growth + skip_ref[:, lanes] * x
        fresh = product([bt_block], split(jnp.concatenate(weighted, axis=1), terms))
        state_ref[...] = jnp.concatenate(grown, axis=1) * state_ref[...] + fresh
    end_ref[...] = state_ref[...]
    gated = mixed_ref[...] * silu(z_ref[...])
    gated_low = (gated * gain_ref[...]).astype(BF)
    gated_ref[...] = gated_low
    partial = jnp.dot(gated_low, out_low_ref[...], preferred_element_type=F32)
    partial_ref[...] = partial.reshape(partial_ref.shape).astype(partial_ref.dtype)
    squares = jnp.sum(gated * gated, axis=1, keepdims=True)
    slot = place_ref[1] + step * block + lax.broadcasted_iota(jnp.int32, (block, 1), 0)
    back = jnp.where(slot < place_ref[0], cot_ref[...].astype(F32), 0.0)
    scale = jnp.sum(back * partial, axis=1, keepdims=True)
    lane = lax.broadcasted_iota(jnp.int32, (block, LANES), 1)
    sums = jnp.where(lane == 0, squares, jnp.where(lane == 1, scale, 0.0))
    for sub in range(block // CHUNK):
        here = slice(sub * CHUNK, (sub + 1) * CHUNK)
        sums_ref[:, here] = sums[here].T[:SUBLANES]


def forward_scan(place, conv, z, c_mat, bt, rows, skip, gain, out_low, cot, start, half, members, parts):
    tokens, span = conv.shape
    width = cot.shape[1]
    state = c_mat.shape[1]
    block = tokens // members
    subs = block // CHUNK
    by_rows = lambda i, *_: (i, 0)
    by_lanes = lambda i, *_: (0, i)
    whole = lambda i, *_: (0, 0)
    quarter = block // parts
    return pl.pallas_call(
        functools.partial(forward_kernel, half, 2),
        grid_spec=pltpu.PrefetchScalarGridSpec(
            num_scalar_prefetch=1,
            grid=(members,),
            in_specs=[
                pl.BlockSpec((block, span), by_rows),
                pl.BlockSpec((block, span), by_rows),
                pl.BlockSpec((block, state), by_rows),
                pl.BlockSpec((state, block), by_lanes),
                pl.BlockSpec((2 * SUBLANES, block), by_lanes),
                pl.BlockSpec((1, span), whole),
                pl.BlockSpec((1, span), whole),
                pl.BlockSpec((span, width), whole),
                pl.BlockSpec((block, width), by_rows),
                pl.BlockSpec((state, span), whole),
            ],
            out_specs=[
                pl.BlockSpec((block, span), by_rows),
                pl.BlockSpec((subs, state, span), lambda i, *_: (i, 0, 0)),
                pl.BlockSpec((state, span), whole),
                pl.BlockSpec((block, span), by_rows),
                pl.BlockSpec((parts, 1, quarter, width), lambda i, *_: (0, i, 0, 0)),
                pl.BlockSpec((SUBLANES, block), by_lanes),
            ],
            scratch_shapes=[pltpu.VMEM((state, span), F32)],
        ),
        out_shape=[
            jax.ShapeDtypeStruct((tokens, span), F32),
            jax.ShapeDtypeStruct((tokens // CHUNK, state, span), F32),
            jax.ShapeDtypeStruct((state, span), F32),
            jax.ShapeDtypeStruct((tokens, span), BF),
            jax.ShapeDtypeStruct((parts, members, quarter, width), F32),
            jax.ShapeDtypeStruct((SUBLANES, tokens), F32),
        ],
        compiler_params=pltpu.CompilerParams(vmem_limit_bytes=VMEM_BYTES),
    )(place, conv, z, c_mat, bt, rows, skip, gain, out_low, cot, start)


def gate_kernel(
    inner_all, place_ref, cot_ref, norm_ref, z_ref, mixed_ref, gain_ref, out_turned_ref,
    grad_mixed_ref, grad_z_ref, grad_summed_ref, gain_grad_ref,
):
    step = pl.program_id(0)
    block = cot_ref.shape[0]
    norm = jnp.concatenate(
        [columns(norm_ref[:, sub * CHUNK : (sub + 1) * CHUNK]) for sub in range(block // CHUNK)], 0
    )
    norm_scale, grad_scale = norm[:, 0:1], norm[:, 1:2]
    slot = place_ref[1] + step * block + lax.broadcasted_iota(jnp.int32, (block, 1), 0)
    back = jnp.where(slot < place_ref[0], cot_ref[...].astype(F32), 0.0)
    grad_summed = (norm_scale * back).astype(BF)
    grad_summed_ref[...] = grad_summed
    grad_low = jnp.dot(grad_summed, out_turned_ref[...], preferred_element_type=F32)
    z, mixed = z_ref[...], mixed_ref[...]
    sigmoid = jax.nn.sigmoid(z)
    gate = z * sigmoid
    gated = mixed * gate
    shrink = grad_scale * norm_scale * norm_scale * norm_scale / inner_all
    grad_gated = grad_low * gain_ref[...] - shrink * gated
    grad_mixed_ref[...] = grad_gated * gate
    grad_z_ref[...] = (grad_gated * mixed * (sigmoid * (1.0 + z * (1.0 - sigmoid)))).astype(BF)

    @pl.when(step == 0)
    def _():
        gain_grad_ref[...] = jnp.zeros_like(gain_grad_ref)

    gain_grad_ref[...] += jnp.sum(grad_low * gated, axis=0, keepdims=True)


def gate_back(place, cot, norm_rows, z, mixed, gain, out_turned, inner_all, members):
    tokens, span = z.shape
    width = cot.shape[1]
    block = tokens // members
    by_rows = lambda i, *_: (i, 0)
    whole = lambda i, *_: (0, 0)
    return pl.pallas_call(
        functools.partial(gate_kernel, inner_all),
        grid_spec=pltpu.PrefetchScalarGridSpec(
            num_scalar_prefetch=1,
            grid=(members,),
            in_specs=[
                pl.BlockSpec((block, width), by_rows),
                pl.BlockSpec((SUBLANES, block), lambda i, *_: (0, i)),
                pl.BlockSpec((block, span), by_rows),
                pl.BlockSpec((block, span), by_rows),
                pl.BlockSpec((1, span), whole),
                pl.BlockSpec((width, span), whole),
            ],
            out_specs=[
                pl.BlockSpec((block, span), by_rows),
                pl.BlockSpec((block, span), by_rows),
                pl.BlockSpec((block, width), by_rows),
                pl.BlockSpec((1, span), whole),
            ],
        ),
        out_shape=[
            jax.ShapeDtypeStruct((tokens, span), F32),
            jax.ShapeDtypeStruct((tokens, span), BF),
            jax.ShapeDtypeStruct((tokens, width), BF),
            jax.ShapeDtypeStruct((1, span), F32),
        ],
        compiler_params=pltpu.CompilerParams(vmem_limit_bytes=VMEM_BYTES),
    )(place, cot, norm_rows, z, mixed, gain, out_turned)


def backward_kernel(
    half, terms, taps, grad_ref, conv_ref, conv_in_ref, b_ref, c_ref, bt_ref, ct_ref, rows_ref, states_ref,
    end_ref, skip_ref, weight_ref, back_ref, halo_ref,
    grad_x_ref, grad_bc_ref, rows_out_ref, first_ref, edge_ref, small_ref,
    carry_ref, after_ref, shift_ref,
):
    step = pl.program_id(0)
    block = conv_ref.shape[0]
    span = conv_ref.shape[1]
    pairs = span // LANES
    state = b_ref.shape[1]
    subs = block // CHUNK

    @pl.when(step == 0)
    def _():
        carry_ref[...] = back_ref[...]
        after_ref[...] = end_ref[...]
        shift_ref[:SUBLANES] = halo_ref[...]
        small_ref[...] = jnp.zeros_like(small_ref)

    row = lax.broadcasted_iota(jnp.int32, (CHUNK, CHUNK), 0)
    lane = lax.broadcasted_iota(jnp.int32, (CHUNK, CHUNK), 1)
    causal = row <= lane
    for sub in reversed(range(subs)):
        here = slice(sub * CHUNK, (sub + 1) * CHUNK)
        rows = rows_ref[:, here]
        cols = columns(rows)
        b_block, c_block, bt_block, ct_block = b_ref[here], c_ref[here], bt_ref[:, here], ct_ref[:, here]
        scores = product([b_block], [ct_block])
        entered = states_ref[sub]
        carry = carry_ref[...]
        entered_parts = split(entered, terms)
        carry_parts = split(carry, terms)
        carried = product([c_block], entered_parts)
        pulled = product([b_block], carry_parts)
        joint = jnp.sum(carry * after_ref[...], axis=0, keepdims=True)
        after_ref[...] = entered
        head_of = lax.broadcasted_iota(jnp.int32, (SUBLANES, span), 1) // half
        joint = jnp.sum(
            jnp.where(head_of == lax.broadcasted_iota(jnp.int32, (SUBLANES, span), 0), joint, 0.0),
            axis=1,
            keepdims=True,
        )
        weighted, grown_grad, grown = [], [], []
        grad_scores = jnp.zeros((CHUNK, CHUNK), F32)
        col_sums = jnp.zeros((CHUNK, LANES), F32)
        row_sums = []
        for pair in range(pairs):
            lanes = slice(pair * LANES, (pair + 1) * LANES)
            first, second = 2 * pair, 2 * pair + 1

            def pair_cols(offset):
                return lane_pair(
                    cols[:, offset + first : offset + first + 1],
                    cols[:, offset + second : offset + second + 1],
                    half,
                )

            conv = conv_ref[here, lanes]
            sigmoid = jax.nn.sigmoid(conv)
            x = conv * sigmoid
            grad = grad_ref[here, lanes]
            cum, size = pair_cols(SUBLANES), pair_cols(0)
            scaled = x * size
            last = cum[CHUNK - 1 : CHUNK]
            growth = jnp.exp(cum)
            tail = jnp.exp(last - cum)
            weighted.append(scaled * tail)
            grown_grad.append(grad * growth)
            grown.append(growth[CHUNK - 1 : CHUNK])
            grad_apart = split(apart(grad, half), terms)
            dots = product(split(scaled, terms), grad_apart, ROWS_OF_BOTH)
            kernels = []
            for k, head in enumerate((first, second)):
                gap = rows[SUBLANES + head : SUBLANES + head + 1] - cols[:, SUBLANES + head : SUBLANES + head + 1]
                decay = jnp.exp(jnp.where(causal, gap, -1e30))
                grad_score = decay * dots[:, k * CHUNK : (k + 1) * CHUNK]
                grad_scores = grad_scores + grad_score
                kernels.append(decay * scores)
                both = grad_score * scores
                row_sums.append(jnp.sum(both, axis=0, keepdims=True))
                col_sums = jnp.where(
                    lane == head, col_sums - jnp.sum(both, axis=1, keepdims=True), col_sums
                )
            pulled_pair = tail * pulled[:, lanes]
            force = product(split(jnp.concatenate(kernels, axis=1), terms), grad_apart) + pulled_pair
            grad_x = size * force + skip_ref[:, lanes] * grad
            flow = grown_grad[-1] * carried[:, lanes] - scaled * pulled_pair
            direct = x * force
            for head, flow_sum, direct_sum in zip(
                (first, second), head_sums(flow, half), head_sums(direct, half)
            ):
                col_sums = jnp.where(lane == head, col_sums + flow_sum, col_sums)
                col_sums = jnp.where(lane == SUBLANES + head, direct_sum, col_sums)
            small_ref[taps + 1 : taps + 2, lanes] += jnp.sum(grad * x, axis=0, keepdims=True)
            grad_conv = (grad_x * (sigmoid * (1.0 + conv * (1.0 - sigmoid)))).astype(BF).astype(F32)
            shift_ref[CHUNK : CHUNK + SUBLANES, lanes] = shift_ref[:SUBLANES, lanes]
            shift_ref[:CHUNK, lanes] = grad_conv
            conv_in = conv_in_ref[here, lanes].astype(F32)
            total = None
            for tap in range(taps):
                moved = shift_ref[taps - 1 - tap : taps - 1 - tap + CHUNK, lanes]
                term = weight_ref[tap : tap + 1, lanes] * moved
                total = term if total is None else total + term
                small_ref[tap : tap + 1, lanes] += jnp.sum(conv_in * moved, axis=0, keepdims=True)
            small_ref[taps : taps + 1, lanes] += jnp.sum(grad_conv, axis=0, keepdims=True)
            grad_x_ref[here, lanes] = total.astype(BF)
        grown_parts = split(jnp.concatenate(grown_grad, axis=1), terms)
        weighted_parts = split(jnp.concatenate(weighted, axis=1), terms)
        grad_b = product(carry_parts, weighted_parts, ROWS_OF_BOTH) + product(
            [ct_block], split(grad_scores.T, terms)
        )
        grad_c = product(entered_parts, grown_parts, ROWS_OF_BOTH) + product(
            [bt_block], split(grad_scores, terms)
        )
        grad_bc_ref[:state, here] = grad_b
        grad_bc_ref[state:, here] = grad_c
        carry_ref[...] = jnp.concatenate(grown, axis=1) * carry + product([ct_block], grown_parts)
        turned = col_sums.T
        row_sums.append(jnp.zeros((SUBLANES - 2 * pairs, CHUNK), F32))
        slots = lax.broadcasted_iota(jnp.int32, (SUBLANES, CHUNK), 1)
        rows_out_ref[:SUBLANES, here] = (
            jnp.concatenate(row_sums, axis=0)
            + turned[:SUBLANES]
            + jnp.where(slots == CHUNK - 1, joint, 0.0)
        )
        rows_out_ref[SUBLANES:, here] = turned[SUBLANES : 2 * SUBLANES]
    first_ref[...] = carry_ref[...]
    edge_ref[...] = shift_ref[:SUBLANES]


def backward_scan(grad, conv, conv_in, b_mat, c_mat, bt, ct, rows, states, end, skip, weight, back, halo, half, members):
    tokens, span = conv.shape
    state = b_mat.shape[1]
    taps = weight.shape[0]
    block = tokens // members
    subs = block // CHUNK
    final = members - 1
    by_rows = lambda i: (final - i, 0)
    by_lanes = lambda i: (0, final - i)
    whole = lambda i: (0, 0)
    return pl.pallas_call(
        functools.partial(backward_kernel, half, 2, taps),
        grid=(members,),
        in_specs=[
            pl.BlockSpec((block, span), by_rows),
            pl.BlockSpec((block, span), by_rows),
            pl.BlockSpec((block, span), by_rows),
            pl.BlockSpec((block, state), by_rows),
            pl.BlockSpec((block, state), by_rows),
            pl.BlockSpec((state, block), by_lanes),
            pl.BlockSpec((state, block), by_lanes),
            pl.BlockSpec((2 * SUBLANES, block), by_lanes),
            pl.BlockSpec((subs, state, span), lambda i: (final - i, 0, 0)),
            pl.BlockSpec((state, span), whole),
            pl.BlockSpec((1, span), whole),
            pl.BlockSpec((taps, span), whole),
            pl.BlockSpec((state, span), whole),
            pl.BlockSpec((SUBLANES, span), whole),
        ],
        out_specs=[
            pl.BlockSpec((block, span), by_rows),
            pl.BlockSpec((2 * state, block), by_lanes),
            pl.BlockSpec((2 * SUBLANES, block), by_lanes),
            pl.BlockSpec((state, span), whole),
            pl.BlockSpec((SUBLANES, span), whole),
            pl.BlockSpec((SUBLANES, span), whole),
        ],
        out_shape=[
            jax.ShapeDtypeStruct((tokens, span), BF),
            jax.ShapeDtypeStruct((2 * state, tokens), F32),
            jax.ShapeDtypeStruct((2 * SUBLANES, tokens), F32),
            jax.ShapeDtypeStruct((state, span), F32),
            jax.ShapeDtypeStruct((SUBLANES, span), F32),
            jax.ShapeDtypeStruct((SUBLANES, span), F32),
        ],
        scratch_shapes=[
            pltpu.VMEM((state, span), F32),
            pltpu.VMEM((state, span), F32),
            pltpu.VMEM((CHUNK + SUBLANES, span), F32),
        ],
        compiler_params=pltpu.CompilerParams(vmem_limit_bytes=VMEM_BYTES),
    )(grad, conv, conv_in, b_mat, c_mat, bt, ct, rows, states, end, skip, weight, back, halo)


def newton_kernel(gram_ref, pick_ref, rows_ref, gram, first, second, third, polys):
    width = gram_ref.shape[0]
    tile = 256
    tiles = [slice(i, i + tile) for i in range(0, width, tile)]

    def store(pair, here, values):
        high = values.astype(BF)
        pair[0, here] = high
        pair[1, here] = (values - high.astype(F32)).astype(BF)

    def times(left, here, right):
        high, low = left[0, here], left[1, here]
        total = jnp.dot(high, right[1], preferred_element_type=F32)
        total = total + jnp.dot(low, right[0], preferred_element_type=F32)
        return total + jnp.dot(high, right[0], preferred_element_type=F32)

    def eye(here):
        row = lax.broadcasted_iota(jnp.int32, (tile, width), 0) + here.start
        return row == lax.broadcasted_iota(jnp.int32, (tile, width), 1)

    size = jnp.zeros((1, 1), F32)
    for here in tiles:
        size = size + jnp.sum(jnp.where(eye(here), gram_ref[here], 0.0), keepdims=True)
    factor = 1.0 / (jnp.sqrt(size) + 1e-07)
    for here in tiles:
        gram[here] = gram_ref[here] * (factor * factor)
        store(first, here, gram[here])
    for step in range(NS_STEPS):
        for here in tiles:
            square = times(first, here, first)
            store(second, here, square)
            poly = jnp.where(eye(here), COEF_A, 0.0) + COEF_B * gram[here] + COEF_C * square
            store(polys.at[step], here, poly)
            gram[here] = COEF_A * gram[here] + COEF_B * square
        if step + 1 < NS_STEPS:
            for here in tiles:
                store(third, here, gram[here] + COEF_C * times(second, here, first))
            for here in tiles:
                gram[here] = times(third, here, polys.at[step])
            for here in tiles:
                store(first, here, gram[here])
    picked = pick_ref[...]
    last = polys.at[NS_STEPS - 1]
    rows = jnp.dot(picked, last[0], preferred_element_type=F32) + jnp.dot(
        picked, last[1], preferred_element_type=F32
    )
    for step in reversed(range(NS_STEPS - 1)):
        rows = product(split(rows, 2), [polys[step, 0], polys[step, 1]])
    rows_ref[...] = rows * factor


def newton_rows(gram, picked):
    width = gram.shape[0]
    pair = pltpu.VMEM((2, width, width), BF)
    return pl.pallas_call(
        newton_kernel,
        out_shape=jax.ShapeDtypeStruct(picked.shape, F32),
        in_specs=[pl.BlockSpec(memory_space=pltpu.VMEM)] * 2,
        out_specs=pl.BlockSpec(memory_space=pltpu.VMEM),
        scratch_shapes=[
            pltpu.VMEM((width, width), F32),
            pair,
            pair,
            pair,
            pltpu.VMEM((NS_STEPS, 2, width, width), BF),
        ],
        compiler_params=pltpu.CompilerParams(vmem_limit_bytes=VMEM_BYTES),
    )(gram, picked)


def whole_gram(pieces):
    gram = sum(
        jnp.dot(piece, piece.T, precision=lax.Precision.HIGH, preferred_element_type=F32)
        for piece in pieces
    )
    low = lax.axis_index("head") % 2
    halves = gram.reshape((2, -1) + gram.shape[1:])
    half = pick(halves, low, 0) + flip(pick(halves, 1 - low, 0), "head", 1)
    half = half + flip(half, "head", 2)
    other = flip(half, "head", 1)
    return jnp.concatenate(
        [jnp.where(low == 0, half, other), jnp.where(low == 0, other, half)], axis=0
    )


def per_device(
    inputs,
    lengths,
    norm_gain,
    in_proj,
    conv_weight,
    conv_bias,
    head_params,
    gate_gain,
    out_proj,
    cotangent,
    norm_gain_mom,
    in_proj_mom,
    conv_weight_mom,
    conv_bias_mom,
    head_params_mom,
    gate_gain_mom,
    out_proj_mom,
):
    members, extent, model_width = inputs.shape
    seq_count = lax.axis_size("seq")
    head_count = lax.axis_size("head")
    seq_place = lax.axis_index("seq")
    head_place = lax.axis_index("head")
    heads_here = head_params.shape[1]
    head_span = gate_gain.shape[0]
    head_size = head_span // heads_here
    channels = conv_bias.shape[0]
    state_size = (channels - head_span) * head_count // 2
    inner_all = head_span * head_count
    group_cols = in_proj.shape[1]
    proj_all = group_cols * head_count
    tap_count = conv_weight.shape[0]
    share = model_width // seq_count
    tokens = members * extent
    quarter = extent // head_count
    runs = seq_count // members

    def to_sequence(blocks):
        piece = lax.dynamic_slice_in_dim(blocks, head_place * quarter, quarter, 1)
        piece = spread(piece, members)
        return piece, gather_head(piece, 1).reshape(tokens, -1)

    def from_sequence(piece):
        return gather_head(spread(piece.astype(BF), members), 1).reshape(inputs.shape)

    def own(per_token):
        return pick(per_token.reshape((members, head_count, quarter, -1)), head_place, 1)

    data_piece, data = to_sequence(inputs)
    cot_piece, cot = to_sequence(cotangent)
    data_piece, data = data_piece.astype(F32), data.astype(F32)
    run_place = seq_place // members
    length = lengths[seq_place % members]
    first_slot = run_place * tokens
    place = jnp.stack([length, first_slot]).astype(jnp.int32)
    root_scale = lax.rsqrt(jnp.mean(data * data, axis=-1, keepdims=True) + EPSILON)
    lowered = (data * root_scale * norm_gain).astype(BF)
    in_low = in_proj.astype(BF)
    x_end = 2 * head_span
    bc_end = head_span + channels
    halo = tap_count - 1

    def from_run(edge, step):
        if runs == 1:
            return jnp.zeros_like(edge)
        pairs = [(i, i + step) for i in range(seq_count) if 0 <= i + step < seq_count]
        return lax.ppermute(edge, "seq", pairs)

    side = lax.dot_general(
        in_low[:, x_end:], lowered, (((0,), (1,)), ((), ())), preferred_element_type=F32
    )
    bc_in = side[: bc_end - x_end].astype(BF)
    bc_weight = conv_weight[:, head_span:, None]
    bc_padded = jnp.concatenate([from_run(bc_in[:, tokens - halo :], members), bc_in], axis=1)
    bc_conv = conv_bias[head_span:, None] + jnp.zeros(bc_in.shape, F32)
    for offset in range(tap_count):
        bc_conv = bc_conv + bc_weight[offset] * bc_padded[:, offset : offset + tokens]
    bc_full = gather_head(silu(bc_conv).astype(BF), 0).reshape(2, state_size, tokens)
    bt, ct = bc_full[0], bc_full[1]
    b_mat, c_mat = bt.T, ct.T
    pre_steps = side[bc_end - x_end :] + head_params[0][:, None]
    step_sizes = jax.nn.softplus(pre_steps)
    decay_rate = -jnp.exp(head_params[1])[:, None]
    chunk_row = lax.broadcasted_iota(jnp.int32, (CHUNK, CHUNK), 0)
    chunk_col = lax.broadcasted_iota(jnp.int32, (CHUNK, CHUNK), 1)
    upto = (chunk_row <= chunk_col).astype(F32)

    def chunk_dot(rows, matrix):
        return jnp.dot(rows.reshape(-1, CHUNK), matrix, precision=PRECISE).reshape(rows.shape)

    cumulative = chunk_dot(step_sizes * decay_rate, upto)
    spare = jnp.zeros((SUBLANES - heads_here, tokens), F32)
    rows = jnp.concatenate([step_sizes, spare, cumulative, spare], axis=0)
    growth = jnp.repeat(jnp.exp(jnp.sum(step_sizes * decay_rate, axis=1)), head_size)[None]

    z_part = jnp.dot(lowered, in_low[:, :head_span], preferred_element_type=F32)
    x_in = jnp.dot(lowered, in_low[:, head_span:x_end], preferred_element_type=F32).astype(BF)
    x_weight = conv_weight[:, :head_span]
    x_padded = jnp.concatenate([from_run(x_in[tokens - halo :], members), x_in], axis=0)
    x_conv = conv_bias[:head_span] + jnp.zeros(x_in.shape, F32)
    for offset in range(tap_count):
        x_conv = x_conv + x_weight[offset] * x_padded[offset : offset + tokens]

    skip = jnp.repeat(head_params[2], head_size)[None]
    gain = gate_gain[None]
    out_low = out_proj.astype(BF)

    def scan_from(start):
        return forward_scan(
            place, x_conv, z_part, c_mat, bt, rows, skip, gain, out_low, cot, start, head_size, members, head_count
        )

    start = jnp.zeros((state_size, head_span), F32)
    if runs > 1:
        start = entering(growth, scan_from(start)[2], members, False)
    mixed, states, state_end, gated_low, partial_out, sums = scan_from(start)
    square_sum, grad_scale = sum_over(sums[:2], "head")
    norm_scale = lax.rsqrt(square_sum / inner_all + EPSILON)
    norm_rows = jnp.concatenate(
        [norm_scale[None], grad_scale[None], jnp.zeros((SUBLANES - 2, tokens), F32)], axis=0
    )
    grad_mixed, grad_z, grad_summed, gate_gain_grad = gate_back(
        place, cot, norm_rows, z_part, mixed, gain, out_low.T, inner_all, members
    )
    gate_gain_grad = gate_gain_grad[0]

    def rows_of(term):
        return lax.psum_scatter(term, "seq", scatter_dimension=0, tiled=True)

    early = jnp.concatenate(
        [
            jnp.dot(lowered.T, grad_z, preferred_element_type=F32),
            jnp.dot(grad_summed.T, gated_low, preferred_element_type=F32),
        ],
        axis=1,
    )
    early_rows = rows_of(early)

    summed = scatter_head(partial_out, 0, BF)
    slots = first_slot + lax.broadcasted_iota(jnp.int32, (tokens, 1), 0)
    valid_mask = own((slots < length).astype(F32))
    result = valid_mask * (data_piece + own(norm_scale) * summed)
    output = from_sequence(result)
    result_squares = jnp.sum(result * result)

    def scan_back(back, edge):
        return backward_scan(
            grad_mixed, x_conv, x_in, b_mat, c_mat, bt, ct, rows, states, state_end, skip, x_weight,
            back, edge, head_size, members,
        )

    back = jnp.zeros_like(state_end)
    edge = jnp.zeros((SUBLANES, head_span), F32)
    if runs > 1:
        back = entering(growth, scan_back(back, edge)[3], members, True)
        edge = from_run(scan_back(back, edge)[4], -members)
    grad_x_in, grad_bc, grad_rows, _, _, small = scan_back(back, edge)
    grad_bc = scatter_head(grad_bc.reshape(head_count, -1, tokens), 0, F32)
    grad_cum, grad_direct = grad_rows[:heads_here], grad_rows[SUBLANES : SUBLANES + heads_here]
    grad_decay = chunk_dot(grad_cum, upto.T)
    grad_pre = (grad_direct + grad_decay * decay_rate) * jax.nn.sigmoid(pre_steps)
    head_params_grad = jnp.stack(
        [
            jnp.sum(grad_pre, axis=1),
            jnp.sum(grad_decay * step_sizes, axis=1) * decay_rate[:, 0],
            jnp.sum(small[tap_count + 1].reshape(heads_here, head_size), axis=1),
        ]
    )
    grad_conv = (grad_bc * silu_slope(bc_conv)).astype(BF)
    trailing = jnp.concatenate([grad_conv, from_run(grad_conv[:, :halo], -members)], axis=1)
    grad_bc_in = jnp.zeros(bc_in.shape, F32)
    tap_grads = []
    for offset in range(tap_count):
        lead = halo - offset
        moved = trailing[:, lead : lead + tokens].astype(F32)
        grad_bc_in = grad_bc_in + bc_weight[offset] * moved
        tap_grads.append(jnp.sum(moved * bc_in, axis=1))
    conv_weight_grad = jnp.concatenate([small[:tap_count], jnp.stack(tap_grads)], axis=1)
    conv_bias_grad = jnp.concatenate([small[tap_count], jnp.sum(grad_conv.astype(F32), axis=1)])
    grad_side = jnp.concatenate([grad_bc_in, grad_pre], axis=0).astype(BF).T
    grad_late = jnp.concatenate([grad_x_in, grad_side], axis=1)
    late_rows = rows_of(jnp.dot(lowered.T, grad_late, preferred_element_type=F32))
    in_proj_grad = jnp.concatenate([early_rows[:, :head_span], late_rows], axis=1)
    out_grad_rows = early_rows[:, head_span:]
    partial_in = jnp.dot(
        jnp.concatenate([grad_z, grad_late], axis=1), in_low.T, preferred_element_type=F32
    )
    grad_lowered = scatter_head(partial_in.reshape(members, head_count, quarter, -1), 1, BF)
    root_piece = own(root_scale)
    normed_piece = data_piece * root_piece
    norm_gain_grad = jnp.sum(grad_lowered * normed_piece, axis=(0, 1))
    grad_normed = grad_lowered * norm_gain
    input_grad = valid_mask * cot_piece.astype(F32) + root_piece * (
        grad_normed - normed_piece * jnp.mean(grad_normed * normed_piece, axis=-1, keepdims=True)
    )
    input_grad = from_sequence(input_grad).astype(F32)
    norm_gain_grad, result_squares = sum_over((norm_gain_grad, result_squares), "head")
    small_parts = (
        norm_gain_grad,
        conv_weight_grad,
        conv_bias_grad,
        head_params_grad,
        gate_gain_grad,
        result_squares,
    )
    packed = sum_over(jnp.concatenate([part.reshape(-1) for part in small_parts]), "seq")
    unpacked = []
    for part in small_parts:
        unpacked.append(packed[: part.size].reshape(part.shape))
        packed = packed[part.size :]
    (
        norm_gain_grad,
        conv_weight_grad,
        conv_bias_grad,
        head_params_grad,
        gate_gain_grad,
        squares_all,
    ) = unpacked
    rms = jnp.sqrt(squares_all / (jnp.sum(lengths).astype(F32) * model_width))
    in_proj_mom_new = 0.5 * in_proj_mom + in_proj_grad
    out_rows_mom = 0.5 * out_proj_mom.T + out_grad_rows
    def whole(rows):
        return lax.all_gather(rows, "seq", axis=0, tiled=True)

    early_whole = whole(jnp.concatenate([in_proj_mom_new[:, :head_span], out_rows_mom], axis=1))
    late_whole = whole(in_proj_mom_new[:, head_span:])
    full_out = early_whole[:, head_span:]
    full_in = early_whole[:, :head_span]
    picked_rows = -(-share // (2 * SUBLANES)) * 2 * SUBLANES
    picked = seq_place * share + lax.broadcasted_iota(jnp.int32, (picked_rows, model_width), 0)
    picked = (picked == lax.broadcasted_iota(jnp.int32, picked.shape, 1)).astype(BF)
    turn_out = newton_rows(whole_gram([full_out]), picked)[:share]
    turn_in = newton_rows(whole_gram([full_in, late_whole]), picked)[:share]

    def turned(turn, matrix):
        return jnp.dot(turn, matrix, precision=lax.Precision.HIGH, preferred_element_type=F32)

    rows_out = turned(turn_out, full_out)
    rows_in = jnp.concatenate([turned(turn_in, full_in), turned(turn_in, late_whole)], axis=1)
    in_old_rows = lax.dynamic_slice_in_dim(in_proj, seq_place * share, share, 0)
    in_proj_new = in_old_rows - MUON_RATE * 0.2 * math.sqrt(max(model_width, proj_all)) * rows_in
    out_old_cols = lax.dynamic_slice_in_dim(out_proj, seq_place * share, share, 1)
    out_proj_new = (
        out_old_cols - MUON_RATE * 0.2 * math.sqrt(max(inner_all, model_width)) * rows_out.T
    )
    divisor = math.sqrt(members * extent * seq_count)
    norm_gain_mom_new = 0.5 * norm_gain_mom + norm_gain_grad
    conv_weight_mom_new = 0.5 * conv_weight_mom + conv_weight_grad
    conv_bias_mom_new = 0.5 * conv_bias_mom + conv_bias_grad
    head_params_mom_new = 0.5 * head_params_mom + head_params_grad
    gate_gain_mom_new = 0.5 * gate_gain_mom + gate_gain_grad
    norm_gain_new = norm_gain - SMALL_RATE * norm_gain_mom_new / divisor
    conv_weight_new = conv_weight - SMALL_RATE * conv_weight_mom_new / divisor
    conv_bias_new = conv_bias - SMALL_RATE * conv_bias_mom_new / divisor
    head_params_new = head_params - SMALL_RATE * head_params_mom_new / divisor
    gate_gain_new = gate_gain - SMALL_RATE * gate_gain_mom_new / divisor
    return (
        output,
        input_grad,
        norm_gain_grad,
        in_proj_grad,
        conv_weight_grad,
        conv_bias_grad,
        head_params_grad,
        gate_gain_grad,
        out_grad_rows.T,
        norm_gain_mom_new,
        in_proj_mom_new,
        conv_weight_mom_new,
        conv_bias_mom_new,
        head_params_mom_new,
        gate_gain_mom_new,
        out_rows_mom.T,
        norm_gain_new,
        in_proj_new,
        conv_weight_new,
        conv_bias_new,
        head_params_new,
        gate_gain_new,
        out_proj_new,
        rms,
    )


def solution(mesh):
    return jax.shard_map(
        per_device,
        mesh=mesh,
        in_specs=(
            P(None, "seq", None),
            P(),
            P(),
            P(None, "head"),
            P(None, "head"),
            P("head"),
            P(None, "head"),
            P("head"),
            P("head", None),
            P(None, "seq", None),
            P(),
            P("seq", "head"),
            P(None, "head"),
            P("head"),
            P(None, "head"),
            P("head"),
            P("head", "seq"),
        ),
        out_specs=(
            P(None, "seq", None),
            P(None, "seq", None),
            P(),
            P("seq", "head"),
            P(None, "head"),
            P("head"),
            P(None, "head"),
            P("head"),
            P("head", "seq"),
            P(),
            P("seq", "head"),
            P(None, "head"),
            P("head"),
            P(None, "head"),
            P("head"),
            P("head", "seq"),
            P(),
            P("seq", "head"),
            P(None, "head"),
            P("head"),
            P(None, "head"),
            P("head"),
            P("head", "seq"),
            P(),
        ),
        check_vma=False,
    )
```

```python
import functools
import math

import jax
import jax.numpy as jnp
from jax import lax
from jax.experimental import pallas as pl
from jax.experimental.pallas import tpu as pltpu
from jax.sharding import PartitionSpec as P

NS_STEPS = 5
EPSILON = 1e-05
COEF_A = 3.4445
COEF_B = -4.775
COEF_C = 2.0315
MUON_RATE = 0.2
SMALL_RATE = 0.2
PRECISE = lax.Precision.HIGHEST
BF = jnp.bfloat16
F32 = jnp.float32


def silu(values):
    return values * jax.nn.sigmoid(values)


def silu_slope(values):
    sigmoid_value = jax.nn.sigmoid(values)
    return sigmoid_value * (1.0 + values * (1.0 - sigmoid_value))


def flip(value, axis, bit):
    count = lax.axis_size(axis)
    return lax.ppermute(value, axis, [(i, i ^ bit) for i in range(count)])


def sum_over(value, axis):
    bit = 1
    while bit < lax.axis_size(axis):
        value = jax.tree.map(lambda part: part + flip(part, axis, bit), value)
        bit *= 2
    return value


def pick(stacked, index, axis):
    return lax.dynamic_index_in_dim(stacked, index, axis, keepdims=False)


def head_order(piece, beside, across, corner, axis):
    place = lax.axis_index("head")
    low, high = place % 2, place // 2
    near = jnp.where(low == 0, jnp.stack([piece, beside], axis), jnp.stack([beside, piece], axis))
    far = jnp.where(low == 0, jnp.stack([across, corner], axis), jnp.stack([corner, across], axis))
    return jnp.where(
        high == 0, jnp.concatenate([near, far], axis), jnp.concatenate([far, near], axis)
    )


def gather_head(piece, axis):
    across = flip(piece, "head", 2)
    return head_order(piece, flip(piece, "head", 1), across, flip(across, "head", 1), axis)


def head_halves(parts, axis):
    low = lax.axis_index("head") % 2
    shape = parts.shape
    parts = parts.reshape(shape[:axis] + (2, 2) + shape[axis + 1 :])
    return pick(parts, low, axis + 1) + flip(pick(parts, 1 - low, axis + 1), "head", 1)


def head_quarters(half, axis, wire):
    high = lax.axis_index("head") // 2
    return pick(half, high, axis), pick(half, 1 - high, axis).astype(wire)


def head_sum(kept, sent):
    return kept + flip(sent, "head", 2).astype(F32)


def whole_rows(rows):
    return lax.all_gather(rows, "seq", axis=0, tiled=True)


def apart_from_here(*values):
    return lax.optimization_barrier(values)


def spread(blocks, members):
    count = lax.axis_size("seq")
    runs = [list(range(i, i + members)) for i in range(0, count, members)]
    return lax.all_to_all(
        blocks, "seq", 0, 0, tiled=True, axis_index_groups=runs if len(runs) > 1 else None
    )


def entering(growth, state, members, backward):
    count = lax.axis_size("seq")
    runs = count // members
    mine = lax.axis_index("seq") // members
    step = -members if backward else members
    pairs = [(i, i + step) for i in range(count) if 0 <= i + step < count]
    total = jnp.zeros_like(state)
    for _ in range(runs - 1):
        total = lax.ppermute(growth * total + state, "seq", pairs)
    return total


CHUNK = 128
LANES = 128
SUBLANES = 8
VMEM_BYTES = 56 * 1024 * 1024


def split(values, terms):
    pieces = []
    for _ in range(terms):
        pieces.append(values.astype(BF))
        values = values - pieces[-1].astype(F32)
    return pieces


def product(left, right, dims=((1,), (0,))):
    total = None
    for i, a in enumerate(left):
        for j, b in enumerate(right):
            if i + j < max(len(left), len(right)):
                part = lax.dot_general(a, b, (dims, ((), ())), preferred_element_type=F32)
                total = part if total is None else total + part
    return total


ROWS_OF_BOTH = ((1,), (1,))


def columns(rows):
    count, extent = rows.shape
    return jnp.concatenate([rows, jnp.zeros((LANES - count, extent), F32)], axis=0).T


def lane_pair(left, right, half):
    lane = lax.broadcasted_iota(jnp.int32, (CHUNK, LANES), 1)
    return jnp.where(lane < half, left, right)


def apart(pair, half):
    lane = lax.broadcasted_iota(jnp.int32, pair.shape, 1)
    zero = jnp.zeros_like(pair)
    return jnp.concatenate([jnp.where(lane < half, pair, zero), jnp.where(lane < half, zero, pair)], 0)


def head_sums(values, half):
    lane = lax.broadcasted_iota(jnp.int32, values.shape, 1)
    first = jnp.sum(jnp.where(lane < half, values, 0.0), axis=1, keepdims=True)
    return first, jnp.sum(values, axis=1, keepdims=True) - first


def lasting(microseconds):
    return pl.CostEstimate(flops=int(microseconds * 3e8), bytes_accessed=0, transcendentals=0)


def forward_kernel(
    half, terms, place_ref, conv_ref, z_ref, bc0_ref, bc1_ref, bc2_ref, bc3_ref, rows_ref, skip_ref, gain_ref,
    out_low_ref, cot0_ref, cot1_ref, cot2_ref, cot3_ref, start_ref,
    mixed_ref, states_ref, end_ref, gated_ref, kept_ref, sent_ref, sums_ref, bc_ref, cot_ref, state_ref,
):
    step = pl.program_id(0)
    block = conv_ref.shape[0]
    span = conv_ref.shape[1]
    pairs = span // LANES

    @pl.when(step == 0)
    def _():
        state_ref[...] = start_ref[...]

    share = bc0_ref.shape[0]
    quarter = cot0_ref.shape[1]
    for distance, (bc, cot) in enumerate(
        zip((bc0_ref, bc1_ref, bc2_ref, bc3_ref), (cot0_ref, cot1_ref, cot2_ref, cot3_ref))
    ):
        place = place_ref[2] ^ distance
        bc_ref[pl.ds(pl.multiple_of(place * share, share), share)] = bc[...]
        cot_ref[pl.ds(pl.multiple_of(place * quarter, quarter), quarter)] = cot[0]
    state = 2 * share

    causal = lax.broadcasted_iota(jnp.int32, (CHUNK, CHUNK), 0) >= lax.broadcasted_iota(
        jnp.int32, (CHUNK, CHUNK), 1
    )
    for sub in range(block // CHUNK):
        here = slice(sub * CHUNK, (sub + 1) * CHUNK)
        rows = rows_ref[:, here]
        cols = columns(rows)
        bt_block = bc_ref[:state, here]
        c_block = bc_ref[state:, here].T
        scores = product([c_block], [bt_block])
        states_ref[sub] = state_ref[...]
        state_parts = split(state_ref[...], terms)
        carried = product([c_block], state_parts)
        weighted, grown = [], []
        for pair in range(pairs):
            lanes = slice(pair * LANES, (pair + 1) * LANES)
            first, second = 2 * pair, 2 * pair + 1
            x = silu(conv_ref[here, lanes])

            def pair_cols(table, offset):
                return lane_pair(
                    table[:, offset + first : offset + first + 1],
                    table[:, offset + second : offset + second + 1],
                    half,
                )

            cum = pair_cols(cols, SUBLANES)
            scaled = x * pair_cols(cols, 0)
            last = cum[CHUNK - 1 : CHUNK]
            growth = jnp.exp(cum)
            weighted.append(scaled * jnp.exp(last - cum))
            grown.append(growth[CHUNK - 1 : CHUNK])
            mixing = []
            for head in (first, second):
                gap = cols[:, SUBLANES + head : SUBLANES + head + 1] - rows[SUBLANES + head : SUBLANES + head + 1]
                mixing.append(jnp.exp(jnp.where(causal, gap, -1e30)) * scores)
            inner = product(
                split(jnp.concatenate(mixing, axis=1), terms), split(apart(scaled, half), terms)
            )
            mixed_ref[here, lanes] = inner + carried[:, lanes] * growth + skip_ref[:, lanes] * x
        fresh = product([bt_block], split(jnp.concatenate(weighted, axis=1), terms))
        state_ref[...] = jnp.concatenate(grown, axis=1) * state_ref[...] + fresh
    end_ref[...] = state_ref[...]
    gated = mixed_ref[...] * silu(z_ref[...])
    gated_low = (gated * gain_ref[...]).astype(BF)
    gated_ref[...] = gated_low
    partial = jnp.dot(gated_low, out_low_ref[...], preferred_element_type=F32)
    quarters = partial.reshape((2, 2) + kept_ref.shape[2:])
    low = place_ref[2] % 2
    kept_ref[:, 0] = jnp.where(low == 0, quarters[:, 0], quarters[:, 1])
    sent_ref[:, 0] = jnp.where(low == 0, quarters[:, 1], quarters[:, 0])
    squares = jnp.sum(gated * gated, axis=1, keepdims=True)
    slot = place_ref[1] + step * block + lax.broadcasted_iota(jnp.int32, (block, 1), 0)
    back = jnp.where(slot < place_ref[0], cot_ref[...].astype(F32), 0.0)
    scale = jnp.sum(back * partial, axis=1, keepdims=True)
    lane = lax.broadcasted_iota(jnp.int32, (block, LANES), 1)
    sums = jnp.where(lane == 0, squares, jnp.where(lane == 1, scale, 0.0))
    for sub in range(block // CHUNK):
        here = slice(sub * CHUNK, (sub + 1) * CHUNK)
        sums_ref[:, here] = sums[here].T[:SUBLANES]


def forward_scan(place, conv, z, bc, rows, skip, gain, out_low, cot, start, half, members):
    tokens, span = conv.shape
    share = bc[0].shape[0]
    quarter, width = cot[0].shape[1:]
    state = 2 * share
    block = tokens // members
    subs = block // CHUNK
    by_rows = lambda i, *_: (i, 0)
    by_lanes = lambda i, *_: (0, i)
    whole = lambda i, *_: (0, 0)
    halves = lambda i, *_: (0, i, 0, 0)
    return pl.pallas_call(
        functools.partial(forward_kernel, half, 2),
        grid_spec=pltpu.PrefetchScalarGridSpec(
            num_scalar_prefetch=1,
            grid=(members,),
            in_specs=[
                pl.BlockSpec((block, span), by_rows),
                pl.BlockSpec((block, span), by_rows),
            ]
            + [pl.BlockSpec((share, block), by_lanes)] * 4
            + [
                pl.BlockSpec((3 * SUBLANES, block), by_lanes),
                pl.BlockSpec((1, span), whole),
                pl.BlockSpec((1, span), whole),
                pl.BlockSpec((span, width), whole),
            ]
            + [pl.BlockSpec((1, quarter, width), lambda i, *_: (i, 0, 0))] * 4
            + [pl.BlockSpec((state, span), whole)],
            out_specs=[
                pl.BlockSpec((block, span), by_rows),
                pl.BlockSpec((subs, state, span), lambda i, *_: (i, 0, 0)),
                pl.BlockSpec((state, span), whole),
                pl.BlockSpec((block, span), by_rows),
                pl.BlockSpec((2, 1, quarter, width), halves),
                pl.BlockSpec((2, 1, quarter, width), halves),
                pl.BlockSpec((SUBLANES, block), by_lanes),
                pl.BlockSpec((2 * state, block), by_lanes),
                pl.BlockSpec((block, width), by_rows),
            ],
            scratch_shapes=[pltpu.VMEM((state, span), F32)],
        ),
        out_shape=[
            jax.ShapeDtypeStruct((tokens, span), F32),
            jax.ShapeDtypeStruct((tokens // CHUNK, state, span), F32),
            jax.ShapeDtypeStruct((state, span), F32),
            jax.ShapeDtypeStruct((tokens, span), BF),
            jax.ShapeDtypeStruct((2, members, quarter, width), F32),
            jax.ShapeDtypeStruct((2, members, quarter, width), F32),
            jax.ShapeDtypeStruct((SUBLANES, tokens), F32),
            jax.ShapeDtypeStruct((2 * state, tokens), BF),
            jax.ShapeDtypeStruct((tokens, width), BF),
        ],
        compiler_params=pltpu.CompilerParams(vmem_limit_bytes=VMEM_BYTES),
        cost_estimate=lasting(17),
    )(place, conv, z, *bc, rows, skip, gain, out_low, *cot, start)


def gate_kernel(
    inner_all, place_ref, cot_ref, norm_ref, z_ref, mixed_ref, gain_ref, out_turned_ref,
    grad_mixed_ref, grad_z_ref, grad_summed_ref, gain_grad_ref,
):
    step = pl.program_id(0)
    block = cot_ref.shape[0]
    norm = jnp.concatenate(
        [columns(norm_ref[:, sub * CHUNK : (sub + 1) * CHUNK]) for sub in range(block // CHUNK)], 0
    )
    norm_scale, grad_scale = norm[:, 0:1], norm[:, 1:2]
    slot = place_ref[1] + step * block + lax.broadcasted_iota(jnp.int32, (block, 1), 0)
    back = jnp.where(slot < place_ref[0], cot_ref[...].astype(F32), 0.0)
    grad_summed = (norm_scale * back).astype(BF)
    grad_summed_ref[...] = grad_summed
    grad_low = jnp.dot(grad_summed, out_turned_ref[...], preferred_element_type=F32)
    z, mixed = z_ref[...], mixed_ref[...]
    sigmoid = jax.nn.sigmoid(z)
    gate = z * sigmoid
    gated = mixed * gate
    shrink = grad_scale * norm_scale * norm_scale * norm_scale / inner_all
    grad_gated = grad_low * gain_ref[...] - shrink * gated
    grad_mixed_ref[...] = grad_gated * gate
    grad_z_ref[...] = (grad_gated * mixed * (sigmoid * (1.0 + z * (1.0 - sigmoid)))).astype(BF)

    @pl.when(step == 0)
    def _():
        gain_grad_ref[...] = jnp.zeros_like(gain_grad_ref)

    gain_grad_ref[...] += jnp.sum(grad_low * gated, axis=0, keepdims=True)


def gate_back(place, cot, norm_rows, z, mixed, gain, out_turned, inner_all, members):
    tokens, span = z.shape
    width = cot.shape[1]
    block = tokens // members
    by_rows = lambda i, *_: (i, 0)
    whole = lambda i, *_: (0, 0)
    return pl.pallas_call(
        functools.partial(gate_kernel, inner_all),
        grid_spec=pltpu.PrefetchScalarGridSpec(
            num_scalar_prefetch=1,
            grid=(members,),
            in_specs=[
                pl.BlockSpec((block, width), by_rows),
                pl.BlockSpec((SUBLANES, block), lambda i, *_: (0, i)),
                pl.BlockSpec((block, span), by_rows),
                pl.BlockSpec((block, span), by_rows),
                pl.BlockSpec((1, span), whole),
                pl.BlockSpec((width, span), whole),
            ],
            out_specs=[
                pl.BlockSpec((block, span), by_rows),
                pl.BlockSpec((block, span), by_rows),
                pl.BlockSpec((block, width), by_rows),
                pl.BlockSpec((1, span), whole),
            ],
        ),
        out_shape=[
            jax.ShapeDtypeStruct((tokens, span), F32),
            jax.ShapeDtypeStruct((tokens, span), BF),
            jax.ShapeDtypeStruct((tokens, width), BF),
            jax.ShapeDtypeStruct((1, span), F32),
        ],
        compiler_params=pltpu.CompilerParams(vmem_limit_bytes=VMEM_BYTES),
        cost_estimate=lasting(12),
    )(place, cot, norm_rows, z, mixed, gain, out_turned)


def backward_kernel(
    half, terms, taps, low_ref, grad_ref, conv_ref, conv_in_ref, bc_ref, rows_ref,
    states_ref, end_ref, skip_ref, weight_ref, rate_ref, back_ref, halo_ref,
    grad_x_ref, kept_ref, sent_ref, first_ref, edge_ref, small_ref, pre_ref, sums_ref,
    carry_ref, after_ref, shift_ref,
):
    step = pl.program_id(0)
    block = conv_ref.shape[0]
    span = conv_ref.shape[1]
    pairs = span // LANES
    state = bc_ref.shape[0] // 2
    subs = block // CHUNK

    @pl.when(step == 0)
    def _():
        carry_ref[...] = back_ref[...]
        after_ref[...] = end_ref[...]
        shift_ref[:SUBLANES] = halo_ref[...]
        small_ref[...] = jnp.zeros_like(small_ref)
        sums_ref[...] = jnp.zeros_like(sums_ref)

    low = low_ref[0]
    row = lax.broadcasted_iota(jnp.int32, (CHUNK, CHUNK), 0)
    lane = lax.broadcasted_iota(jnp.int32, (CHUNK, CHUNK), 1)
    causal = row <= lane
    for sub in reversed(range(subs)):
        here = slice(sub * CHUNK, (sub + 1) * CHUNK)
        rows = rows_ref[:, here]
        cols = columns(rows)
        bt_block, ct_block = bc_ref[:state, here], bc_ref[state:, here]
        b_block, c_block = bt_block.T, ct_block.T
        scores = product([b_block], [ct_block])
        entered = states_ref[sub]
        carry = carry_ref[...]
        entered_parts = split(entered, terms)
        carry_parts = split(carry, terms)
        carried = product([c_block], entered_parts)
        pulled = product([b_block], carry_parts)
        joint = jnp.sum(carry * after_ref[...], axis=0, keepdims=True)
        after_ref[...] = entered
        head_of = lax.broadcasted_iota(jnp.int32, (SUBLANES, span), 1) // half
        joint = jnp.sum(
            jnp.where(head_of == lax.broadcasted_iota(jnp.int32, (SUBLANES, span), 0), joint, 0.0),
            axis=1,
            keepdims=True,
        )
        weighted, grown_grad, grown = [], [], []
        grad_scores = jnp.zeros((CHUNK, CHUNK), F32)
        col_sums = jnp.zeros((CHUNK, LANES), F32)
        row_sums = []
        for pair in range(pairs):
            lanes = slice(pair * LANES, (pair + 1) * LANES)
            first, second = 2 * pair, 2 * pair + 1

            def pair_cols(offset):
                return lane_pair(
                    cols[:, offset + first : offset + first + 1],
                    cols[:, offset + second : offset + second + 1],
                    half,
                )

            conv = conv_ref[here, lanes]
            sigmoid = jax.nn.sigmoid(conv)
            x = conv * sigmoid
            grad = grad_ref[here, lanes]
            cum, size = pair_cols(SUBLANES), pair_cols(0)
            scaled = x * size
            last = cum[CHUNK - 1 : CHUNK]
            growth = jnp.exp(cum)
            tail = jnp.exp(last - cum)
            weighted.append(scaled * tail)
            grown_grad.append(grad * growth)
            grown.append(growth[CHUNK - 1 : CHUNK])
            grad_apart = split(apart(grad, half), terms)
            dots = product(split(scaled, terms), grad_apart, ROWS_OF_BOTH)
            kernels = []
            for k, head in enumerate((first, second)):
                gap = rows[SUBLANES + head : SUBLANES + head + 1] - cols[:, SUBLANES + head : SUBLANES + head + 1]
                decay = jnp.exp(jnp.where(causal, gap, -1e30))
                grad_score = decay * dots[:, k * CHUNK : (k + 1) * CHUNK]
                grad_scores = grad_scores + grad_score
                kernels.append(decay * scores)
                both = grad_score * scores
                row_sums.append(jnp.sum(both, axis=0, keepdims=True))
                col_sums = jnp.where(
                    lane == head, col_sums - jnp.sum(both, axis=1, keepdims=True), col_sums
                )
            pulled_pair = tail * pulled[:, lanes]
            force = product(split(jnp.concatenate(kernels, axis=1), terms), grad_apart) + pulled_pair
            grad_x = size * force + skip_ref[:, lanes] * grad
            flow = grown_grad[-1] * carried[:, lanes] - scaled * pulled_pair
            direct = x * force
            for head, flow_sum, direct_sum in zip(
                (first, second), head_sums(flow, half), head_sums(direct, half)
            ):
                col_sums = jnp.where(lane == head, col_sums + flow_sum, col_sums)
                col_sums = jnp.where(lane == SUBLANES + head, direct_sum, col_sums)
            small_ref[taps + 1 : taps + 2, lanes] += jnp.sum(grad * x, axis=0, keepdims=True)
            grad_conv = (grad_x * (sigmoid * (1.0 + conv * (1.0 - sigmoid)))).astype(BF).astype(F32)
            shift_ref[CHUNK : CHUNK + SUBLANES, lanes] = shift_ref[:SUBLANES, lanes]
            shift_ref[:CHUNK, lanes] = grad_conv
            conv_in = conv_in_ref[here, lanes].astype(F32)
            total = None
            for tap in range(taps):
                moved = shift_ref[taps - 1 - tap : taps - 1 - tap + CHUNK, lanes]
                term = weight_ref[tap : tap + 1, lanes] * moved
                total = term if total is None else total + term
                small_ref[tap : tap + 1, lanes] += jnp.sum(conv_in * moved, axis=0, keepdims=True)
            small_ref[taps : taps + 1, lanes] += jnp.sum(grad_conv, axis=0, keepdims=True)
            grad_x_ref[here, lanes] = total.astype(BF)
        grown_parts = split(jnp.concatenate(grown_grad, axis=1), terms)
        weighted_parts = split(jnp.concatenate(weighted, axis=1), terms)
        grad_b = product(carry_parts, weighted_parts, ROWS_OF_BOTH) + product(
            [ct_block], split(grad_scores.T, terms)
        )
        grad_c = product(entered_parts, grown_parts, ROWS_OF_BOTH) + product(
            [bt_block], split(grad_scores, terms)
        )
        middle = state // 2
        for k, part in enumerate((grad_b, grad_c)):
            place = slice(k * middle, (k + 1) * middle)
            kept_ref[place, here] = jnp.where(low == 0, part[:middle], part[middle:])
            sent_ref[place, here] = jnp.where(low == 0, part[middle:], part[:middle])
        carry_ref[...] = jnp.concatenate(grown, axis=1) * carry + product([ct_block], grown_parts)
        turned = col_sums.T
        row_sums.append(jnp.zeros((SUBLANES - 2 * pairs, CHUNK), F32))
        slots = lax.broadcasted_iota(jnp.int32, (SUBLANES, CHUNK), 1)
        grad_cum = (
            jnp.concatenate(row_sums, axis=0)
            + turned[:SUBLANES]
            + jnp.where(slots == CHUNK - 1, joint, 0.0)
        )
        grad_decay = product(split(grad_cum, 3), [(row >= lane).astype(BF)])
        grad_pre = (turned[SUBLANES : 2 * SUBLANES] + grad_decay * rate_ref[...]) * rows[2 * SUBLANES :]
        pre_ref[:, here] = grad_pre
        sums_ref[:SUBLANES] += grad_pre
        sums_ref[SUBLANES:] += grad_decay * rows[:SUBLANES]
    first_ref[...] = carry_ref[...]
    edge_ref[...] = shift_ref[:SUBLANES]


def backward_scan(
    low, grad, conv, conv_in, bc, rows, states, end, skip, weight, rate, back, halo, half,
    members,
):
    tokens, span = conv.shape
    state = bc.shape[0] // 2
    taps = weight.shape[0]
    block = tokens // members
    subs = block // CHUNK
    final = members - 1
    by_rows = lambda i, *_: (final - i, 0)
    by_lanes = lambda i, *_: (0, final - i)
    whole = lambda i, *_: (0, 0)
    return pl.pallas_call(
        functools.partial(backward_kernel, half, 2, taps),
        grid_spec=pltpu.PrefetchScalarGridSpec(
        num_scalar_prefetch=1,
        grid=(members,),
        in_specs=[
            pl.BlockSpec((block, span), by_rows),
            pl.BlockSpec((block, span), by_rows),
            pl.BlockSpec((block, span), by_rows),
            pl.BlockSpec((2 * state, block), by_lanes),
            pl.BlockSpec((3 * SUBLANES, block), by_lanes),
            pl.BlockSpec((subs, state, span), lambda i, *_: (final - i, 0, 0)),
            pl.BlockSpec((state, span), whole),
            pl.BlockSpec((1, span), whole),
            pl.BlockSpec((taps, span), whole),
            pl.BlockSpec((SUBLANES, 1), whole),
            pl.BlockSpec((state, span), whole),
            pl.BlockSpec((SUBLANES, span), whole),
        ],
        out_specs=[
            pl.BlockSpec((block, span), by_rows),
            pl.BlockSpec((state, block), by_lanes),
            pl.BlockSpec((state, block), by_lanes),
            pl.BlockSpec((state, span), whole),
            pl.BlockSpec((SUBLANES, span), whole),
            pl.BlockSpec((SUBLANES, span), whole),
            pl.BlockSpec((SUBLANES, block), by_lanes),
            pl.BlockSpec((2 * SUBLANES, LANES), whole),
        ],
        scratch_shapes=[
            pltpu.VMEM((state, span), F32),
            pltpu.VMEM((state, span), F32),
            pltpu.VMEM((CHUNK + SUBLANES, span), F32),
        ],
        ),
        out_shape=[
            jax.ShapeDtypeStruct((tokens, span), BF),
            jax.ShapeDtypeStruct((state, tokens), F32),
            jax.ShapeDtypeStruct((state, tokens), F32),
            jax.ShapeDtypeStruct((state, span), F32),
            jax.ShapeDtypeStruct((SUBLANES, span), F32),
            jax.ShapeDtypeStruct((SUBLANES, span), F32),
            jax.ShapeDtypeStruct((SUBLANES, tokens), F32),
            jax.ShapeDtypeStruct((2 * SUBLANES, LANES), F32),
        ],
        compiler_params=pltpu.CompilerParams(vmem_limit_bytes=VMEM_BYTES),
        cost_estimate=lasting(25),
    )(
        scalars(low), grad, conv, conv_in, bc, rows, states, end, skip, weight,
        jnp.pad(rate, ((0, SUBLANES - rate.shape[0]), (0, 0))), back, halo,
    )


def vmem(count):
    return [pl.BlockSpec(memory_space=pltpu.VMEM)] * count


def scalars(*values):
    return jnp.stack(values).astype(jnp.int32)


def stage(kernel, out_shape, operands, smem=0, micros=0.01):
    return pl.pallas_call(
        kernel,
        out_shape=out_shape,
        in_specs=[pl.BlockSpec(memory_space=pltpu.SMEM)] * smem + vmem(len(operands) - smem),
        out_specs=jax.tree.map(lambda _: pl.BlockSpec(memory_space=pltpu.VMEM), out_shape),
        compiler_params=pltpu.CompilerParams(vmem_limit_bytes=VMEM_BYTES),
        cost_estimate=lasting(micros),
    )(*operands)


def shaped(shape, dtype=F32):
    return jax.ShapeDtypeStruct(shape, dtype)


def add_kernel(a_ref, b_ref, out_ref):
    out_ref[...] = a_ref[...] + b_ref[...].astype(F32)


def added(a, b):
    return stage(add_kernel, shaped(a.shape), [a, b])


def split_kernel(axis, high_ref, kept_ref, come_ref, own_ref, sent_ref):
    high = high_ref[0]
    total = [
        kept_ref[(slice(None),) * axis + (k,)] + come_ref[(slice(None),) * axis + (k,)] for k in (0, 1)
    ]
    own_ref[...] = jnp.where(high == 0, total[0], total[1])
    sent_ref[...] = jnp.where(high == 0, total[1], total[0]).astype(BF)


def split_halves(kept, come, axis, high):
    shape = kept.shape[:axis] + kept.shape[axis + 1 :]
    return stage(
        functools.partial(split_kernel, axis),
        [shaped(shape), shaped(shape, BF)],
        [scalars(high), kept, come],
        smem=1,
    )


def rows_kernel(pieces, *refs):
    old_ref, sum_ref, mom_ref = refs[pieces:]
    left = 0
    for ref in refs[:pieces]:
        cols = slice(left, left + ref.shape[2])
        left = cols.stop
        total = jnp.sum(ref[...].astype(F32), axis=0)
        sum_ref[:, cols] = total
        mom_ref[:, cols] = 0.5 * old_ref[:, cols] + total


def rows_step(come, old):
    return stage(
        functools.partial(rows_kernel, len(come)), [shaped(old.shape), shaped(old.shape)], [*come, old]
    )


def weight_kernel(turned_ref, grad_ref, out_ref):
    out_ref[...] = jnp.dot(turned_ref[...], grad_ref[...], preferred_element_type=F32).astype(BF)


def weight_grad(turned, grad):
    return stage(weight_kernel, shaped((turned.shape[0], grad.shape[1]), BF), [turned, grad])


def side_kernel(taps, kept_ref, come_ref, conv_ref, conv_in_ref, weight_ref, halo_ref, pre_ref, turned_ref,
                side_ref, small_ref, out_ref):
    tokens = kept_ref.shape[1]
    conv = conv_ref[...]
    sigmoid = jax.nn.sigmoid(conv)
    slope = sigmoid * (1.0 + conv * (1.0 - sigmoid))
    grad = ((kept_ref[...] + come_ref[...].astype(F32)) * slope).astype(BF).astype(F32)
    conv_in = conv_in_ref[...].astype(F32)
    wide = jnp.concatenate([grad, halo_ref[...]], axis=1)
    lane = lax.broadcasted_iota(jnp.int32, small_ref.shape, 1)
    small = jnp.where(lane == taps, jnp.sum(grad, axis=1, keepdims=True), 0.0)
    total = None
    for tap in range(taps):
        lead = taps - 1 - tap
        moved = pltpu.roll(wide, wide.shape[1] - lead, 1)[:, :tokens] if lead else grad
        term = weight_ref[:, tap : tap + 1] * moved
        total = term if total is None else total + term
        small = jnp.where(lane == tap, jnp.sum(moved * conv_in, axis=1, keepdims=True), small)
    small_ref[...] = small
    used = total.shape[0] + pre_ref.shape[0]
    spare = jnp.zeros((LANES - used, tokens), F32)
    side = jnp.concatenate([total, pre_ref[...], spare], axis=0).astype(BF).T
    side_ref[:, :LANES] = side
    if side_ref.shape[1] > LANES:
        side_ref[:, LANES:] = jnp.zeros((tokens, side_ref.shape[1] - LANES), BF)
    out_ref[:, :LANES] = jnp.dot(turned_ref[...], side, preferred_element_type=F32).astype(BF)
    if out_ref.shape[1] > LANES:
        out_ref[:, LANES:] = jnp.zeros((out_ref.shape[0], out_ref.shape[1] - LANES), BF)


def lowered_kernel(
    low_ref, z_ref, x_ref, side_ref, weight_ref, data_ref, root_ref, kept_ref, sent_ref, gain_ref
):
    step = pl.program_id(0)
    span = z_ref.shape[1]
    total = jnp.dot(z_ref[...], weight_ref[:span], preferred_element_type=F32)
    total = total + jnp.dot(x_ref[...], weight_ref[span : 2 * span], preferred_element_type=F32)
    total = total + jnp.dot(side_ref[...], weight_ref[2 * span :], preferred_element_type=F32)
    normed = data_ref[...].astype(F32) * root_ref[...]

    @pl.when(step == 0)
    def _():
        gain_ref[...] = jnp.zeros_like(gain_ref)

    gain_ref[...] += jnp.sum(total * normed, axis=0, keepdims=True)
    parts = total.reshape((2, 2) + kept_ref.shape[2:])
    low = low_ref[0]
    kept_ref[0] = jnp.where(low == 0, parts[:, 0], parts[:, 1])
    sent_ref[0] = jnp.where(low == 0, parts[:, 1], parts[:, 0])


def lowered_grad(low, grad_z, grad_x, side, weight, data, root, members):
    tokens, width = data.shape
    block = tokens // members
    by_rows = lambda i, *_: (i, 0)
    whole = lambda i, *_: (0, 0)
    half = (1, 2, block // 4, width)
    return pl.pallas_call(
        lowered_kernel,
        grid_spec=pltpu.PrefetchScalarGridSpec(
            num_scalar_prefetch=1,
            grid=(members,),
            in_specs=[
                pl.BlockSpec((block, grad_z.shape[1]), by_rows),
                pl.BlockSpec((block, grad_x.shape[1]), by_rows),
                pl.BlockSpec((block, side.shape[1]), by_rows),
                pl.BlockSpec(weight.shape, whole),
                pl.BlockSpec((block, width), by_rows),
                pl.BlockSpec((block, 1), by_rows),
            ],
            out_specs=[
                pl.BlockSpec(half, lambda i, *_: (i, 0, 0, 0)),
                pl.BlockSpec(half, lambda i, *_: (i, 0, 0, 0)),
                pl.BlockSpec((1, width), whole),
            ],
        ),
        out_shape=[
            shaped((members,) + half[1:]),
            shaped((members,) + half[1:]),
            shaped((1, width)),
        ],
        compiler_params=pltpu.CompilerParams(vmem_limit_bytes=VMEM_BYTES),
        cost_estimate=lasting(0.01),
    )(scalars(low), grad_z, grad_x, side, weight, data, root)


def result_kernel(kept_ref, come_ref, data_ref, norm_ref, mask_ref, out_ref, squares_ref):
    result = kept_ref[...] + come_ref[...].astype(F32)
    result = mask_ref[...] * (data_ref[...].astype(F32) + norm_ref[...] * result)
    out_ref[...] = result.astype(BF)
    squares_ref[...] = jnp.sum(result * result, axis=(0, 1), keepdims=True)[0]


def input_kernel(kept_ref, come_ref, data_ref, cot_ref, root_ref, mask_ref, gain_ref, result_ref, out_ref):
    quarter = kept_ref.shape[1]
    grad = (kept_ref[...] + come_ref[...].astype(F32)) * gain_ref[...]
    normed = data_ref[...].astype(F32) * root_ref[...]
    shrink = jnp.mean(grad * normed, axis=-1, keepdims=True)
    back = mask_ref[...] * cot_ref[...].astype(F32)
    out_ref[:, :quarter] = result_ref[...]
    out_ref[:, quarter:] = (back + root_ref[...] * (grad - normed * shrink)).astype(BF)


def small_kernel(small_ref, bc_ref, sums_ref, gate_ref, gain_ref, squares_ref, out_ref):
    out_ref[...] = jnp.zeros_like(out_ref)
    row = 0
    for k in range(small_ref.shape[1] // LANES):
        out_ref[row : row + SUBLANES] = small_ref[:, k * LANES : (k + 1) * LANES]
        row += SUBLANES
    turned = bc_ref[...].T[:SUBLANES]
    out_ref[row : row + SUBLANES, : turned.shape[1]] = turned
    row += SUBLANES
    out_ref[row : row + 2 * SUBLANES] = sums_ref[...]
    row += 2 * SUBLANES
    for ref in (gate_ref, gain_ref, squares_ref):
        for k in range(ref.shape[1] // LANES):
            out_ref[row : row + 1] = ref[:, k * LANES : (k + 1) * LANES]
            row += 1


def order_kernel(place_ref, *refs):
    output_ref, grad_ref = refs[4:]
    quarter = refs[0].shape[1] // 2
    for distance, ref in enumerate(refs[:4]):
        start = pl.multiple_of((place_ref[0] ^ distance) * quarter, quarter)
        output_ref[0, pl.ds(start, quarter)] = ref[0, :quarter]
        grad_ref[0, pl.ds(start, quarter)] = ref[0, quarter:].astype(F32)


def in_order(place, pieces):
    members, both, width = pieces[0].shape
    rows = 2 * both
    block = lambda i, *_: (i, 0, 0)
    return pl.pallas_call(
        order_kernel,
        grid_spec=pltpu.PrefetchScalarGridSpec(
            num_scalar_prefetch=1,
            grid=(members,),
            in_specs=[pl.BlockSpec((1, both, width), block)] * 4,
            out_specs=[pl.BlockSpec((1, rows, width), block)] * 2,
        ),
        out_shape=[shaped((members, rows, width), BF), shaped((members, rows, width))],
        compiler_params=pltpu.CompilerParams(vmem_limit_bytes=VMEM_BYTES),
        cost_estimate=lasting(5),
    )(scalars(place), *pieces)


def norm_kernel(inner_all, mine_ref, come_ref, out_ref):
    total = mine_ref[...] + come_ref[...]
    row = lax.broadcasted_iota(jnp.int32, total.shape, 0)
    out_ref[...] = jnp.where(row == 0, lax.rsqrt(total / inner_all + EPSILON), total)


def enter_kernel(
    taps, heads, place_ref, own_ref, beside_ref, across_ref, corner_ref, gain_ref, side_weight_ref, weight_ref,
    halo_ref, params_ref, data_ref, lowered_ref, root_ref, bc_ref, conv_ref, conv_in_ref, rows_ref, carry_ref,
):
    quarter = own_ref.shape[1]
    block = data_ref.shape[0]
    channels = bc_ref.shape[0]
    for distance, ref in enumerate((own_ref, beside_ref, across_ref, corner_ref)):
        start = pl.multiple_of((place_ref[0] ^ distance) * quarter, quarter)
        data_ref[pl.ds(start, quarter)] = ref[0]
    data = data_ref[...].astype(F32)
    root = lax.rsqrt(jnp.mean(data * data, axis=1, keepdims=True) + EPSILON)
    root_ref[...] = root
    lowered = (data * root * gain_ref[...]).astype(BF)
    lowered_ref[...] = lowered
    side = lax.dot_general(
        side_weight_ref[...], lowered, (ROWS_OF_BOTH, ((), ())), preferred_element_type=F32
    )

    @pl.when(pl.program_id(0) == 0)
    def _():
        carry_ref[...] = halo_ref[...]

    conv_low = side[:channels].astype(BF)
    conv_in_ref[...] = conv_low
    conv_in = conv_low.astype(F32)
    wide = jnp.concatenate([carry_ref[...], conv_in], axis=1)
    carry_ref[...] = conv_in[:, block - LANES :]
    conv = weight_ref[:, taps : taps + 1] + weight_ref[:, taps - 1 : taps] * conv_in
    for tap in range(taps - 1):
        conv = conv + weight_ref[:, tap : tap + 1] * pltpu.roll(wide, taps - 1 - tap, 1)[:, LANES:]
    conv_ref[...] = conv
    bc_ref[...] = silu(conv).astype(BF)

    head = lax.broadcasted_iota(jnp.int32, (SUBLANES, block), 0)
    pre = side[channels : channels + SUBLANES] + params_ref[:, 0:1]
    size = jnp.where(head < heads, jax.nn.softplus(pre), 0.0)
    change = size * params_ref[:, 1:2]
    row = lax.broadcasted_iota(jnp.int32, (CHUNK, CHUNK), 0)
    upto = (row <= lax.broadcasted_iota(jnp.int32, (CHUNK, CHUNK), 1)).astype(BF)
    rows_ref[:SUBLANES] = size
    for sub in range(block // CHUNK):
        here = slice(sub * CHUNK, (sub + 1) * CHUNK)
        rows_ref[SUBLANES : 2 * SUBLANES, here] = product(split(change[:, here], 3), [upto])
    rows_ref[2 * SUBLANES :] = jnp.where(head < heads, jax.nn.sigmoid(pre), 0.0)


def enter(place, pieces, gain, side_weight, weight, halo, params, taps, heads, channels):
    members, quarter, width = pieces[0].shape
    block = 4 * quarter
    tokens = members * block
    by_rows = lambda i, *_: (i, 0)
    by_lanes = lambda i, *_: (0, i)
    whole = lambda i, *_: (0, 0)
    return pl.pallas_call(
        functools.partial(enter_kernel, taps, heads),
        grid_spec=pltpu.PrefetchScalarGridSpec(
            num_scalar_prefetch=1,
            grid=(members,),
            in_specs=[pl.BlockSpec((1, quarter, width), lambda i, *_: (i, 0, 0))] * 4
            + [
                pl.BlockSpec((1, width), whole),
                pl.BlockSpec(side_weight.shape, whole),
                pl.BlockSpec(weight.shape, whole),
                pl.BlockSpec(halo.shape, whole),
                pl.BlockSpec(params.shape, whole),
            ],
            out_specs=[
                pl.BlockSpec((block, width), by_rows),
                pl.BlockSpec((block, width), by_rows),
                pl.BlockSpec((block, 1), by_rows),
                pl.BlockSpec((channels, block), by_lanes),
                pl.BlockSpec((channels, block), by_lanes),
                pl.BlockSpec((channels, block), by_lanes),
                pl.BlockSpec((3 * SUBLANES, block), by_lanes),
            ],
            scratch_shapes=[pltpu.VMEM((channels, LANES), F32)],
        ),
        out_shape=[
            jax.ShapeDtypeStruct((tokens, width), BF),
            jax.ShapeDtypeStruct((tokens, width), BF),
            jax.ShapeDtypeStruct((tokens, 1), F32),
            jax.ShapeDtypeStruct((channels, tokens), BF),
            jax.ShapeDtypeStruct((channels, tokens), F32),
            jax.ShapeDtypeStruct((channels, tokens), BF),
            jax.ShapeDtypeStruct((3 * SUBLANES, tokens), F32),
        ],
        compiler_params=pltpu.CompilerParams(vmem_limit_bytes=VMEM_BYTES),
        cost_estimate=lasting(8),
    )(scalars(place), *pieces, gain, side_weight, weight, halo, params)


def columns_kernel(
    taps, lowered_ref, z_weight_ref, x_weight_ref, weight_ref, bias_ref, halo_ref, z_ref, x_in_ref, conv_ref,
    shift_ref,
):
    block = lowered_ref.shape[0]
    lowered = lowered_ref[...]
    z_ref[...] = jnp.dot(lowered, z_weight_ref[...], preferred_element_type=F32)
    conv_low = jnp.dot(lowered, x_weight_ref[...], preferred_element_type=F32).astype(BF)
    x_in_ref[...] = conv_low

    @pl.when(pl.program_id(0) == 0)
    def _():
        shift_ref[:SUBLANES] = halo_ref[...]

    shift_ref[SUBLANES:] = conv_low.astype(F32)
    conv = jnp.broadcast_to(bias_ref[...], conv_ref.shape)
    for tap in range(taps):
        first = SUBLANES - (taps - 1) + tap
        conv = conv + weight_ref[tap : tap + 1] * shift_ref[first : first + block]
    conv_ref[...] = conv
    shift_ref[:SUBLANES] = shift_ref[block:]


def z_and_x(lowered, z_weight, x_weight, weight, bias, halo, members):
    tokens, width = lowered.shape
    span = z_weight.shape[1]
    block = tokens // members
    by_rows = lambda i: (i, 0)
    whole = lambda i: (0, 0)
    return pl.pallas_call(
        functools.partial(columns_kernel, weight.shape[0]),
        grid=(members,),
        in_specs=[
            pl.BlockSpec((block, width), by_rows),
            pl.BlockSpec((width, span), whole),
            pl.BlockSpec((width, span), whole),
            pl.BlockSpec(weight.shape, whole),
            pl.BlockSpec((1, span), whole),
            pl.BlockSpec((SUBLANES, span), whole),
        ],
        out_specs=[pl.BlockSpec((block, span), by_rows)] * 3,
        out_shape=[
            jax.ShapeDtypeStruct((tokens, span), F32),
            jax.ShapeDtypeStruct((tokens, span), BF),
            jax.ShapeDtypeStruct((tokens, span), F32),
        ],
        scratch_shapes=[pltpu.VMEM((block + SUBLANES, span), F32)],
        compiler_params=pltpu.CompilerParams(vmem_limit_bytes=VMEM_BYTES),
        cost_estimate=lasting(8),
    )(lowered, z_weight, x_weight, weight, bias, halo)


TILE = 256


def tiles_of(width):
    starts = range(0, width, TILE)
    return [(i, j) for i in starts for j in starts if i <= j]


def at(start):
    return slice(start, start + TILE)


def put(pair, i, j, values):
    for row, col, tile in ((i, j, values), (j, i, values.T))[: 1 if i == j else 2]:
        high = tile.astype(BF)
        pair[0, at(row), at(col)] = high
        pair[1, at(row), at(col)] = (tile - high.astype(F32)).astype(BF)


def tile_of(left, right, i, j):
    high, low = left[0, at(i)], left[1, at(i)]
    total = jnp.dot(high, right[1, :, at(j)], preferred_element_type=F32)
    total = total + jnp.dot(low, right[0, :, at(j)], preferred_element_type=F32)
    return total + jnp.dot(high, right[0, :, at(j)], preferred_element_type=F32)


def eye(rows, cols):
    return lax.broadcasted_iota(jnp.int32, (rows, cols), 0) == lax.broadcasted_iota(
        jnp.int32, (rows, cols), 1
    )


def newton_kernel(opens, closes, steps, *refs):
    refs = list(refs)
    low_ref = refs.pop(0) if opens else None
    gram_in = refs.pop(0)
    other_in = refs.pop(0) if opens else None
    factor_in = None if opens else refs.pop(0)
    before = [refs.pop(0)] if closes and not opens else []
    picked_ref = refs.pop(0) if closes else None
    gram_out = refs.pop(0) if not closes else None
    rows_ref = refs.pop(0) if closes else None
    factor_out = refs.pop(0) if opens and not closes else None
    polys = refs.pop(0) if steps else None
    gram, first, second, third = refs
    width = gram.shape[0]
    tiles = tiles_of(width)
    if opens:
        low = low_ref[0]
        upper = jnp.where(low == 0, gram_in[:TILE], other_in[:TILE])
        lower = jnp.where(low == 0, other_in[:TILE], gram_in[:TILE])
        gram[at(0)] = upper
        gram[at(TILE), TILE:] = lower[:, : width - TILE]
        gram[at(2 * TILE), 2 * TILE :] = lower[:, width - TILE :]
        size = jnp.zeros((1, 1), F32)
        for i in range(0, width, TILE):
            size = size + jnp.sum(jnp.where(eye(TILE, TILE), gram[at(i), at(i)], 0.0), keepdims=True)
        factor = 1.0 / (jnp.sqrt(size) + 1e-07)
        if factor_out is not None:
            factor_out[...] = jnp.broadcast_to(factor, factor_out.shape)
    else:
        factor = factor_in[0:1, 0:1]
    for i, j in tiles:
        values = gram[at(i), at(j)] * (factor * factor) if opens else gram_in[at(i), at(j)]
        gram[at(i), at(j)] = values
        put(first, i, j, values)
    for step in range(steps):
        for i, j in tiles:
            square = tile_of(first, first, i, j)
            put(second, i, j, square)
            held = gram[at(i), at(j)]
            poly = COEF_B * held + COEF_C * square
            put(polys.at[step], i, j, jnp.where(eye(TILE, TILE), COEF_A, 0.0) + poly if i == j else poly)
            gram[at(i), at(j)] = COEF_A * held + COEF_B * square
        for i, j in tiles:
            put(third, i, j, gram[at(i), at(j)] + COEF_C * tile_of(second, first, i, j))
        for i, j in tiles:
            values = tile_of(third, polys.at[step], i, j)
            gram[at(i), at(j)] = values
            put(first, i, j, values)
    if not closes:
        for i, j in tiles:
            gram_out[at(i), at(j)] = gram[at(i), at(j)]
        return
    picked = picked_ref[...]
    held = [jnp.dot(picked, first[k], preferred_element_type=F32) for k in range(2)]
    rows = COEF_A * picked.astype(F32) + COEF_B * (held[0] + held[1])
    rows = rows + COEF_C * product([part.astype(BF) for part in held], [first[0], first[1]])
    chain = [(ref, k) for ref in before for k in range(ref.shape[0])]
    chain += [(polys, k) for k in range(steps)]
    for ref, k in reversed(chain):
        rows = product(split(rows, 2), [ref[k, 0], ref[k, 1]])
    rows_ref[...] = rows * factor


def newton_call(opens, closes, steps, micros, operands, picked, width):
    pair = pltpu.VMEM((2, width, width), BF)
    whole = pl.BlockSpec(memory_space=pltpu.VMEM)
    out_shape = []
    if closes:
        operands = operands + [picked]
        out_shape.append(jax.ShapeDtypeStruct(picked.shape, F32))
    else:
        out_shape.append(jax.ShapeDtypeStruct((width, width), F32))
        if opens:
            out_shape.append(jax.ShapeDtypeStruct((SUBLANES, LANES), F32))
        out_shape.append(jax.ShapeDtypeStruct((steps, 2, width, width), BF))
    kept = [pltpu.VMEM((steps, 2, width, width), BF)] if closes and steps else []
    return pl.pallas_call(
        functools.partial(newton_kernel, opens, closes, steps),
        out_shape=out_shape,
        in_specs=([pl.BlockSpec(memory_space=pltpu.SMEM)] if opens else [])
        + [whole] * (len(operands) - opens),
        out_specs=[whole] * len(out_shape),
        scratch_shapes=kept + [pltpu.VMEM((width, width), F32), pair, pair, pair],
        compiler_params=pltpu.CompilerParams(vmem_limit_bytes=VMEM_BYTES),
        cost_estimate=lasting(micros),
    )(*operands)


def newton_rows(pack, other, picked):
    low = scalars(lax.axis_index("head") % 2)
    return newton_call(True, True, NS_STEPS - 1, 30, [low, pack, other], picked, pack.shape[1])[0]


def newton_opening(pack, other):
    low = scalars(lax.axis_index("head") % 2)
    return newton_call(True, False, 2, 15, [low, pack, other], None, pack.shape[1])


def newton_closing(opening, picked):
    return newton_call(False, True, NS_STEPS - 3, 18, list(opening), picked, picked.shape[1])[0]


def gram_kernel(cols, low_ref, extras_ref, *refs):
    sent_ref, kept_ref = refs[-1], refs[-2]
    refs = refs[:-2]
    width = refs[0].shape[0]
    terms = []
    for (left, right), ref in zip(cols, refs):
        piece = ref[:, left : -(-right // LANES) * LANES]
        lane = lax.broadcasted_iota(jnp.int32, piece.shape, 1)
        terms.append(split(jnp.where(lane < right - left, piece, 0.0), 2))

    def strip(i):
        return sum(
            product([part[at(i)] for part in term], [part[i:] for part in term], ROWS_OF_BOTH)
            for term in terms
        )

    packs = (strip(0), jnp.concatenate([strip(TILE), strip(2 * TILE)], axis=1))
    low = low_ref[0]
    kept_ref[:TILE] = jnp.where(low == 0, packs[0], packs[1])
    sent_ref[:TILE] = jnp.where(low == 0, packs[1], packs[0])
    extras = extras_ref[...]
    if extras.shape[1] < width:
        rows = extras[-2 * (width // LANES) - 1 : -1].reshape(2, -1, LANES)
        rows = [jnp.concatenate([rows[k, j : j + 1] for j in range(width // LANES)], 1) for k in (0, 1)]
        extras = jnp.concatenate(rows + [jnp.zeros((SUBLANES - 2, width), F32)], axis=0)
    kept_ref[TILE:] = extras
    sent_ref[TILE:] = extras


def gram_packs(pieces, extras):
    width = pieces[0][0].shape[0]
    return stage(
        functools.partial(gram_kernel, [piece[1:] for piece in pieces]),
        [shaped((TILE + SUBLANES, width))] * 2,
        [scalars(lax.axis_index("head") % 2), extras] + [piece[0] for piece in pieces],
        smem=1,
        micros=5,
    )


def per_device(
    inputs,
    lengths,
    norm_gain,
    in_proj,
    conv_weight,
    conv_bias,
    head_params,
    gate_gain,
    out_proj,
    cotangent,
    norm_gain_mom,
    in_proj_mom,
    conv_weight_mom,
    conv_bias_mom,
    head_params_mom,
    gate_gain_mom,
    out_proj_mom,
):
    members, extent, model_width = inputs.shape
    seq_count = lax.axis_size("seq")
    head_count = lax.axis_size("head")
    seq_place = lax.axis_index("seq")
    head_place = lax.axis_index("head")
    heads_here = head_params.shape[1]
    head_span = gate_gain.shape[0]
    head_size = head_span // heads_here
    channels = conv_bias.shape[0]
    state_size = (channels - head_span) * head_count // 2
    inner_all = head_span * head_count
    group_cols = in_proj.shape[1]
    proj_all = group_cols * head_count
    tap_count = conv_weight.shape[0]
    share = model_width // seq_count
    tokens = members * extent
    quarter = extent // head_count
    runs = seq_count // members

    def own_blocks(blocks):
        return lax.dynamic_slice_in_dim(blocks, head_place * quarter, quarter, 1)

    def own(per_token):
        return pick(per_token.reshape((members, head_count, quarter, -1)), head_place, 1)

    run_place = seq_place // members
    length = lengths[seq_place % members]
    first_slot = run_place * tokens
    place = scalars(length, first_slot, head_place)
    in_low = in_proj.astype(BF)
    out_low = out_proj.astype(BF)
    x_end = 2 * head_span
    bc_end = head_span + channels
    bc_count = channels - head_span
    halo = tap_count - 1
    side_cols = -(-(group_cols - x_end) // LANES) * LANES
    small_rows = SUBLANES * (head_span // LANES + 3) + head_span // LANES + 2 * (model_width // LANES) + 1
    data_piece = own_blocks(inputs)
    data_piece = spread(data_piece, members)
    cot_sent = own_blocks(cotangent)
    decay_rate = -jnp.exp(head_params[1])[:, None]

    def from_run(edge, step):
        pairs = [(i, i + step) for i in range(seq_count) if 0 <= i + step < seq_count]
        return lax.ppermute(edge, "seq", pairs)

    side_weight = jnp.pad(in_low[:, x_end:], ((0, 0), (0, side_cols - (group_cols - x_end)))).T
    weight_cols = jnp.concatenate([conv_weight[:, head_span:], conv_bias[None, head_span:]], axis=0).T
    weight_cols = jnp.pad(weight_cols, ((0, 0), (0, LANES - tap_count - 1)))
    params = jnp.stack([head_params[0], decay_rate[:, 0]], axis=1)
    params = jnp.pad(params, ((0, SUBLANES - heads_here), (0, LANES - 2)))
    z_weight, x_proj = in_low[:, :head_span], in_low[:, head_span:x_end]
    x_weight = conv_weight[:, :head_span]
    skip = jnp.repeat(head_params[2], head_size)[None]
    data_piece, cot_sent, side_weight, weight_cols, params, z_weight, x_proj, out_low = apart_from_here(
        data_piece, cot_sent, side_weight, weight_cols, params, z_weight, x_proj, out_low
    )
    cot_piece = spread(cot_sent, members)
    across = flip(data_piece, "head", 2)
    corner = flip(across, "head", 1)
    beside = flip(data_piece, "head", 1)
    cot_piece, across, corner, beside = apart_from_here(cot_piece, across, corner, beside)
    pieces = [data_piece, beside, across, corner]
    cot_across = flip(cot_piece, "head", 2)
    x_halo = jnp.zeros((SUBLANES, head_span), F32)
    bc_halo = jnp.zeros((bc_count, LANES), F32)
    if runs > 1:
        ends = gather_head(data_piece, 1).reshape(tokens, model_width)[tokens - SUBLANES :].astype(F32)
        ends = ends * lax.rsqrt(jnp.mean(ends * ends, axis=-1, keepdims=True) + EPSILON) * norm_gain
        ends = jnp.dot(ends.astype(BF), in_low[:, head_span:bc_end], preferred_element_type=F32)
        ends = from_run(ends.astype(BF), members).astype(F32)
        x_halo = ends[:, :head_span]
        bc_halo = jnp.pad(ends[:, head_span:].T, ((0, 0), (LANES - SUBLANES, 0)))
    data_low, lowered, root_scale, bc_own, bc_conv, bc_in, rows = enter(
        head_place, pieces, norm_gain[None], side_weight, weight_cols, bc_halo, params, tap_count, heads_here,
        bc_count,
    )
    bc_own, lowered = apart_from_here(bc_own, lowered)
    bc_across = flip(bc_own, "head", 2)
    bc_beside = flip(bc_own, "head", 1)
    z_part, x_in, x_conv = z_and_x(
        lowered, z_weight, x_proj, x_weight, conv_bias[None, :head_span], x_halo, members
    )
    bc_across, bc_beside, cot_across, z_part = apart_from_here(
        bc_across, bc_beside, cot_across, z_part
    )
    bc_corner = flip(bc_across, "head", 1)
    cot_pieces = [cot_piece, flip(cot_piece, "head", 1), cot_across, flip(cot_across, "head", 1)]
    bc_pieces = [bc_own, bc_beside, bc_across, bc_corner]
    step_sizes = rows[:heads_here]
    growth = jnp.repeat(jnp.exp(jnp.sum(step_sizes * decay_rate, axis=1)), head_size)[None]
    gain = gate_gain[None]

    def scan_from(start):
        return forward_scan(
            place, x_conv, z_part, bc_pieces, rows, skip, gain, out_low, cot_pieces, start, head_size, members
        )

    start = jnp.zeros((state_size, head_span), F32)
    if runs > 1:
        start = entering(growth, scan_from(start)[2], members, False)
    mixed, states, state_end, gated_low, partial_kept, partial_sent, sums, bc_full, cot = scan_from(start)
    sums, partial_sent = apart_from_here(sums, partial_sent)
    sums = added(sums, flip(sums, "head", 1))
    norm_rows = stage(
        functools.partial(norm_kernel, inner_all), shaped(sums.shape), [sums, flip(sums, "head", 2)]
    )
    norm_scale = norm_rows[0]
    partial_come = flip(partial_sent, "head", 1)
    grad_mixed, grad_z, grad_summed, gate_gain_grad = gate_back(
        place, cot, norm_rows, z_part, mixed, gain, out_low.T, inner_all, members
    )
    low, high = head_place % 2, head_place // 2


    def come_rows(blocks):
        return lax.all_to_all(blocks.reshape((seq_count, share, -1)), "seq", 0, 0, tiled=True)

    turned_lowered = lowered.T
    early_sent = jnp.concatenate(
        [
            jnp.dot(grad_summed.T, gated_low, preferred_element_type=F32),
            jnp.dot(turned_lowered, grad_z, preferred_element_type=F32),
        ],
        axis=1,
    ).astype(BF)
    slots = first_slot + lax.broadcasted_iota(jnp.int32, (tokens, 1), 0)
    valid_mask = own((slots < length).astype(F32))
    norm_piece = own(norm_scale)
    root_piece = own(root_scale)
    early_old = jnp.concatenate([out_proj_mom.T, in_proj_mom[:, :head_span]], axis=1)
    in_low_wide = jnp.pad(in_low, ((0, 0), (0, x_end + side_cols - group_cols))).T
    late_old = jnp.pad(in_proj_mom[:, head_span:], ((0, 0), (0, x_end + side_cols - group_cols)))
    early_sent, partial_kept, partial_come = apart_from_here(early_sent, partial_kept, partial_come)
    early_come = come_rows(early_sent)
    summed_kept, summed_sent = split_halves(partial_kept, partial_come, 0, high)
    (
        grad_mixed, summed_kept, summed_sent, valid_mask, norm_piece, root_piece, early_old,
        weight_cols, in_low_wide, late_old, turned_lowered, root_scale,
    ) = apart_from_here(
        grad_mixed, summed_kept, summed_sent, valid_mask, norm_piece, root_piece, early_old,
        weight_cols, in_low_wide, late_old, turned_lowered, root_scale,
    )
    summed_come = flip(summed_sent, "head", 2)

    def scan_back(back, edge):
        return backward_scan(
            low, grad_mixed, x_conv, x_in, bc_full, rows, states, state_end, skip, x_weight,
            decay_rate, back, edge, head_size, members,
        )

    back = jnp.zeros_like(state_end)
    edge = jnp.zeros((SUBLANES, head_span), F32)
    if runs > 1:
        back = entering(growth, scan_back(back, edge)[3], members, True)
        edge = from_run(scan_back(back, edge)[4], -members)
    grad_x_in, bc_kept, bc_sent, _, _, small, grad_pre, head_sums_out = scan_back(back, edge)

    bc_come = flip(bc_sent, "head", 1)
    bc_kept, early_come = apart_from_here(bc_kept, early_come)
    early_rows, early_mom = rows_step([early_come], early_old)
    early_mom, bc_kept, summed_kept = apart_from_here(early_mom, bc_kept, summed_kept)
    full_early = whole_rows(early_mom)
    result, result_squares = stage(
        result_kernel,
        [shaped(data_piece.shape, BF), shaped((1, model_width))],
        [summed_kept, summed_come, data_piece, norm_piece, valid_mask],
        micros=20,
    )
    bc_kept, result = apart_from_here(bc_kept, result)
    bc_shape = (2, bc_kept.shape[0] // 2, tokens)
    bc_kept, bc_sent = split_halves(bc_kept.reshape(bc_shape), bc_come.reshape(bc_shape), 0, high)
    bc_kept, bc_sent, grad_x_in = apart_from_here(bc_kept, bc_sent, grad_x_in)
    bc_come = flip(bc_sent, "head", 2)
    x_sent, bc_kept = apart_from_here(weight_grad(turned_lowered, grad_x_in), bc_kept)

    halo_cols = jnp.zeros((bc_in.shape[0], LANES), F32)
    if runs > 1:
        first = (bc_kept[:, :halo] + bc_come[:, :halo].astype(F32)) * silu_slope(bc_conv[:, :halo])
        first = from_run(first.astype(BF), -members).astype(F32)
        halo_cols = jnp.pad(first, ((0, 0), (0, LANES - halo)))
    grad_side, bc_small, side_sent = stage(
        functools.partial(side_kernel, tap_count),
        [
            shaped((tokens, side_cols), BF),
            shaped((bc_in.shape[0], LANES)),
            shaped((model_width, side_cols), BF),
        ],
        [bc_kept, bc_come, bc_conv, bc_in, weight_cols, halo_cols, grad_pre, turned_lowered],
    )
    late_sent, grad_side = apart_from_here(
        jnp.concatenate([x_sent, side_sent], axis=1), grad_side
    )
    late_come = come_rows(late_sent)
    full_early, grad_side = apart_from_here(full_early, grad_side)
    no_extras = jnp.zeros((SUBLANES, model_width), F32)
    pack, pack_sent = gram_packs([(full_early, 0, head_span)], no_extras)
    pack, grad_side = apart_from_here(added(pack, flip(pack_sent, "head", 1)), grad_side)
    pack_come = flip(pack, "head", 2)

    lowered_kept, lowered_sent, norm_gain_grad = lowered_grad(
        low, grad_z, grad_x_in, grad_side, in_low_wide, data_low, root_scale, members
    )
    lowered_kept, lowered_sent, late_come = apart_from_here(lowered_kept, lowered_sent, late_come)
    lowered_come = flip(lowered_sent, "head", 1)
    late_rows, late_mom = rows_step([late_come], late_old)
    late_mom, lowered_kept = apart_from_here(late_mom, lowered_kept)
    full_late = whole_rows(late_mom)
    lowered_kept, lowered_sent = split_halves(lowered_kept, lowered_come, 1, high)
    small_sums = stage(
        small_kernel,
        shaped((small_rows, LANES)),
        [small, bc_small, head_sums_out, gate_gain_grad, norm_gain_grad, result_squares],
    )
    lowered_kept, lowered_sent, small_sums, pack, pack_come = apart_from_here(
        lowered_kept, lowered_sent, small_sums, pack, pack_come
    )
    lowered_come = flip(lowered_sent, "head", 2)
    row_count = -(-share // (2 * SUBLANES)) * 2 * SUBLANES
    picked = seq_place * share + lax.broadcasted_iota(jnp.int32, (row_count, model_width), 0)
    picked = (picked == lax.broadcasted_iota(jnp.int32, picked.shape, 1)).astype(BF)
    pack_out = added(pack, pack_come)
    other_out = flip(pack_out, "head", 1)
    bit = 1
    while bit < seq_count:
        small_sums = added(small_sums, flip(small_sums, "seq", bit))
        bit *= 2
    lowered_kept, small_sums, pack_out, other_out = apart_from_here(
        lowered_kept, small_sums, pack_out, other_out
    )
    pieces = stage(
        input_kernel,
        shaped((members, 2 * quarter, model_width), BF),
        [
            lowered_kept, lowered_come, data_piece, cot_piece, root_piece, valid_mask, norm_gain[None, None],
            result,
        ],
    )
    pieces, full_late = apart_from_here(pieces, full_late)
    pieces = spread(pieces, members)
    late_used = group_cols - head_span
    pack, pack_sent = gram_packs(
        [(full_early, head_span, 2 * head_span), (full_late, 0, late_used)], small_sums
    )
    pack, pack_out, other_out = apart_from_here(
        added(pack, flip(pack_sent, "head", 1)), pack_out, other_out
    )
    pack_come = flip(pack, "head", 2)
    turn_out = newton_rows(pack_out, other_out, picked)
    pack, turn_out, pieces = apart_from_here(pack, turn_out, pieces)
    pack, pieces = apart_from_here(added(pack, pack_come), pieces)
    beside, across = flip(pieces, "head", 1), flip(pieces, "head", 2)
    turn_in = newton_rows(pack, flip(pack, "head", 1), picked)
    turn_in, across, beside = apart_from_here(turn_in, across, beside)
    corner = flip(across, "head", 1)
    turn_in, turn_out = turn_in[:share], turn_out[:share]

    taps_rows = SUBLANES * (head_span // LANES)
    x_small = small_sums[:taps_rows].reshape(-1, SUBLANES, LANES)
    x_small = jnp.moveaxis(x_small, 0, 1).reshape(SUBLANES, head_span)
    bc_small = small_sums[taps_rows : taps_rows + SUBLANES, : channels - head_span]
    both_small = jnp.concatenate([x_small, bc_small], axis=1)
    conv_weight_grad, conv_bias_grad = both_small[:tap_count], both_small[tap_count]
    head_rows = jnp.sum(
        small_sums[taps_rows + SUBLANES : taps_rows + 3 * SUBLANES].reshape(2, SUBLANES, LANES), axis=2
    )[:, :heads_here]
    head_params_grad = jnp.stack(
        [
            head_rows[0],
            head_rows[1] * decay_rate[:, 0],
            jnp.sum(x_small[tap_count + 1].reshape(heads_here, head_size), axis=1),
        ]
    )
    gate_row = taps_rows + 3 * SUBLANES
    gate_gain_grad = small_sums[gate_row : gate_row + head_span // LANES].reshape(-1)
    norm_gain_grad, squares_all = pack[TILE], jnp.sum(pack[TILE + 1])

    out_grad_rows = early_rows[:, :head_span]
    out_rows_mom = early_mom[:, :head_span]
    in_proj_grad = jnp.concatenate(
        [early_rows[:, head_span:], late_rows[:, :late_used]], axis=1
    )
    in_proj_mom_new = jnp.concatenate([early_mom[:, head_span:], late_mom[:, :late_used]], axis=1)

    def turned(turn, matrix):
        return jnp.dot(turn, matrix, precision=lax.Precision.HIGH, preferred_element_type=F32)

    rows_early, rows_late = full_early, full_late
    rows_out = turned(turn_out, rows_early[:, :head_span])
    rows_in = jnp.concatenate(
        [turned(turn_in, rows_early[:, head_span:]), turned(turn_in, rows_late)], axis=1
    )[:, :group_cols]
    output, input_grad = in_order(head_place, [pieces, beside, across, corner])
    rms = jnp.sqrt(squares_all / (jnp.sum(lengths).astype(F32) * model_width))
    in_old_rows = lax.dynamic_slice_in_dim(in_proj, seq_place * share, share, 0)
    in_proj_new = in_old_rows - MUON_RATE * 0.2 * math.sqrt(max(model_width, proj_all)) * rows_in
    out_old_cols = lax.dynamic_slice_in_dim(out_proj, seq_place * share, share, 1)
    out_proj_new = (
        out_old_cols - MUON_RATE * 0.2 * math.sqrt(max(inner_all, model_width)) * rows_out.T
    )
    divisor = math.sqrt(members * extent * seq_count)
    norm_gain_mom_new = 0.5 * norm_gain_mom + norm_gain_grad
    conv_weight_mom_new = 0.5 * conv_weight_mom + conv_weight_grad
    conv_bias_mom_new = 0.5 * conv_bias_mom + conv_bias_grad
    head_params_mom_new = 0.5 * head_params_mom + head_params_grad
    gate_gain_mom_new = 0.5 * gate_gain_mom + gate_gain_grad
    norm_gain_new = norm_gain - SMALL_RATE * norm_gain_mom_new / divisor
    conv_weight_new = conv_weight - SMALL_RATE * conv_weight_mom_new / divisor
    conv_bias_new = conv_bias - SMALL_RATE * conv_bias_mom_new / divisor
    head_params_new = head_params - SMALL_RATE * head_params_mom_new / divisor
    gate_gain_new = gate_gain - SMALL_RATE * gate_gain_mom_new / divisor
    return (
        output,
        input_grad,
        norm_gain_grad,
        in_proj_grad,
        conv_weight_grad,
        conv_bias_grad,
        head_params_grad,
        gate_gain_grad,
        out_grad_rows.T,
        norm_gain_mom_new,
        in_proj_mom_new,
        conv_weight_mom_new,
        conv_bias_mom_new,
        head_params_mom_new,
        gate_gain_mom_new,
        out_rows_mom.T,
        norm_gain_new,
        in_proj_new,
        conv_weight_new,
        conv_bias_new,
        head_params_new,
        gate_gain_new,
        out_proj_new,
        rms,
    )


def solution(mesh):
    return jax.shard_map(
        per_device,
        mesh=mesh,
        in_specs=(
            P(None, "seq", None),
            P(),
            P(),
            P(None, "head"),
            P(None, "head"),
            P("head"),
            P(None, "head"),
            P("head"),
            P("head", None),
            P(None, "seq", None),
            P(),
            P("seq", "head"),
            P(None, "head"),
            P("head"),
            P(None, "head"),
            P("head"),
            P("head", "seq"),
        ),
        out_specs=(
            P(None, "seq", None),
            P(None, "seq", None),
            P(),
            P("seq", "head"),
            P(None, "head"),
            P("head"),
            P(None, "head"),
            P("head"),
            P("head", "seq"),
            P(),
            P("seq", "head"),
            P(None, "head"),
            P("head"),
            P(None, "head"),
            P("head"),
            P("head", "seq"),
            P(),
            P("seq", "head"),
            P(None, "head"),
            P("head"),
            P(None, "head"),
            P("head"),
            P("head", "seq"),
            P(),
        ),
        check_vma=False,
    )
```

```python
import functools
import math

import jax
import jax.numpy as jnp
from jax import lax
from jax.experimental import pallas as pl
from jax.experimental.pallas import tpu as pltpu
from jax.sharding import PartitionSpec as P

NS_STEPS = 5
EPSILON = 1e-05
COEF_A = 3.4445
COEF_B = -4.775
COEF_C = 2.0315
MUON_RATE = 0.2
SMALL_RATE = 0.2
PRECISE = lax.Precision.HIGHEST
BF = jnp.bfloat16
F32 = jnp.float32


def silu(values):
    return values * jax.nn.sigmoid(values)


def silu_slope(values):
    sigmoid_value = jax.nn.sigmoid(values)
    return sigmoid_value * (1.0 + values * (1.0 - sigmoid_value))


def flip(value, axis, bit):
    count = lax.axis_size(axis)
    return lax.ppermute(value, axis, [(i, i ^ bit) for i in range(count)])


def sum_over(value, axis):
    bit = 1
    while bit < lax.axis_size(axis):
        value = jax.tree.map(lambda part: part + flip(part, axis, bit), value)
        bit *= 2
    return value


def pick(stacked, index, axis):
    return lax.dynamic_index_in_dim(stacked, index, axis, keepdims=False)


def head_order(piece, beside, across, corner, axis):
    place = lax.axis_index("head")
    low, high = place % 2, place // 2
    near = jnp.where(low == 0, jnp.stack([piece, beside], axis), jnp.stack([beside, piece], axis))
    far = jnp.where(low == 0, jnp.stack([across, corner], axis), jnp.stack([corner, across], axis))
    return jnp.where(
        high == 0, jnp.concatenate([near, far], axis), jnp.concatenate([far, near], axis)
    )


def gather_head(piece, axis):
    across = flip(piece, "head", 2)
    return head_order(piece, flip(piece, "head", 1), across, flip(across, "head", 1), axis)


def head_halves(parts, axis):
    low = lax.axis_index("head") % 2
    shape = parts.shape
    parts = parts.reshape(shape[:axis] + (2, 2) + shape[axis + 1 :])
    return pick(parts, low, axis + 1) + flip(pick(parts, 1 - low, axis + 1), "head", 1)


def head_quarters(half, axis, wire):
    high = lax.axis_index("head") // 2
    return pick(half, high, axis), pick(half, 1 - high, axis).astype(wire)


def head_sum(kept, sent):
    return kept + flip(sent, "head", 2).astype(F32)


def whole_rows(rows):
    return lax.all_gather(rows, "seq", axis=0, tiled=True)


def apart_from_here(*values):
    return lax.optimization_barrier(values)


def spread(blocks, members):
    count = lax.axis_size("seq")
    runs = [list(range(i, i + members)) for i in range(0, count, members)]
    return lax.all_to_all(
        blocks, "seq", 0, 0, tiled=True, axis_index_groups=runs if len(runs) > 1 else None
    )


def entering(growth, state, members, backward):
    count = lax.axis_size("seq")
    runs = count // members
    mine = lax.axis_index("seq") // members
    step = -members if backward else members
    pairs = [(i, i + step) for i in range(count) if 0 <= i + step < count]
    total = jnp.zeros_like(state)
    for _ in range(runs - 1):
        total = lax.ppermute(growth * total + state, "seq", pairs)
    return total


CHUNK = 128
LANES = 128
SUBLANES = 8
VMEM_BYTES = 56 * 1024 * 1024


def split(values, terms):
    pieces = []
    for _ in range(terms):
        pieces.append(values.astype(BF))
        values = values - pieces[-1].astype(F32)
    return pieces


def product(left, right, dims=((1,), (0,))):
    total = None
    for i, a in enumerate(left):
        for j, b in enumerate(right):
            if i + j < max(len(left), len(right)):
                part = lax.dot_general(a, b, (dims, ((), ())), preferred_element_type=F32)
                total = part if total is None else total + part
    return total


ROWS_OF_BOTH = ((1,), (1,))


def columns(rows):
    count, extent = rows.shape
    return jnp.concatenate([rows, jnp.zeros((LANES - count, extent), F32)], axis=0).T


def lane_pair(left, right, half):
    lane = lax.broadcasted_iota(jnp.int32, (CHUNK, LANES), 1)
    return jnp.where(lane < half, left, right)


def apart(pair, half):
    lane = lax.broadcasted_iota(jnp.int32, pair.shape, 1)
    zero = jnp.zeros_like(pair)
    return jnp.concatenate([jnp.where(lane < half, pair, zero), jnp.where(lane < half, zero, pair)], 0)


def head_sums(values, half):
    lane = lax.broadcasted_iota(jnp.int32, values.shape, 1)
    first = jnp.sum(jnp.where(lane < half, values, 0.0), axis=1, keepdims=True)
    return first, jnp.sum(values, axis=1, keepdims=True) - first


def lasting(microseconds):
    return pl.CostEstimate(flops=int(microseconds * 3e8), bytes_accessed=0, transcendentals=0)


def forward_kernel(
    half, terms, place_ref, conv_ref, z_ref, bc0_ref, bc1_ref, bc2_ref, bc3_ref, rows_ref, skip_ref, gain_ref,
    out_low_ref, cot0_ref, cot1_ref, cot2_ref, cot3_ref, start_ref,
    mixed_ref, states_ref, end_ref, gated_ref, kept_ref, sent_ref, sums_ref, bc_ref, cot_ref, state_ref,
):
    step = pl.program_id(0)
    block = conv_ref.shape[0]
    span = conv_ref.shape[1]
    pairs = span // LANES

    @pl.when(step == 0)
    def _():
        state_ref[...] = start_ref[...]

    share = bc0_ref.shape[0]
    quarter = cot0_ref.shape[1]
    for distance, (bc, cot) in enumerate(
        zip((bc0_ref, bc1_ref, bc2_ref, bc3_ref), (cot0_ref, cot1_ref, cot2_ref, cot3_ref))
    ):
        place = place_ref[2] ^ distance
        bc_ref[pl.ds(pl.multiple_of(place * share, share), share)] = bc[...]
        cot_ref[pl.ds(pl.multiple_of(place * quarter, quarter), quarter)] = cot[0]
    state = 2 * share

    causal = lax.broadcasted_iota(jnp.int32, (CHUNK, CHUNK), 0) >= lax.broadcasted_iota(
        jnp.int32, (CHUNK, CHUNK), 1
    )
    for sub in range(block // CHUNK):
        here = slice(sub * CHUNK, (sub + 1) * CHUNK)
        rows = rows_ref[:, here]
        cols = columns(rows)
        bt_block = bc_ref[:state, here]
        c_block = bc_ref[state:, here].T
        scores = product([c_block], [bt_block])
        states_ref[sub] = state_ref[...]
        state_parts = split(state_ref[...], terms)
        carried = product([c_block], state_parts)
        weighted, grown = [], []
        for pair in range(pairs):
            lanes = slice(pair * LANES, (pair + 1) * LANES)
            first, second = 2 * pair, 2 * pair + 1
            x = silu(conv_ref[here, lanes])

            def pair_cols(table, offset):
                return lane_pair(
                    table[:, offset + first : offset + first + 1],
                    table[:, offset + second : offset + second + 1],
                    half,
                )

            cum = pair_cols(cols, SUBLANES)
            scaled = x * pair_cols(cols, 0)
            last = cum[CHUNK - 1 : CHUNK]
            growth = jnp.exp(cum)
            weighted.append(scaled * jnp.exp(last - cum))
            grown.append(growth[CHUNK - 1 : CHUNK])
            mixing = []
            for head in (first, second):
                gap = cols[:, SUBLANES + head : SUBLANES + head + 1] - rows[SUBLANES + head : SUBLANES + head + 1]
                mixing.append(jnp.exp(jnp.where(causal, gap, -1e30)) * scores)
            inner = product(
                split(jnp.concatenate(mixing, axis=1), terms), split(apart(scaled, half), terms)
            )
            mixed_ref[here, lanes] = inner + carried[:, lanes] * growth + skip_ref[:, lanes] * x
        fresh = product([bt_block], split(jnp.concatenate(weighted, axis=1), terms))
        state_ref[...] = jnp.concatenate(grown, axis=1) * state_ref[...] + fresh
    end_ref[...] = state_ref[...]
    gated = mixed_ref[...] * silu(z_ref[...])
    gated_low = (gated * gain_ref[...]).astype(BF)
    gated_ref[...] = gated_low
    partial = jnp.dot(gated_low, out_low_ref[...], preferred_element_type=F32)
    quarters = partial.reshape((2, 2) + kept_ref.shape[2:])
    low = place_ref[2] % 2
    kept_ref[:, 0] = jnp.where(low == 0, quarters[:, 0], quarters[:, 1])
    sent_ref[:, 0] = jnp.where(low == 0, quarters[:, 1], quarters[:, 0])
    squares = jnp.sum(gated * gated, axis=1, keepdims=True)
    slot = place_ref[1] + step * block + lax.broadcasted_iota(jnp.int32, (block, 1), 0)
    back = jnp.where(slot < place_ref[0], cot_ref[...].astype(F32), 0.0)
    scale = jnp.sum(back * partial, axis=1, keepdims=True)
    lane = lax.broadcasted_iota(jnp.int32, (block, LANES), 1)
    sums = jnp.where(lane == 0, squares, jnp.where(lane == 1, scale, 0.0))
    for sub in range(block // CHUNK):
        here = slice(sub * CHUNK, (sub + 1) * CHUNK)
        sums_ref[:, here] = sums[here].T[:SUBLANES]


def forward_scan(place, conv, z, bc, rows, skip, gain, out_low, cot, start, half, members):
    tokens, span = conv.shape
    share = bc[0].shape[0]
    quarter, width = cot[0].shape[1:]
    state = 2 * share
    block = tokens // members
    subs = block // CHUNK
    by_rows = lambda i, *_: (i, 0)
    by_lanes = lambda i, *_: (0, i)
    whole = lambda i, *_: (0, 0)
    halves = lambda i, *_: (0, i, 0, 0)
    return pl.pallas_call(
        functools.partial(forward_kernel, half, 2),
        grid_spec=pltpu.PrefetchScalarGridSpec(
            num_scalar_prefetch=1,
            grid=(members,),
            in_specs=[
                pl.BlockSpec((block, span), by_rows),
                pl.BlockSpec((block, span), by_rows),
            ]
            + [pl.BlockSpec((share, block), by_lanes)] * 4
            + [
                pl.BlockSpec((3 * SUBLANES, block), by_lanes),
                pl.BlockSpec((1, span), whole),
                pl.BlockSpec((1, span), whole),
                pl.BlockSpec((span, width), whole),
            ]
            + [pl.BlockSpec((1, quarter, width), lambda i, *_: (i, 0, 0))] * 4
            + [pl.BlockSpec((state, span), whole)],
            out_specs=[
                pl.BlockSpec((block, span), by_rows),
                pl.BlockSpec((subs, state, span), lambda i, *_: (i, 0, 0)),
                pl.BlockSpec((state, span), whole),
                pl.BlockSpec((block, span), by_rows),
                pl.BlockSpec((2, 1, quarter, width), halves),
                pl.BlockSpec((2, 1, quarter, width), halves),
                pl.BlockSpec((SUBLANES, block), by_lanes),
                pl.BlockSpec((2 * state, block), by_lanes),
                pl.BlockSpec((block, width), by_rows),
            ],
            scratch_shapes=[pltpu.VMEM((state, span), F32)],
        ),
        out_shape=[
            jax.ShapeDtypeStruct((tokens, span), F32),
            jax.ShapeDtypeStruct((tokens // CHUNK, state, span), F32),
            jax.ShapeDtypeStruct((state, span), F32),
            jax.ShapeDtypeStruct((tokens, span), BF),
            jax.ShapeDtypeStruct((2, members, quarter, width), F32),
            jax.ShapeDtypeStruct((2, members, quarter, width), F32),
            jax.ShapeDtypeStruct((SUBLANES, tokens), F32),
            jax.ShapeDtypeStruct((2 * state, tokens), BF),
            jax.ShapeDtypeStruct((tokens, width), BF),
        ],
        compiler_params=pltpu.CompilerParams(vmem_limit_bytes=VMEM_BYTES),
        cost_estimate=lasting(17),
    )(place, conv, z, *bc, rows, skip, gain, out_low, *cot, start)


def gate_kernel(
    inner_all, place_ref, cot_ref, norm_ref, z_ref, mixed_ref, gain_ref, out_turned_ref,
    grad_mixed_ref, grad_z_ref, grad_summed_ref, gain_grad_ref,
):
    step = pl.program_id(0)
    block = cot_ref.shape[0]
    norm = jnp.concatenate(
        [columns(norm_ref[:, sub * CHUNK : (sub + 1) * CHUNK]) for sub in range(block // CHUNK)], 0
    )
    norm_scale, grad_scale = norm[:, 0:1], norm[:, 1:2]
    slot = place_ref[1] + step * block + lax.broadcasted_iota(jnp.int32, (block, 1), 0)
    back = jnp.where(slot < place_ref[0], cot_ref[...].astype(F32), 0.0)
    grad_summed = (norm_scale * back).astype(BF)
    grad_summed_ref[...] = grad_summed
    grad_low = jnp.dot(grad_summed, out_turned_ref[...], preferred_element_type=F32)
    z, mixed = z_ref[...], mixed_ref[...]
    sigmoid = jax.nn.sigmoid(z)
    gate = z * sigmoid
    gated = mixed * gate
    shrink = grad_scale * norm_scale * norm_scale * norm_scale / inner_all
    grad_gated = grad_low * gain_ref[...] - shrink * gated
    grad_mixed_ref[...] = grad_gated * gate
    grad_z_ref[...] = (grad_gated * mixed * (sigmoid * (1.0 + z * (1.0 - sigmoid)))).astype(BF)

    @pl.when(step == 0)
    def _():
        gain_grad_ref[...] = jnp.zeros_like(gain_grad_ref)

    gain_grad_ref[...] += jnp.sum(grad_low * gated, axis=0, keepdims=True)


def gate_back(place, cot, norm_rows, z, mixed, gain, out_turned, inner_all, members):
    tokens, span = z.shape
    width = cot.shape[1]
    block = tokens // members
    by_rows = lambda i, *_: (i, 0)
    whole = lambda i, *_: (0, 0)
    return pl.pallas_call(
        functools.partial(gate_kernel, inner_all),
        grid_spec=pltpu.PrefetchScalarGridSpec(
            num_scalar_prefetch=1,
            grid=(members,),
            in_specs=[
                pl.BlockSpec((block, width), by_rows),
                pl.BlockSpec((SUBLANES, block), lambda i, *_: (0, i)),
                pl.BlockSpec((block, span), by_rows),
                pl.BlockSpec((block, span), by_rows),
                pl.BlockSpec((1, span), whole),
                pl.BlockSpec((width, span), whole),
            ],
            out_specs=[
                pl.BlockSpec((block, span), by_rows),
                pl.BlockSpec((block, span), by_rows),
                pl.BlockSpec((block, width), by_rows),
                pl.BlockSpec((1, span), whole),
            ],
        ),
        out_shape=[
            jax.ShapeDtypeStruct((tokens, span), F32),
            jax.ShapeDtypeStruct((tokens, span), BF),
            jax.ShapeDtypeStruct((tokens, width), BF),
            jax.ShapeDtypeStruct((1, span), F32),
        ],
        compiler_params=pltpu.CompilerParams(vmem_limit_bytes=VMEM_BYTES),
        cost_estimate=lasting(12),
    )(place, cot, norm_rows, z, mixed, gain, out_turned)


def backward_kernel(
    half, terms, taps, low_ref, grad_ref, conv_ref, conv_in_ref, bc_ref, rows_ref,
    states_ref, end_ref, skip_ref, weight_ref, rate_ref, back_ref, halo_ref,
    grad_x_ref, kept_ref, sent_ref, first_ref, edge_ref, small_ref, pre_ref, sums_ref,
    carry_ref, after_ref, shift_ref,
):
    step = pl.program_id(0)
    block = conv_ref.shape[0]
    span = conv_ref.shape[1]
    pairs = span // LANES
    state = bc_ref.shape[0] // 2
    subs = block // CHUNK

    @pl.when(step == 0)
    def _():
        carry_ref[...] = back_ref[...]
        after_ref[...] = end_ref[...]
        shift_ref[:SUBLANES] = halo_ref[...]
        small_ref[...] = jnp.zeros_like(small_ref)
        sums_ref[...] = jnp.zeros_like(sums_ref)

    low = low_ref[0]
    row = lax.broadcasted_iota(jnp.int32, (CHUNK, CHUNK), 0)
    lane = lax.broadcasted_iota(jnp.int32, (CHUNK, CHUNK), 1)
    causal = row <= lane
    for sub in reversed(range(subs)):
        here = slice(sub * CHUNK, (sub + 1) * CHUNK)
        rows = rows_ref[:, here]
        cols = columns(rows)
        bt_block, ct_block = bc_ref[:state, here], bc_ref[state:, here]
        b_block, c_block = bt_block.T, ct_block.T
        scores = product([b_block], [ct_block])
        entered = states_ref[sub]
        carry = carry_ref[...]
        entered_parts = split(entered, terms)
        carry_parts = split(carry, terms)
        carried = product([c_block], entered_parts)
        pulled = product([b_block], carry_parts)
        joint = jnp.sum(carry * after_ref[...], axis=0, keepdims=True)
        after_ref[...] = entered
        head_of = lax.broadcasted_iota(jnp.int32, (SUBLANES, span), 1) // half
        joint = jnp.sum(
            jnp.where(head_of == lax.broadcasted_iota(jnp.int32, (SUBLANES, span), 0), joint, 0.0),
            axis=1,
            keepdims=True,
        )
        weighted, grown_grad, grown = [], [], []
        grad_scores = jnp.zeros((CHUNK, CHUNK), F32)
        col_sums = jnp.zeros((CHUNK, LANES), F32)
        row_sums = []
        for pair in range(pairs):
            lanes = slice(pair * LANES, (pair + 1) * LANES)
            first, second = 2 * pair, 2 * pair + 1

            def pair_cols(offset):
                return lane_pair(
                    cols[:, offset + first : offset + first + 1],
                    cols[:, offset + second : offset + second + 1],
                    half,
                )

            conv = conv_ref[here, lanes]
            sigmoid = jax.nn.sigmoid(conv)
            x = conv * sigmoid
            grad = grad_ref[here, lanes]
            cum, size = pair_cols(SUBLANES), pair_cols(0)
            scaled = x * size
            last = cum[CHUNK - 1 : CHUNK]
            growth = jnp.exp(cum)
            tail = jnp.exp(last - cum)
            weighted.append(scaled * tail)
            grown_grad.append(grad * growth)
            grown.append(growth[CHUNK - 1 : CHUNK])
            grad_apart = split(apart(grad, half), terms)
            dots = product(split(scaled, terms), grad_apart, ROWS_OF_BOTH)
            kernels = []
            for k, head in enumerate((first, second)):
                gap = rows[SUBLANES + head : SUBLANES + head + 1] - cols[:, SUBLANES + head : SUBLANES + head + 1]
                decay = jnp.exp(jnp.where(causal, gap, -1e30))
                grad_score = decay * dots[:, k * CHUNK : (k + 1) * CHUNK]
                grad_scores = grad_scores + grad_score
                kernels.append(decay * scores)
                both = grad_score * scores
                row_sums.append(jnp.sum(both, axis=0, keepdims=True))
                col_sums = jnp.where(
                    lane == head, col_sums - jnp.sum(both, axis=1, keepdims=True), col_sums
                )
            pulled_pair = tail * pulled[:, lanes]
            force = product(split(jnp.concatenate(kernels, axis=1), terms), grad_apart) + pulled_pair
            grad_x = size * force + skip_ref[:, lanes] * grad
            flow = grown_grad[-1] * carried[:, lanes] - scaled * pulled_pair
            direct = x * force
            for head, flow_sum, direct_sum in zip(
                (first, second), head_sums(flow, half), head_sums(direct, half)
            ):
                col_sums = jnp.where(lane == head, col_sums + flow_sum, col_sums)
                col_sums = jnp.where(lane == SUBLANES + head, direct_sum, col_sums)
            small_ref[taps + 1 : taps + 2, lanes] += jnp.sum(grad * x, axis=0, keepdims=True)
            grad_conv = (grad_x * (sigmoid * (1.0 + conv * (1.0 - sigmoid)))).astype(BF).astype(F32)
            shift_ref[CHUNK : CHUNK + SUBLANES, lanes] = shift_ref[:SUBLANES, lanes]
            shift_ref[:CHUNK, lanes] = grad_conv
            conv_in = conv_in_ref[here, lanes].astype(F32)
            total = None
            for tap in range(taps):
                moved = shift_ref[taps - 1 - tap : taps - 1 - tap + CHUNK, lanes]
                term = weight_ref[tap : tap + 1, lanes] * moved
                total = term if total is None else total + term
                small_ref[tap : tap + 1, lanes] += jnp.sum(conv_in * moved, axis=0, keepdims=True)
            small_ref[taps : taps + 1, lanes] += jnp.sum(grad_conv, axis=0, keepdims=True)
            grad_x_ref[here, lanes] = total.astype(BF)
        grown_parts = split(jnp.concatenate(grown_grad, axis=1), terms)
        weighted_parts = split(jnp.concatenate(weighted, axis=1), terms)
        grad_b = product(carry_parts, weighted_parts, ROWS_OF_BOTH) + product(
            [ct_block], split(grad_scores.T, terms)
        )
        grad_c = product(entered_parts, grown_parts, ROWS_OF_BOTH) + product(
            [bt_block], split(grad_scores, terms)
        )
        middle = state // 2
        for k, part in enumerate((grad_b, grad_c)):
            place = slice(k * middle, (k + 1) * middle)
            kept_ref[place, here] = jnp.where(low == 0, part[:middle], part[middle:])
            sent_ref[place, here] = jnp.where(low == 0, part[middle:], part[:middle])
        carry_ref[...] = jnp.concatenate(grown, axis=1) * carry + product([ct_block], grown_parts)
        turned = col_sums.T
        row_sums.append(jnp.zeros((SUBLANES - 2 * pairs, CHUNK), F32))
        slots = lax.broadcasted_iota(jnp.int32, (SUBLANES, CHUNK), 1)
        grad_cum = (
            jnp.concatenate(row_sums, axis=0)
            + turned[:SUBLANES]
            + jnp.where(slots == CHUNK - 1, joint, 0.0)
        )
        grad_decay = product(split(grad_cum, 3), [(row >= lane).astype(BF)])
        grad_pre = (turned[SUBLANES : 2 * SUBLANES] + grad_decay * rate_ref[...]) * rows[2 * SUBLANES :]
        pre_ref[:, here] = grad_pre
        sums_ref[:SUBLANES] += grad_pre
        sums_ref[SUBLANES:] += grad_decay * rows[:SUBLANES]
    first_ref[...] = carry_ref[...]
    edge_ref[...] = shift_ref[:SUBLANES]


def backward_scan(
    low, grad, conv, conv_in, bc, rows, states, end, skip, weight, rate, back, halo, half,
    members,
):
    tokens, span = conv.shape
    state = bc.shape[0] // 2
    taps = weight.shape[0]
    block = tokens // members
    subs = block // CHUNK
    final = members - 1
    by_rows = lambda i, *_: (final - i, 0)
    by_lanes = lambda i, *_: (0, final - i)
    whole = lambda i, *_: (0, 0)
    return pl.pallas_call(
        functools.partial(backward_kernel, half, 2, taps),
        grid_spec=pltpu.PrefetchScalarGridSpec(
        num_scalar_prefetch=1,
        grid=(members,),
        in_specs=[
            pl.BlockSpec((block, span), by_rows),
            pl.BlockSpec((block, span), by_rows),
            pl.BlockSpec((block, span), by_rows),
            pl.BlockSpec((2 * state, block), by_lanes),
            pl.BlockSpec((3 * SUBLANES, block), by_lanes),
            pl.BlockSpec((subs, state, span), lambda i, *_: (final - i, 0, 0)),
            pl.BlockSpec((state, span), whole),
            pl.BlockSpec((1, span), whole),
            pl.BlockSpec((taps, span), whole),
            pl.BlockSpec((SUBLANES, 1), whole),
            pl.BlockSpec((state, span), whole),
            pl.BlockSpec((SUBLANES, span), whole),
        ],
        out_specs=[
            pl.BlockSpec((block, span), by_rows),
            pl.BlockSpec((state, block), by_lanes),
            pl.BlockSpec((state, block), by_lanes),
            pl.BlockSpec((state, span), whole),
            pl.BlockSpec((SUBLANES, span), whole),
            pl.BlockSpec((SUBLANES, span), whole),
            pl.BlockSpec((SUBLANES, block), by_lanes),
            pl.BlockSpec((2 * SUBLANES, LANES), whole),
        ],
        scratch_shapes=[
            pltpu.VMEM((state, span), F32),
            pltpu.VMEM((state, span), F32),
            pltpu.VMEM((CHUNK + SUBLANES, span), F32),
        ],
        ),
        out_shape=[
            jax.ShapeDtypeStruct((tokens, span), BF),
            jax.ShapeDtypeStruct((state, tokens), F32),
            jax.ShapeDtypeStruct((state, tokens), F32),
            jax.ShapeDtypeStruct((state, span), F32),
            jax.ShapeDtypeStruct((SUBLANES, span), F32),
            jax.ShapeDtypeStruct((SUBLANES, span), F32),
            jax.ShapeDtypeStruct((SUBLANES, tokens), F32),
            jax.ShapeDtypeStruct((2 * SUBLANES, LANES), F32),
        ],
        compiler_params=pltpu.CompilerParams(vmem_limit_bytes=VMEM_BYTES),
        cost_estimate=lasting(25),
    )(
        scalars(low), grad, conv, conv_in, bc, rows, states, end, skip, weight,
        jnp.pad(rate, ((0, SUBLANES - rate.shape[0]), (0, 0))), back, halo,
    )


def vmem(count):
    return [pl.BlockSpec(memory_space=pltpu.VMEM)] * count


def scalars(*values):
    return jnp.stack(values).astype(jnp.int32)


def stage(kernel, out_shape, operands, smem=0, micros=0.01):
    return pl.pallas_call(
        kernel,
        out_shape=out_shape,
        in_specs=[pl.BlockSpec(memory_space=pltpu.SMEM)] * smem + vmem(len(operands) - smem),
        out_specs=jax.tree.map(lambda _: pl.BlockSpec(memory_space=pltpu.VMEM), out_shape),
        compiler_params=pltpu.CompilerParams(vmem_limit_bytes=VMEM_BYTES),
        cost_estimate=lasting(micros),
    )(*operands)


def shaped(shape, dtype=F32):
    return jax.ShapeDtypeStruct(shape, dtype)


def add_kernel(a_ref, b_ref, out_ref):
    out_ref[...] = a_ref[...] + b_ref[...].astype(F32)


def added(a, b):
    return stage(add_kernel, shaped(a.shape), [a, b])


def split_kernel(axis, high_ref, kept_ref, come_ref, own_ref, sent_ref):
    high = high_ref[0]
    total = [
        kept_ref[(slice(None),) * axis + (k,)] + come_ref[(slice(None),) * axis + (k,)] for k in (0, 1)
    ]
    own_ref[...] = jnp.where(high == 0, total[0], total[1])
    sent_ref[...] = jnp.where(high == 0, total[1], total[0]).astype(BF)


def split_halves(kept, come, axis, high):
    shape = kept.shape[:axis] + kept.shape[axis + 1 :]
    return stage(
        functools.partial(split_kernel, axis),
        [shaped(shape), shaped(shape, BF)],
        [scalars(high), kept, come],
        smem=1,
    )


def rows_kernel(pieces, *refs):
    old_ref, sum_ref, mom_ref = refs[pieces], refs[-2], refs[-1]
    left = 0
    for ref in refs[:pieces]:
        cols = slice(left, left + ref.shape[2])
        left = cols.stop
        total = jnp.sum(ref[...].astype(F32), axis=0)
        sum_ref[:, cols] = total
        mom_ref[:, cols] = 0.5 * old_ref[:, cols] + total
    if mom_ref.shape[1] > left:
        mom_ref[:, left:] = refs[pieces + 1][...]


def rows_step(come, old, *others, micros=0.01):
    wide = old.shape[1] + sum(other.shape[1] for other in others)
    return stage(
        functools.partial(rows_kernel, len(come)),
        [shaped(old.shape), shaped((old.shape[0], wide))],
        [*come, old, *others],
        micros=micros,
    )


def weight_kernel(turned_ref, grad_ref, out_ref):
    out_ref[...] = jnp.dot(turned_ref[...], grad_ref[...], preferred_element_type=F32).astype(BF)


def weight_grad(turned, grad):
    return stage(weight_kernel, shaped((turned.shape[0], grad.shape[1]), BF), [turned, grad])


def side_kernel(taps, kept_ref, come_ref, conv_ref, conv_in_ref, weight_ref, halo_ref, pre_ref, turned_ref,
                x_ref, side_ref, small_ref, out_ref):
    tokens = kept_ref.shape[1]
    conv = conv_ref[...]
    sigmoid = jax.nn.sigmoid(conv)
    slope = sigmoid * (1.0 + conv * (1.0 - sigmoid))
    grad = ((kept_ref[...] + come_ref[...].astype(F32)) * slope).astype(BF).astype(F32)
    conv_in = conv_in_ref[...].astype(F32)
    wide = jnp.concatenate([grad, halo_ref[...]], axis=1)
    lane = lax.broadcasted_iota(jnp.int32, small_ref.shape, 1)
    small = jnp.where(lane == taps, jnp.sum(grad, axis=1, keepdims=True), 0.0)
    total = None
    for tap in range(taps):
        lead = taps - 1 - tap
        moved = pltpu.roll(wide, wide.shape[1] - lead, 1)[:, :tokens] if lead else grad
        term = weight_ref[:, tap : tap + 1] * moved
        total = term if total is None else total + term
        small = jnp.where(lane == tap, jnp.sum(moved * conv_in, axis=1, keepdims=True), small)
    small_ref[...] = small
    used = total.shape[0] + pre_ref.shape[0]
    spare = jnp.zeros((LANES - used, tokens), F32)
    side = jnp.concatenate([total, pre_ref[...], spare], axis=0).astype(BF).T
    side_ref[...] = side
    span = x_ref.shape[1]
    out_ref[:, :span] = x_ref[...]
    out_ref[:, span:] = jnp.dot(turned_ref[...], side, preferred_element_type=F32).astype(BF)


def lowered_kernel(
    low_ref, z_ref, x_ref, side_ref, weight_ref, data_ref, root_ref, kept_ref, sent_ref, gain_ref
):
    step = pl.program_id(0)
    span = z_ref.shape[1]
    total = jnp.dot(z_ref[...], weight_ref[:span], preferred_element_type=F32)
    total = total + jnp.dot(x_ref[...], weight_ref[span : 2 * span], preferred_element_type=F32)
    total = total + jnp.dot(side_ref[...], weight_ref[2 * span :], preferred_element_type=F32)
    normed = data_ref[...].astype(F32) * root_ref[...]

    @pl.when(step == 0)
    def _():
        gain_ref[...] = jnp.zeros_like(gain_ref)

    gain_ref[...] += jnp.sum(total * normed, axis=0, keepdims=True)
    parts = total.reshape((2, 2) + kept_ref.shape[2:])
    low = low_ref[0]
    kept_ref[0] = jnp.where(low == 0, parts[:, 0], parts[:, 1])
    sent_ref[0] = jnp.where(low == 0, parts[:, 1], parts[:, 0])


def lowered_grad(low, grad_z, grad_x, side, weight, data, root, members):
    tokens, width = data.shape
    block = tokens // members
    by_rows = lambda i, *_: (i, 0)
    whole = lambda i, *_: (0, 0)
    half = (1, 2, block // 4, width)
    return pl.pallas_call(
        lowered_kernel,
        grid_spec=pltpu.PrefetchScalarGridSpec(
            num_scalar_prefetch=1,
            grid=(members,),
            in_specs=[
                pl.BlockSpec((block, grad_z.shape[1]), by_rows),
                pl.BlockSpec((block, grad_x.shape[1]), by_rows),
                pl.BlockSpec((block, side.shape[1]), by_rows),
                pl.BlockSpec(weight.shape, whole),
                pl.BlockSpec((block, width), by_rows),
                pl.BlockSpec((block, 1), by_rows),
            ],
            out_specs=[
                pl.BlockSpec(half, lambda i, *_: (i, 0, 0, 0)),
                pl.BlockSpec(half, lambda i, *_: (i, 0, 0, 0)),
                pl.BlockSpec((1, width), whole),
            ],
        ),
        out_shape=[
            shaped((members,) + half[1:]),
            shaped((members,) + half[1:]),
            shaped((1, width)),
        ],
        compiler_params=pltpu.CompilerParams(vmem_limit_bytes=VMEM_BYTES),
        cost_estimate=lasting(0.01),
    )(scalars(low), grad_z, grad_x, side, weight, data, root)


def result_kernel(kept_ref, come_ref, data_ref, norm_ref, mask_ref, out_ref, squares_ref):
    result = kept_ref[...] + come_ref[...].astype(F32)
    result = mask_ref[...] * (data_ref[...].astype(F32) + norm_ref[...] * result)
    out_ref[...] = result.astype(BF)
    squares_ref[...] = jnp.sum(result * result, axis=(0, 1), keepdims=True)[0]


def input_kernel(kept_ref, come_ref, data_ref, cot_ref, root_ref, mask_ref, gain_ref, result_ref, out_ref):
    quarter = kept_ref.shape[1]
    grad = (kept_ref[...] + come_ref[...].astype(F32)) * gain_ref[...]
    normed = data_ref[...].astype(F32) * root_ref[...]
    shrink = jnp.mean(grad * normed, axis=-1, keepdims=True)
    back = mask_ref[...] * cot_ref[...].astype(F32)
    out_ref[:, :quarter] = result_ref[...]
    out_ref[:, quarter:] = (back + root_ref[...] * (grad - normed * shrink)).astype(BF)


def small_kernel(small_ref, bc_ref, sums_ref, gate_ref, gain_ref, squares_ref, out_ref):
    out_ref[...] = jnp.zeros_like(out_ref)
    row = 0
    for k in range(small_ref.shape[1] // LANES):
        out_ref[row : row + SUBLANES] = small_ref[:, k * LANES : (k + 1) * LANES]
        row += SUBLANES
    turned = bc_ref[...].T[:SUBLANES]
    out_ref[row : row + SUBLANES, : turned.shape[1]] = turned
    row += SUBLANES
    out_ref[row : row + 2 * SUBLANES] = sums_ref[...]
    row += 2 * SUBLANES
    for ref in (gate_ref, gain_ref, squares_ref):
        for k in range(ref.shape[1] // LANES):
            out_ref[row : row + 1] = ref[:, k * LANES : (k + 1) * LANES]
            row += 1


def order_kernel(place_ref, *refs):
    output_ref, grad_ref = refs[4:]
    quarter = refs[0].shape[1] // 2
    for distance, ref in enumerate(refs[:4]):
        start = pl.multiple_of((place_ref[0] ^ distance) * quarter, quarter)
        output_ref[0, pl.ds(start, quarter)] = ref[0, :quarter]
        grad_ref[0, pl.ds(start, quarter)] = ref[0, quarter:].astype(F32)


def in_order(place, pieces):
    members, both, width = pieces[0].shape
    rows = 2 * both
    block = lambda i, *_: (i, 0, 0)
    return pl.pallas_call(
        order_kernel,
        grid_spec=pltpu.PrefetchScalarGridSpec(
            num_scalar_prefetch=1,
            grid=(members,),
            in_specs=[pl.BlockSpec((1, both, width), block)] * 4,
            out_specs=[pl.BlockSpec((1, rows, width), block)] * 2,
        ),
        out_shape=[shaped((members, rows, width), BF), shaped((members, rows, width))],
        compiler_params=pltpu.CompilerParams(vmem_limit_bytes=VMEM_BYTES),
        cost_estimate=lasting(5),
    )(scalars(place), *pieces)


def norm_kernel(inner_all, mine_ref, come_ref, out_ref):
    total = mine_ref[...] + come_ref[...]
    row = lax.broadcasted_iota(jnp.int32, total.shape, 0)
    out_ref[...] = jnp.where(row == 0, lax.rsqrt(total / inner_all + EPSILON), total)


def enter_kernel(
    taps, heads, place_ref, own_ref, beside_ref, across_ref, corner_ref, gain_ref, side_weight_ref, weight_ref,
    halo_ref, params_ref, data_ref, lowered_ref, root_ref, bc_ref, conv_ref, conv_in_ref, rows_ref, carry_ref,
):
    quarter = own_ref.shape[1]
    block = data_ref.shape[0]
    channels = bc_ref.shape[0]
    for distance, ref in enumerate((own_ref, beside_ref, across_ref, corner_ref)):
        start = pl.multiple_of((place_ref[0] ^ distance) * quarter, quarter)
        data_ref[pl.ds(start, quarter)] = ref[0]
    data = data_ref[...].astype(F32)
    root = lax.rsqrt(jnp.mean(data * data, axis=1, keepdims=True) + EPSILON)
    root_ref[...] = root
    lowered = (data * root * gain_ref[...]).astype(BF)
    lowered_ref[...] = lowered
    side = lax.dot_general(
        side_weight_ref[...], lowered, (ROWS_OF_BOTH, ((), ())), preferred_element_type=F32
    )

    @pl.when(pl.program_id(0) == 0)
    def _():
        carry_ref[...] = halo_ref[...]

    conv_low = side[:channels].astype(BF)
    conv_in_ref[...] = conv_low
    conv_in = conv_low.astype(F32)
    wide = jnp.concatenate([carry_ref[...], conv_in], axis=1)
    carry_ref[...] = conv_in[:, block - LANES :]
    conv = weight_ref[:, taps : taps + 1] + weight_ref[:, taps - 1 : taps] * conv_in
    for tap in range(taps - 1):
        conv = conv + weight_ref[:, tap : tap + 1] * pltpu.roll(wide, taps - 1 - tap, 1)[:, LANES:]
    conv_ref[...] = conv
    bc_ref[...] = silu(conv).astype(BF)

    head = lax.broadcasted_iota(jnp.int32, (SUBLANES, block), 0)
    pre = side[channels : channels + SUBLANES] + params_ref[:, 0:1]
    size = jnp.where(head < heads, jax.nn.softplus(pre), 0.0)
    change = size * params_ref[:, 1:2]
    row = lax.broadcasted_iota(jnp.int32, (CHUNK, CHUNK), 0)
    upto = (row <= lax.broadcasted_iota(jnp.int32, (CHUNK, CHUNK), 1)).astype(BF)
    rows_ref[:SUBLANES] = size
    for sub in range(block // CHUNK):
        here = slice(sub * CHUNK, (sub + 1) * CHUNK)
        rows_ref[SUBLANES : 2 * SUBLANES, here] = product(split(change[:, here], 3), [upto])
    rows_ref[2 * SUBLANES :] = jnp.where(head < heads, jax.nn.sigmoid(pre), 0.0)


def enter(place, pieces, gain, side_weight, weight, halo, params, taps, heads, channels):
    members, quarter, width = pieces[0].shape
    block = 4 * quarter
    tokens = members * block
    by_rows = lambda i, *_: (i, 0)
    by_lanes = lambda i, *_: (0, i)
    whole = lambda i, *_: (0, 0)
    return pl.pallas_call(
        functools.partial(enter_kernel, taps, heads),
        grid_spec=pltpu.PrefetchScalarGridSpec(
            num_scalar_prefetch=1,
            grid=(members,),
            in_specs=[pl.BlockSpec((1, quarter, width), lambda i, *_: (i, 0, 0))] * 4
            + [
                pl.BlockSpec((1, width), whole),
                pl.BlockSpec(side_weight.shape, whole),
                pl.BlockSpec(weight.shape, whole),
                pl.BlockSpec(halo.shape, whole),
                pl.BlockSpec(params.shape, whole),
            ],
            out_specs=[
                pl.BlockSpec((block, width), by_rows),
                pl.BlockSpec((block, width), by_rows),
                pl.BlockSpec((block, 1), by_rows),
                pl.BlockSpec((channels, block), by_lanes),
                pl.BlockSpec((channels, block), by_lanes),
                pl.BlockSpec((channels, block), by_lanes),
                pl.BlockSpec((3 * SUBLANES, block), by_lanes),
            ],
            scratch_shapes=[pltpu.VMEM((channels, LANES), F32)],
        ),
        out_shape=[
            jax.ShapeDtypeStruct((tokens, width), BF),
            jax.ShapeDtypeStruct((tokens, width), BF),
            jax.ShapeDtypeStruct((tokens, 1), F32),
            jax.ShapeDtypeStruct((channels, tokens), BF),
            jax.ShapeDtypeStruct((channels, tokens), F32),
            jax.ShapeDtypeStruct((channels, tokens), BF),
            jax.ShapeDtypeStruct((3 * SUBLANES, tokens), F32),
        ],
        compiler_params=pltpu.CompilerParams(vmem_limit_bytes=VMEM_BYTES),
        cost_estimate=lasting(8),
    )(scalars(place), *pieces, gain, side_weight, weight, halo, params)


def columns_kernel(
    taps, lowered_ref, z_weight_ref, x_weight_ref, weight_ref, bias_ref, halo_ref, z_ref, x_in_ref, conv_ref,
    shift_ref,
):
    block = lowered_ref.shape[0]
    lowered = lowered_ref[...]
    z_ref[...] = jnp.dot(lowered, z_weight_ref[...], preferred_element_type=F32)
    conv_low = jnp.dot(lowered, x_weight_ref[...], preferred_element_type=F32).astype(BF)
    x_in_ref[...] = conv_low

    @pl.when(pl.program_id(0) == 0)
    def _():
        shift_ref[:SUBLANES] = halo_ref[...]

    shift_ref[SUBLANES:] = conv_low.astype(F32)
    conv = jnp.broadcast_to(bias_ref[...], conv_ref.shape)
    for tap in range(taps):
        first = SUBLANES - (taps - 1) + tap
        conv = conv + weight_ref[tap : tap + 1] * shift_ref[first : first + block]
    conv_ref[...] = conv
    shift_ref[:SUBLANES] = shift_ref[block:]


def z_and_x(lowered, z_weight, x_weight, weight, bias, halo, members):
    tokens, width = lowered.shape
    span = z_weight.shape[1]
    block = tokens // members
    by_rows = lambda i: (i, 0)
    whole = lambda i: (0, 0)
    return pl.pallas_call(
        functools.partial(columns_kernel, weight.shape[0]),
        grid=(members,),
        in_specs=[
            pl.BlockSpec((block, width), by_rows),
            pl.BlockSpec((width, span), whole),
            pl.BlockSpec((width, span), whole),
            pl.BlockSpec(weight.shape, whole),
            pl.BlockSpec((1, span), whole),
            pl.BlockSpec((SUBLANES, span), whole),
        ],
        out_specs=[pl.BlockSpec((block, span), by_rows)] * 3,
        out_shape=[
            jax.ShapeDtypeStruct((tokens, span), F32),
            jax.ShapeDtypeStruct((tokens, span), BF),
            jax.ShapeDtypeStruct((tokens, span), F32),
        ],
        scratch_shapes=[pltpu.VMEM((block + SUBLANES, span), F32)],
        compiler_params=pltpu.CompilerParams(vmem_limit_bytes=VMEM_BYTES),
        cost_estimate=lasting(8),
    )(lowered, z_weight, x_weight, weight, bias, halo)


TILE = 256


def tiles_of(width):
    starts = range(0, width, TILE)
    return [(i, j) for i in starts for j in starts if i <= j]


def at(start):
    return slice(start, start + TILE)


def put(pair, i, j, values):
    for row, col, tile in ((i, j, values), (j, i, values.T))[: 1 if i == j else 2]:
        high = tile.astype(BF)
        pair[0, at(row), at(col)] = high
        pair[1, at(row), at(col)] = (tile - high.astype(F32)).astype(BF)


def tile_of(left, right, i, j):
    high, low = left[0, at(i)], left[1, at(i)]
    total = jnp.dot(high, right[1, :, at(j)], preferred_element_type=F32)
    total = total + jnp.dot(low, right[0, :, at(j)], preferred_element_type=F32)
    return total + jnp.dot(high, right[0, :, at(j)], preferred_element_type=F32)


def eye(rows, cols):
    return lax.broadcasted_iota(jnp.int32, (rows, cols), 0) == lax.broadcasted_iota(
        jnp.int32, (rows, cols), 1
    )


def newton_kernel(opens, closes, steps, *refs):
    refs = list(refs)
    low_ref = refs.pop(0) if opens else None
    gram_in = refs.pop(0)
    other_in = refs.pop(0) if opens else None
    factor_in = None if opens else refs.pop(0)
    before = [refs.pop(0)] if closes and not opens else []
    picked_ref = refs.pop(0) if closes else None
    gram_out = refs.pop(0) if not closes else None
    rows_ref = refs.pop(0) if closes else None
    factor_out = refs.pop(0) if opens and not closes else None
    polys = refs.pop(0) if steps else None
    gram, first, second, third = refs
    width = gram.shape[0]
    tiles = tiles_of(width)
    if opens:
        low = low_ref[0]
        upper = jnp.where(low == 0, gram_in[:TILE], other_in[:TILE])
        lower = jnp.where(low == 0, other_in[:TILE], gram_in[:TILE])
        gram[at(0)] = upper
        gram[at(TILE), TILE:] = lower[:, : width - TILE]
        gram[at(2 * TILE), 2 * TILE :] = lower[:, width - TILE :]
        size = jnp.zeros((1, 1), F32)
        for i in range(0, width, TILE):
            size = size + jnp.sum(jnp.where(eye(TILE, TILE), gram[at(i), at(i)], 0.0), keepdims=True)
        factor = 1.0 / (jnp.sqrt(size) + 1e-07)
        if factor_out is not None:
            factor_out[...] = jnp.broadcast_to(factor, factor_out.shape)
    else:
        factor = factor_in[0:1, 0:1]
    for i, j in tiles:
        values = gram[at(i), at(j)] * (factor * factor) if opens else gram_in[at(i), at(j)]
        gram[at(i), at(j)] = values
        put(first, i, j, values)
    for step in range(steps):
        for i, j in tiles:
            square = tile_of(first, first, i, j)
            put(second, i, j, square)
            held = gram[at(i), at(j)]
            poly = COEF_B * held + COEF_C * square
            put(polys.at[step], i, j, jnp.where(eye(TILE, TILE), COEF_A, 0.0) + poly if i == j else poly)
            gram[at(i), at(j)] = COEF_A * held + COEF_B * square
        for i, j in tiles:
            put(third, i, j, gram[at(i), at(j)] + COEF_C * tile_of(second, first, i, j))
        for i, j in tiles:
            values = tile_of(third, polys.at[step], i, j)
            gram[at(i), at(j)] = values
            put(first, i, j, values)
    if not closes:
        for i, j in tiles:
            gram_out[at(i), at(j)] = gram[at(i), at(j)]
        return
    picked = picked_ref[...]
    held = [jnp.dot(picked, first[k], preferred_element_type=F32) for k in range(2)]
    rows = COEF_A * picked.astype(F32) + COEF_B * (held[0] + held[1])
    rows = rows + COEF_C * product([part.astype(BF) for part in held], [first[0], first[1]])
    chain = [(ref, k) for ref in before for k in range(ref.shape[0])]
    chain += [(polys, k) for k in range(steps)]
    for ref, k in reversed(chain):
        rows = product(split(rows, 2), [ref[k, 0], ref[k, 1]])
    rows_ref[...] = rows * factor


def newton_call(opens, closes, steps, micros, operands, picked, width):
    pair = pltpu.VMEM((2, width, width), BF)
    whole = pl.BlockSpec(memory_space=pltpu.VMEM)
    out_shape = []
    if closes:
        operands = operands + [picked]
        out_shape.append(jax.ShapeDtypeStruct(picked.shape, F32))
    else:
        out_shape.append(jax.ShapeDtypeStruct((width, width), F32))
        if opens:
            out_shape.append(jax.ShapeDtypeStruct((SUBLANES, LANES), F32))
        out_shape.append(jax.ShapeDtypeStruct((steps, 2, width, width), BF))
    kept = [pltpu.VMEM((steps, 2, width, width), BF)] if closes and steps else []
    return pl.pallas_call(
        functools.partial(newton_kernel, opens, closes, steps),
        out_shape=out_shape,
        in_specs=([pl.BlockSpec(memory_space=pltpu.SMEM)] if opens else [])
        + [whole] * (len(operands) - opens),
        out_specs=[whole] * len(out_shape),
        scratch_shapes=kept + [pltpu.VMEM((width, width), F32), pair, pair, pair],
        compiler_params=pltpu.CompilerParams(vmem_limit_bytes=VMEM_BYTES),
        cost_estimate=lasting(micros),
    )(*operands)


def newton_rows(pack, other, picked):
    low = scalars(lax.axis_index("head") % 2)
    return newton_call(True, True, NS_STEPS - 1, 30, [low, pack, other], picked, pack.shape[1])[0]


def newton_opening(pack, other):
    low = scalars(lax.axis_index("head") % 2)
    return newton_call(True, False, 2, 15, [low, pack, other], None, pack.shape[1])


def newton_closing(opening, picked):
    return newton_call(False, True, NS_STEPS - 3, 18, list(opening), picked, picked.shape[1])[0]


def gram_kernel(cols, low_ref, extras_ref, *refs):
    sent_ref, kept_ref = refs[-1], refs[-2]
    refs = refs[:-2]
    width = refs[0].shape[0]
    terms = []
    for (left, right), ref in zip(cols, refs):
        piece = ref[:, left : -(-right // LANES) * LANES]
        lane = lax.broadcasted_iota(jnp.int32, piece.shape, 1)
        terms.append(split(jnp.where(lane < right - left, piece, 0.0), 2))

    def strip(i):
        return sum(
            product([part[at(i)] for part in term], [part[i:] for part in term], ROWS_OF_BOTH)
            for term in terms
        )

    packs = (strip(0), jnp.concatenate([strip(TILE), strip(2 * TILE)], axis=1))
    low = low_ref[0]
    kept_ref[:TILE] = jnp.where(low == 0, packs[0], packs[1])
    sent_ref[:TILE] = jnp.where(low == 0, packs[1], packs[0])
    extras = extras_ref[...]
    if extras.shape[1] < width:
        rows = extras[-2 * (width // LANES) - 1 : -1].reshape(2, -1, LANES)
        rows = [jnp.concatenate([rows[k, j : j + 1] for j in range(width // LANES)], 1) for k in (0, 1)]
        extras = jnp.concatenate(rows + [jnp.zeros((SUBLANES - 2, width), F32)], axis=0)
    kept_ref[TILE:] = extras
    sent_ref[TILE:] = extras


def gram_packs(pieces, extras):
    width = pieces[0][0].shape[0]
    return stage(
        functools.partial(gram_kernel, [piece[1:] for piece in pieces]),
        [shaped((TILE + SUBLANES, width))] * 2,
        [scalars(lax.axis_index("head") % 2), extras] + [piece[0] for piece in pieces],
        smem=1,
    )


def per_device(
    inputs,
    lengths,
    norm_gain,
    in_proj,
    conv_weight,
    conv_bias,
    head_params,
    gate_gain,
    out_proj,
    cotangent,
    norm_gain_mom,
    in_proj_mom,
    conv_weight_mom,
    conv_bias_mom,
    head_params_mom,
    gate_gain_mom,
    out_proj_mom,
):
    members, extent, model_width = inputs.shape
    seq_count = lax.axis_size("seq")
    head_count = lax.axis_size("head")
    seq_place = lax.axis_index("seq")
    head_place = lax.axis_index("head")
    heads_here = head_params.shape[1]
    head_span = gate_gain.shape[0]
    head_size = head_span // heads_here
    channels = conv_bias.shape[0]
    state_size = (channels - head_span) * head_count // 2
    inner_all = head_span * head_count
    group_cols = in_proj.shape[1]
    proj_all = group_cols * head_count
    tap_count = conv_weight.shape[0]
    share = model_width // seq_count
    tokens = members * extent
    quarter = extent // head_count
    runs = seq_count // members

    def own_blocks(blocks):
        return lax.dynamic_slice_in_dim(blocks, head_place * quarter, quarter, 1)

    def own(per_token):
        return pick(per_token.reshape((members, head_count, quarter, -1)), head_place, 1)

    run_place = seq_place // members
    length = lengths[seq_place % members]
    first_slot = run_place * tokens
    place = scalars(length, first_slot, head_place)
    in_low = in_proj.astype(BF)
    out_low = out_proj.astype(BF)
    x_end = 2 * head_span
    bc_end = head_span + channels
    bc_count = channels - head_span
    halo = tap_count - 1
    side_cols = -(-(group_cols - x_end) // LANES) * LANES
    small_rows = SUBLANES * (head_span // LANES + 3) + head_span // LANES + 2 * (model_width // LANES) + 1
    data_piece = own_blocks(inputs)
    data_piece = spread(data_piece, members)
    cot_sent = own_blocks(cotangent)
    decay_rate = -jnp.exp(head_params[1])[:, None]

    def from_run(edge, step):
        pairs = [(i, i + step) for i in range(seq_count) if 0 <= i + step < seq_count]
        return lax.ppermute(edge, "seq", pairs)

    side_weight = jnp.pad(in_low[:, x_end:], ((0, 0), (0, side_cols - (group_cols - x_end)))).T
    weight_cols = jnp.concatenate([conv_weight[:, head_span:], conv_bias[None, head_span:]], axis=0).T
    weight_cols = jnp.pad(weight_cols, ((0, 0), (0, LANES - tap_count - 1)))
    params = jnp.stack([head_params[0], decay_rate[:, 0]], axis=1)
    params = jnp.pad(params, ((0, SUBLANES - heads_here), (0, LANES - 2)))
    z_weight, x_proj = in_low[:, :head_span], in_low[:, head_span:x_end]
    x_weight = conv_weight[:, :head_span]
    skip = jnp.repeat(head_params[2], head_size)[None]
    out_turned = out_low.T
    (
        data_piece, cot_sent, side_weight, weight_cols, params, z_weight, x_proj, out_low, out_turned, place, skip,
    ) = apart_from_here(
        data_piece, cot_sent, side_weight, weight_cols, params, z_weight, x_proj, out_low, out_turned, place, skip,
    )
    cot_piece = spread(cot_sent, members)
    across = flip(data_piece, "head", 2)
    corner = flip(across, "head", 1)
    beside = flip(data_piece, "head", 1)
    pieces = [data_piece, beside, across, corner]
    x_halo = jnp.zeros((SUBLANES, head_span), F32)
    bc_halo = jnp.zeros((bc_count, LANES), F32)
    if runs > 1:
        ends = gather_head(data_piece, 1).reshape(tokens, model_width)[tokens - SUBLANES :].astype(F32)
        ends = ends * lax.rsqrt(jnp.mean(ends * ends, axis=-1, keepdims=True) + EPSILON) * norm_gain
        ends = jnp.dot(ends.astype(BF), in_low[:, head_span:bc_end], preferred_element_type=F32)
        ends = from_run(ends.astype(BF), members).astype(F32)
        x_halo = ends[:, :head_span]
        bc_halo = jnp.pad(ends[:, head_span:].T, ((0, 0), (LANES - SUBLANES, 0)))
    data_low, lowered, root_scale, bc_own, bc_conv, bc_in, rows = enter(
        head_place, pieces, norm_gain[None], side_weight, weight_cols, bc_halo, params, tap_count, heads_here,
        bc_count,
    )
    bc_own, lowered, cot_piece = apart_from_here(bc_own, lowered, cot_piece)
    cot_across = flip(cot_piece, "head", 2)
    bc_across = flip(bc_own, "head", 2)
    bc_beside = flip(bc_own, "head", 1)
    z_part, x_in, x_conv = z_and_x(
        lowered, z_weight, x_proj, x_weight, conv_bias[None, :head_span], x_halo, members
    )
    bc_across, bc_beside, cot_across, z_part = apart_from_here(
        bc_across, bc_beside, cot_across, z_part
    )
    bc_corner = flip(bc_across, "head", 1)
    cot_pieces = [cot_piece, flip(cot_piece, "head", 1), cot_across, flip(cot_across, "head", 1)]
    bc_pieces = [bc_own, bc_beside, bc_across, bc_corner]
    step_sizes = rows[:heads_here]
    growth = jnp.repeat(jnp.exp(jnp.sum(step_sizes * decay_rate, axis=1)), head_size)[None]
    gain = gate_gain[None]

    def scan_from(start):
        return forward_scan(
            place, x_conv, z_part, bc_pieces, rows, skip, gain, out_low, cot_pieces, start, head_size, members
        )

    start = jnp.zeros((state_size, head_span), F32)
    if runs > 1:
        start = entering(growth, scan_from(start)[2], members, False)
    mixed, states, state_end, gated_low, partial_kept, partial_sent, sums, bc_full, cot = scan_from(start)
    sums, partial_sent = apart_from_here(sums, partial_sent)
    partial_come = flip(partial_sent, "head", 1)
    sums, lowered = apart_from_here(added(sums, flip(sums, "head", 1)), lowered)
    sums_come, turned_lowered = apart_from_here(flip(sums, "head", 2), lowered.T)
    norm_rows = stage(
        functools.partial(norm_kernel, inner_all), shaped(sums.shape), [sums, sums_come]
    )
    norm_scale = norm_rows[0]
    grad_mixed, grad_z, grad_summed, gate_gain_grad = gate_back(
        place, cot, norm_rows, z_part, mixed, gain, out_turned, inner_all, members
    )
    low, high = head_place % 2, head_place // 2


    def come_rows(blocks):
        return lax.all_to_all(blocks.reshape((seq_count, share, -1)), "seq", 0, 0, tiled=True)

    early_sent = jnp.concatenate(
        [
            jnp.dot(grad_summed.T, gated_low, preferred_element_type=F32),
            jnp.dot(turned_lowered, grad_z, preferred_element_type=F32),
        ],
        axis=1,
    ).astype(BF)
    slots = first_slot + lax.broadcasted_iota(jnp.int32, (tokens, 1), 0)
    valid_mask = own((slots < length).astype(F32))
    norm_piece = own(norm_scale)
    root_piece = own(root_scale)
    early_old = jnp.concatenate([out_proj_mom.T, in_proj_mom[:, :head_span]], axis=1)
    in_low_wide = jnp.pad(in_low, ((0, 0), (0, x_end + side_cols - group_cols))).T
    late_old = jnp.pad(in_proj_mom[:, head_span:], ((0, 0), (0, x_end + side_cols - group_cols)))
    (
        grad_mixed, early_sent, valid_mask, norm_piece, root_piece, early_old, weight_cols, in_low_wide, late_old,
        turned_lowered, root_scale,
    ) = apart_from_here(
        grad_mixed, early_sent, valid_mask, norm_piece, root_piece, early_old, weight_cols, in_low_wide, late_old,
        turned_lowered, root_scale,
    )
    early_come = come_rows(early_sent)

    def scan_back(back, edge):
        return backward_scan(
            low, grad_mixed, x_conv, x_in, bc_full, rows, states, state_end, skip, x_weight,
            decay_rate, back, edge, head_size, members,
        )

    back = jnp.zeros_like(state_end)
    edge = jnp.zeros((SUBLANES, head_span), F32)
    if runs > 1:
        back = entering(growth, scan_back(back, edge)[3], members, True)
        edge = from_run(scan_back(back, edge)[4], -members)
    grad_x_in, bc_kept, bc_sent, _, _, small, grad_pre, head_sums_out = scan_back(back, edge)

    bc_sent, grad_x_in, bc_kept, early_come = apart_from_here(
        bc_sent, grad_x_in, bc_kept, early_come
    )
    bc_come = flip(bc_sent, "head", 1)
    early_rows, early_mom = rows_step([early_come], early_old, micros=20)
    early_mom, bc_kept = apart_from_here(early_mom, bc_kept)
    full_early = whole_rows(early_mom)
    bc_shape = (2, bc_kept.shape[0] // 2, tokens)
    bc_kept, bc_sent = split_halves(bc_kept.reshape(bc_shape), bc_come.reshape(bc_shape), 0, high)
    bc_kept, bc_sent, grad_x_in = apart_from_here(bc_kept, bc_sent, grad_x_in)
    bc_come = flip(bc_sent, "head", 2)
    x_sent = weight_grad(turned_lowered, grad_x_in)
    x_sent, bc_kept = apart_from_here(x_sent, bc_kept)

    halo_cols = jnp.zeros((bc_in.shape[0], LANES), F32)
    if runs > 1:
        first = (bc_kept[:, :halo] + bc_come[:, :halo].astype(F32)) * silu_slope(bc_conv[:, :halo])
        first = from_run(first.astype(BF), -members).astype(F32)
        halo_cols = jnp.pad(first, ((0, 0), (0, LANES - halo)))
    grad_side, bc_small, late_sent = stage(
        functools.partial(side_kernel, tap_count),
        [
            shaped((tokens, side_cols), BF),
            shaped((bc_in.shape[0], LANES)),
            shaped((model_width, head_span + side_cols), BF),
        ],
        [bc_kept, bc_come, bc_conv, bc_in, weight_cols, halo_cols, grad_pre, turned_lowered, x_sent],
    )
    late_sent, grad_side, partial_kept, partial_come = apart_from_here(
        late_sent, grad_side, partial_kept, partial_come
    )
    late_come = come_rows(late_sent)

    summed_kept, summed_sent = split_halves(partial_kept, partial_come, 0, high)
    summed_kept, summed_sent, grad_side = apart_from_here(summed_kept, summed_sent, grad_side)
    summed_come = flip(summed_sent, "head", 2)
    lowered_kept, lowered_sent, norm_gain_grad = lowered_grad(
        low, grad_z, grad_x_in, grad_side, in_low_wide, data_low, root_scale, members
    )
    lowered_kept, lowered_sent, summed_kept = apart_from_here(lowered_kept, lowered_sent, summed_kept)
    lowered_come = flip(lowered_sent, "head", 1)
    lowered_kept, lowered_sent = split_halves(lowered_kept, lowered_come, 1, high)
    lowered_kept, lowered_sent, summed_kept = apart_from_here(lowered_kept, lowered_sent, summed_kept)
    lowered_come = flip(lowered_sent, "head", 2)
    result, result_squares = stage(
        result_kernel,
        [shaped(data_piece.shape, BF), shaped((1, model_width))],
        [summed_kept, summed_come, data_piece, norm_piece, valid_mask],
    )
    small_blocks = -(-small_rows // share)
    small_sums = stage(
        small_kernel,
        shaped((small_blocks * share, LANES)),
        [small, bc_small, head_sums_out, gate_gain_grad, norm_gain_grad, result_squares],
    )
    small_sums = jnp.moveaxis(small_sums.reshape(small_blocks, share, LANES), 0, 1).reshape(share, -1)
    late_come, small_sums, result, lowered_kept = apart_from_here(
        late_come, small_sums, result, lowered_kept
    )

    late_rows, late_mom = rows_step([late_come], late_old, small_sums)
    late_mom, lowered_kept = apart_from_here(late_mom, lowered_kept)
    full_late = whole_rows(late_mom)
    full_early, lowered_kept = apart_from_here(full_early, lowered_kept)

    no_extras = jnp.zeros((SUBLANES, model_width), F32)
    row_count = -(-share // (2 * SUBLANES)) * 2 * SUBLANES
    picked = seq_place * share + lax.broadcasted_iota(jnp.int32, (row_count, model_width), 0)
    picked = (picked == lax.broadcasted_iota(jnp.int32, picked.shape, 1)).astype(BF)
    pack, pack_sent = gram_packs([(full_early, 0, head_span)], no_extras)
    pieces = stage(
        input_kernel,
        shaped((members, 2 * quarter, model_width), BF),
        [
            lowered_kept, lowered_come, data_piece, cot_piece, root_piece, valid_mask, norm_gain[None, None],
            result,
        ],
    )
    pack, pack_sent, pieces = apart_from_here(pack, pack_sent, pieces)
    pack, picked = apart_from_here(added(pack, flip(pack_sent, "head", 1)), picked)
    pack_come = flip(pack, "head", 2)
    pack, pieces = apart_from_here(pack, pieces)
    pieces = spread(pieces, members)
    pack = added(pack, pack_come)
    opening = newton_opening(pack, flip(pack, "head", 1))
    full_late, opening = apart_from_here(full_late, opening)
    small_sums = full_late[:, full_late.shape[1] - small_blocks * LANES :]
    small_sums = jnp.sum(small_sums.reshape(seq_count, share, -1), axis=0)
    small_sums = jnp.moveaxis(small_sums.reshape(share, small_blocks, LANES), 1, 0)
    small_sums = small_sums.reshape(-1, LANES)[:small_rows]
    late_used = group_cols - head_span
    pack, pack_sent = gram_packs(
        [(full_early, head_span, 2 * head_span), (full_late, 0, late_used)], small_sums
    )
    pack, opening = apart_from_here(added(pack, flip(pack_sent, "head", 1)), opening)
    pack_come = flip(pack, "head", 2)
    turn_out = newton_closing(opening, picked)
    pack, turn_out, pieces = apart_from_here(pack, turn_out, pieces)
    pack, pieces = apart_from_here(added(pack, pack_come), pieces)
    beside, across = flip(pieces, "head", 1), flip(pieces, "head", 2)
    turn_in = newton_rows(pack, flip(pack, "head", 1), picked)
    turn_in, across, beside, small_sums = apart_from_here(turn_in, across, beside, small_sums)
    corner = flip(across, "head", 1)
    turn_in, turn_out = turn_in[:share], turn_out[:share]

    taps_rows = SUBLANES * (head_span // LANES)
    x_small = small_sums[:taps_rows].reshape(-1, SUBLANES, LANES)
    x_small = jnp.moveaxis(x_small, 0, 1).reshape(SUBLANES, head_span)
    bc_small = small_sums[taps_rows : taps_rows + SUBLANES, : channels - head_span]
    both_small = jnp.concatenate([x_small, bc_small], axis=1)
    conv_weight_grad, conv_bias_grad = both_small[:tap_count], both_small[tap_count]
    head_rows = jnp.sum(
        small_sums[taps_rows + SUBLANES : taps_rows + 3 * SUBLANES].reshape(2, SUBLANES, LANES), axis=2
    )[:, :heads_here]
    head_params_grad = jnp.stack(
        [
            head_rows[0],
            head_rows[1] * decay_rate[:, 0],
            jnp.sum(x_small[tap_count + 1].reshape(heads_here, head_size), axis=1),
        ]
    )
    gate_row = taps_rows + 3 * SUBLANES
    gate_gain_grad = small_sums[gate_row : gate_row + head_span // LANES].reshape(-1)
    norm_gain_grad, squares_all = pack[TILE], jnp.sum(pack[TILE + 1])

    out_grad_rows = early_rows[:, :head_span]
    out_rows_mom = early_mom[:, :head_span]
    in_proj_grad = jnp.concatenate(
        [early_rows[:, head_span:], late_rows[:, :late_used]], axis=1
    )
    in_proj_mom_new = jnp.concatenate([early_mom[:, head_span:], late_mom[:, :late_used]], axis=1)

    def turned(turn, matrix):
        return jnp.dot(turn, matrix, precision=lax.Precision.HIGH, preferred_element_type=F32)

    rows_early, rows_late = full_early, full_late[:, : x_end + side_cols - head_span]
    rows_out = turned(turn_out, rows_early[:, :head_span])
    rows_in = jnp.concatenate(
        [turned(turn_in, rows_early[:, head_span:]), turned(turn_in, rows_late)], axis=1
    )[:, :group_cols]
    output, input_grad = in_order(head_place, [pieces, beside, across, corner])
    rms = jnp.sqrt(squares_all / (jnp.sum(lengths).astype(F32) * model_width))
    in_old_rows = lax.dynamic_slice_in_dim(in_proj, seq_place * share, share, 0)
    in_proj_new = in_old_rows - MUON_RATE * 0.2 * math.sqrt(max(model_width, proj_all)) * rows_in
    out_old_cols = lax.dynamic_slice_in_dim(out_proj, seq_place * share, share, 1)
    out_proj_new = (
        out_old_cols - MUON_RATE * 0.2 * math.sqrt(max(inner_all, model_width)) * rows_out.T
    )
    divisor = math.sqrt(members * extent * seq_count)
    norm_gain_mom_new = 0.5 * norm_gain_mom + norm_gain_grad
    conv_weight_mom_new = 0.5 * conv_weight_mom + conv_weight_grad
    conv_bias_mom_new = 0.5 * conv_bias_mom + conv_bias_grad
    head_params_mom_new = 0.5 * head_params_mom + head_params_grad
    gate_gain_mom_new = 0.5 * gate_gain_mom + gate_gain_grad
    norm_gain_new = norm_gain - SMALL_RATE * norm_gain_mom_new / divisor
    conv_weight_new = conv_weight - SMALL_RATE * conv_weight_mom_new / divisor
    conv_bias_new = conv_bias - SMALL_RATE * conv_bias_mom_new / divisor
    head_params_new = head_params - SMALL_RATE * head_params_mom_new / divisor
    gate_gain_new = gate_gain - SMALL_RATE * gate_gain_mom_new / divisor
    return (
        output,
        input_grad,
        norm_gain_grad,
        in_proj_grad,
        conv_weight_grad,
        conv_bias_grad,
        head_params_grad,
        gate_gain_grad,
        out_grad_rows.T,
        norm_gain_mom_new,
        in_proj_mom_new,
        conv_weight_mom_new,
        conv_bias_mom_new,
        head_params_mom_new,
        gate_gain_mom_new,
        out_rows_mom.T,
        norm_gain_new,
        in_proj_new,
        conv_weight_new,
        conv_bias_new,
        head_params_new,
        gate_gain_new,
        out_proj_new,
        rms,
    )


def solution(mesh):
    return jax.shard_map(
        per_device,
        mesh=mesh,
        in_specs=(
            P(None, "seq", None),
            P(),
            P(),
            P(None, "head"),
            P(None, "head"),
            P("head"),
            P(None, "head"),
            P("head"),
            P("head", None),
            P(None, "seq", None),
            P(),
            P("seq", "head"),
            P(None, "head"),
            P("head"),
            P(None, "head"),
            P("head"),
            P("head", "seq"),
        ),
        out_specs=(
            P(None, "seq", None),
            P(None, "seq", None),
            P(),
            P("seq", "head"),
            P(None, "head"),
            P("head"),
            P(None, "head"),
            P("head"),
            P("head", "seq"),
            P(),
            P("seq", "head"),
            P(None, "head"),
            P("head"),
            P(None, "head"),
            P("head"),
            P("head", "seq"),
            P(),
            P("seq", "head"),
            P(None, "head"),
            P("head"),
            P(None, "head"),
            P("head"),
            P("head", "seq"),
            P(),
        ),
        check_vma=False,
    )
```

```python
import functools
import math

import jax
import jax.numpy as jnp
from jax import lax
from jax.experimental import pallas as pl
from jax.experimental.pallas import tpu as pltpu
from jax.sharding import PartitionSpec as P

NS_STEPS = 5
EPSILON = 1e-05
COEF_A = 3.4445
COEF_B = -4.775
COEF_C = 2.0315
MUON_RATE = 0.2
SMALL_RATE = 0.2
PRECISE = lax.Precision.HIGHEST
BF = jnp.bfloat16
F32 = jnp.float32


def silu(values):
    return values * jax.nn.sigmoid(values)


def silu_slope(values):
    sigmoid_value = jax.nn.sigmoid(values)
    return sigmoid_value * (1.0 + values * (1.0 - sigmoid_value))


def flip(value, axis, bit):
    count = lax.axis_size(axis)
    return lax.ppermute(value, axis, [(i, i ^ bit) for i in range(count)])


def sum_over(value, axis):
    bit = 1
    while bit < lax.axis_size(axis):
        value = jax.tree.map(lambda part: part + flip(part, axis, bit), value)
        bit *= 2
    return value


def pick(stacked, index, axis):
    return lax.dynamic_index_in_dim(stacked, index, axis, keepdims=False)


def head_order(piece, beside, across, corner, axis):
    place = lax.axis_index("head")
    low, high = place % 2, place // 2
    near = jnp.where(low == 0, jnp.stack([piece, beside], axis), jnp.stack([beside, piece], axis))
    far = jnp.where(low == 0, jnp.stack([across, corner], axis), jnp.stack([corner, across], axis))
    return jnp.where(
        high == 0, jnp.concatenate([near, far], axis), jnp.concatenate([far, near], axis)
    )


def gather_head(piece, axis):
    across = flip(piece, "head", 2)
    return head_order(piece, flip(piece, "head", 1), across, flip(across, "head", 1), axis)


def head_halves(parts, axis):
    low = lax.axis_index("head") % 2
    shape = parts.shape
    parts = parts.reshape(shape[:axis] + (2, 2) + shape[axis + 1 :])
    return pick(parts, low, axis + 1) + flip(pick(parts, 1 - low, axis + 1), "head", 1)


def head_quarters(half, axis, wire):
    high = lax.axis_index("head") // 2
    return pick(half, high, axis), pick(half, 1 - high, axis).astype(wire)


def head_sum(kept, sent):
    return kept + flip(sent, "head", 2).astype(F32)


def whole_rows(rows):
    return lax.all_gather(rows, "seq", axis=0, tiled=True)


def apart_from_here(*values):
    return lax.optimization_barrier(values)


def spread(blocks, members):
    count = lax.axis_size("seq")
    runs = [list(range(i, i + members)) for i in range(0, count, members)]
    return lax.all_to_all(
        blocks, "seq", 0, 0, tiled=True, axis_index_groups=runs if len(runs) > 1 else None
    )


def entering(growth, state, members, backward):
    count = lax.axis_size("seq")
    runs = count // members
    mine = lax.axis_index("seq") // members
    step = -members if backward else members
    pairs = [(i, i + step) for i in range(count) if 0 <= i + step < count]
    total = jnp.zeros_like(state)
    for _ in range(runs - 1):
        total = lax.ppermute(growth * total + state, "seq", pairs)
    return total


CHUNK = 128
LANES = 128
SUBLANES = 8
VMEM_BYTES = 56 * 1024 * 1024


def split(values, terms):
    pieces = []
    for _ in range(terms):
        pieces.append(values.astype(BF))
        values = values - pieces[-1].astype(F32)
    return pieces


def product(left, right, dims=((1,), (0,))):
    total = None
    for i, a in enumerate(left):
        for j, b in enumerate(right):
            if i + j < max(len(left), len(right)):
                part = lax.dot_general(a, b, (dims, ((), ())), preferred_element_type=F32)
                total = part if total is None else total + part
    return total


ROWS_OF_BOTH = ((1,), (1,))


def columns(rows):
    count, extent = rows.shape
    return jnp.concatenate([rows, jnp.zeros((LANES - count, extent), F32)], axis=0).T


def lane_pair(left, right, half):
    lane = lax.broadcasted_iota(jnp.int32, (CHUNK, LANES), 1)
    return jnp.where(lane < half, left, right)


def apart(pair, half):
    lane = lax.broadcasted_iota(jnp.int32, pair.shape, 1)
    zero = jnp.zeros_like(pair)
    return jnp.concatenate([jnp.where(lane < half, pair, zero), jnp.where(lane < half, zero, pair)], 0)


def head_sums(values, half):
    lane = lax.broadcasted_iota(jnp.int32, values.shape, 1)
    first = jnp.sum(jnp.where(lane < half, values, 0.0), axis=1, keepdims=True)
    return first, jnp.sum(values, axis=1, keepdims=True) - first


def lasting(microseconds):
    return pl.CostEstimate(flops=int(microseconds * 3e8), bytes_accessed=0, transcendentals=0)


def forward_kernel(
    half, terms, place_ref, conv_ref, z_ref, bc0_ref, bc1_ref, bc2_ref, bc3_ref, rows_ref, skip_ref, gain_ref,
    out_low_ref, cot_mine_ref, cot_beside_ref, start_ref,
    mixed_ref, states_ref, end_ref, gated_ref, kept_ref, sent_ref, sums_ref, bc_ref, cot_ref, state_ref,
):
    step = pl.program_id(0)
    block = conv_ref.shape[0]
    span = conv_ref.shape[1]
    pairs = span // LANES

    @pl.when(step == 0)
    def _():
        state_ref[...] = start_ref[...]

    share = bc0_ref.shape[0]
    quarter = cot_mine_ref.shape[2]
    for distance, bc in enumerate((bc0_ref, bc1_ref, bc2_ref, bc3_ref)):
        place = place_ref[2] ^ distance
        bc_ref[pl.ds(pl.multiple_of(place * share, share), share)] = bc[...]
    for distance, cot in enumerate((cot_mine_ref, cot_beside_ref)):
        for k in range(2):
            place = 2 * k + (place_ref[2] % 2 ^ distance)
            cot_ref[pl.ds(pl.multiple_of(place * quarter, quarter), quarter)] = cot[0, k]
    state = 2 * share

    causal = lax.broadcasted_iota(jnp.int32, (CHUNK, CHUNK), 0) >= lax.broadcasted_iota(
        jnp.int32, (CHUNK, CHUNK), 1
    )
    for sub in range(block // CHUNK):
        here = slice(sub * CHUNK, (sub + 1) * CHUNK)
        rows = rows_ref[:, here]
        cols = columns(rows)
        bt_block = bc_ref[:state, here]
        c_block = bc_ref[state:, here].T
        scores = product([c_block], [bt_block])
        states_ref[sub] = state_ref[...]
        state_parts = split(state_ref[...], terms)
        carried = product([c_block], state_parts)
        weighted, grown = [], []
        for pair in range(pairs):
            lanes = slice(pair * LANES, (pair + 1) * LANES)
            first, second = 2 * pair, 2 * pair + 1
            x = silu(conv_ref[here, lanes])

            def pair_cols(table, offset):
                return lane_pair(
                    table[:, offset + first : offset + first + 1],
                    table[:, offset + second : offset + second + 1],
                    half,
                )

            cum = pair_cols(cols, SUBLANES)
            scaled = x * pair_cols(cols, 0)
            last = cum[CHUNK - 1 : CHUNK]
            growth = jnp.exp(cum)
            weighted.append(scaled * jnp.exp(last - cum))
            grown.append(growth[CHUNK - 1 : CHUNK])
            mixing = []
            for head in (first, second):
                gap = cols[:, SUBLANES + head : SUBLANES + head + 1] - rows[SUBLANES + head : SUBLANES + head + 1]
                mixing.append(jnp.exp(jnp.where(causal, gap, -1e30)) * scores)
            inner = product(
                split(jnp.concatenate(mixing, axis=1), terms), split(apart(scaled, half), terms)
            )
            mixed_ref[here, lanes] = inner + carried[:, lanes] * growth + skip_ref[:, lanes] * x
        fresh = product([bt_block], split(jnp.concatenate(weighted, axis=1), terms))
        state_ref[...] = jnp.concatenate(grown, axis=1) * state_ref[...] + fresh
    end_ref[...] = state_ref[...]
    gated = mixed_ref[...] * silu(z_ref[...])
    gated_low = (gated * gain_ref[...]).astype(BF)
    gated_ref[...] = gated_low
    partial = jnp.dot(gated_low, out_low_ref[...], preferred_element_type=F32)
    quarters = partial.reshape((2, 2) + kept_ref.shape[2:])
    low = place_ref[2] % 2
    kept_ref[:, 0] = jnp.where(low == 0, quarters[:, 0], quarters[:, 1])
    sent_ref[:, 0] = jnp.where(low == 0, quarters[:, 1], quarters[:, 0])
    squares = jnp.sum(gated * gated, axis=1, keepdims=True)
    slot = place_ref[1] + step * block + lax.broadcasted_iota(jnp.int32, (block, 1), 0)
    back = jnp.where(slot < place_ref[0], cot_ref[...].astype(F32), 0.0)
    scale = jnp.sum(back * partial, axis=1, keepdims=True)
    lane = lax.broadcasted_iota(jnp.int32, (block, LANES), 1)
    sums = jnp.where(lane == 0, squares, jnp.where(lane == 1, scale, 0.0))
    for sub in range(block // CHUNK):
        here = slice(sub * CHUNK, (sub + 1) * CHUNK)
        sums_ref[:, here] = sums[here].T[:SUBLANES]


def forward_scan(place, conv, z, bc, rows, skip, gain, out_low, cot, start, half, members):
    tokens, span = conv.shape
    share = bc[0].shape[0]
    quarter, width = cot[0].shape[2:]
    state = 2 * share
    block = tokens // members
    subs = block // CHUNK
    by_rows = lambda i, *_: (i, 0)
    by_lanes = lambda i, *_: (0, i)
    whole = lambda i, *_: (0, 0)
    halves = lambda i, *_: (0, i, 0, 0)
    return pl.pallas_call(
        functools.partial(forward_kernel, half, 2),
        grid_spec=pltpu.PrefetchScalarGridSpec(
            num_scalar_prefetch=1,
            grid=(members,),
            in_specs=[
                pl.BlockSpec((block, span), by_rows),
                pl.BlockSpec((block, span), by_rows),
            ]
            + [pl.BlockSpec((share, block), by_lanes)] * 4
            + [
                pl.BlockSpec((3 * SUBLANES, block), by_lanes),
                pl.BlockSpec((1, span), whole),
                pl.BlockSpec((1, span), whole),
                pl.BlockSpec((span, width), whole),
            ]
            + [pl.BlockSpec((1, 2, quarter, width), lambda i, *_: (i, 0, 0, 0))] * 2
            + [pl.BlockSpec((state, span), whole)],
            out_specs=[
                pl.BlockSpec((block, span), by_rows),
                pl.BlockSpec((subs, state, span), lambda i, *_: (i, 0, 0)),
                pl.BlockSpec((state, span), whole),
                pl.BlockSpec((block, span), by_rows),
                pl.BlockSpec((2, 1, quarter, width), halves),
                pl.BlockSpec((2, 1, quarter, width), halves),
                pl.BlockSpec((SUBLANES, block), by_lanes),
                pl.BlockSpec((2 * state, block), by_lanes),
                pl.BlockSpec((block, width), by_rows),
            ],
            scratch_shapes=[pltpu.VMEM((state, span), F32)],
        ),
        out_shape=[
            jax.ShapeDtypeStruct((tokens, span), F32),
            jax.ShapeDtypeStruct((tokens // CHUNK, state, span), F32),
            jax.ShapeDtypeStruct((state, span), F32),
            jax.ShapeDtypeStruct((tokens, span), BF),
            jax.ShapeDtypeStruct((2, members, quarter, width), F32),
            jax.ShapeDtypeStruct((2, members, quarter, width), F32),
            jax.ShapeDtypeStruct((SUBLANES, tokens), F32),
            jax.ShapeDtypeStruct((2 * state, tokens), BF),
            jax.ShapeDtypeStruct((tokens, width), BF),
        ],
        compiler_params=pltpu.CompilerParams(vmem_limit_bytes=VMEM_BYTES),
        cost_estimate=lasting(17),
    )(place, conv, z, *bc, rows, skip, gain, out_low, *cot, start)


def gate_kernel(
    inner_all, place_ref, cot_ref, norm_ref, z_ref, mixed_ref, gain_ref, out_turned_ref,
    grad_mixed_ref, grad_z_ref, grad_summed_ref, gain_grad_ref,
):
    step = pl.program_id(0)
    block = cot_ref.shape[0]
    norm = jnp.concatenate(
        [columns(norm_ref[:, sub * CHUNK : (sub + 1) * CHUNK]) for sub in range(block // CHUNK)], 0
    )
    norm_scale, grad_scale = norm[:, 0:1], norm[:, 1:2]
    slot = place_ref[1] + step * block + lax.broadcasted_iota(jnp.int32, (block, 1), 0)
    back = jnp.where(slot < place_ref[0], cot_ref[...].astype(F32), 0.0)
    grad_summed = (norm_scale * back).astype(BF)
    grad_summed_ref[...] = grad_summed
    grad_low = jnp.dot(grad_summed, out_turned_ref[...], preferred_element_type=F32)
    z, mixed = z_ref[...], mixed_ref[...]
    sigmoid = jax.nn.sigmoid(z)
    gate = z * sigmoid
    gated = mixed * gate
    shrink = grad_scale * norm_scale * norm_scale * norm_scale / inner_all
    grad_gated = grad_low * gain_ref[...] - shrink * gated
    grad_mixed_ref[...] = grad_gated * gate
    grad_z_ref[...] = (grad_gated * mixed * (sigmoid * (1.0 + z * (1.0 - sigmoid)))).astype(BF)

    @pl.when(step == 0)
    def _():
        gain_grad_ref[...] = jnp.zeros_like(gain_grad_ref)

    gain_grad_ref[...] += jnp.sum(grad_low * gated, axis=0, keepdims=True)


def gate_back(place, cot, norm_rows, z, mixed, gain, out_turned, inner_all, members):
    tokens, span = z.shape
    width = cot.shape[1]
    block = tokens // members
    by_rows = lambda i, *_: (i, 0)
    whole = lambda i, *_: (0, 0)
    return pl.pallas_call(
        functools.partial(gate_kernel, inner_all),
        grid_spec=pltpu.PrefetchScalarGridSpec(
            num_scalar_prefetch=1,
            grid=(members,),
            in_specs=[
                pl.BlockSpec((block, width), by_rows),
                pl.BlockSpec((SUBLANES, block), lambda i, *_: (0, i)),
                pl.BlockSpec((block, span), by_rows),
                pl.BlockSpec((block, span), by_rows),
                pl.BlockSpec((1, span), whole),
                pl.BlockSpec((width, span), whole),
            ],
            out_specs=[
                pl.BlockSpec((block, span), by_rows),
                pl.BlockSpec((block, span), by_rows),
                pl.BlockSpec((block, width), by_rows),
                pl.BlockSpec((1, span), whole),
            ],
        ),
        out_shape=[
            jax.ShapeDtypeStruct((tokens, span), F32),
            jax.ShapeDtypeStruct((tokens, span), BF),
            jax.ShapeDtypeStruct((tokens, width), BF),
            jax.ShapeDtypeStruct((1, span), F32),
        ],
        compiler_params=pltpu.CompilerParams(vmem_limit_bytes=VMEM_BYTES),
        cost_estimate=lasting(12),
    )(place, cot, norm_rows, z, mixed, gain, out_turned)


def backward_kernel(
    half, terms, taps, low_ref, grad_ref, conv_ref, conv_in_ref, bc_ref, rows_ref,
    states_ref, end_ref, skip_ref, weight_ref, rate_ref, back_ref, halo_ref,
    grad_x_ref, kept_ref, sent_ref, first_ref, edge_ref, small_ref, pre_ref, sums_ref,
    carry_ref, after_ref, shift_ref,
):
    step = pl.program_id(0)
    block = conv_ref.shape[0]
    span = conv_ref.shape[1]
    pairs = span // LANES
    state = bc_ref.shape[0] // 2
    subs = block // CHUNK

    @pl.when(step == 0)
    def _():
        carry_ref[...] = back_ref[...]
        after_ref[...] = end_ref[...]
        shift_ref[:SUBLANES] = halo_ref[...]
        small_ref[...] = jnp.zeros_like(small_ref)
        sums_ref[...] = jnp.zeros_like(sums_ref)

    low = low_ref[0]
    row = lax.broadcasted_iota(jnp.int32, (CHUNK, CHUNK), 0)
    lane = lax.broadcasted_iota(jnp.int32, (CHUNK, CHUNK), 1)
    causal = row <= lane
    for sub in reversed(range(subs)):
        here = slice(sub * CHUNK, (sub + 1) * CHUNK)
        rows = rows_ref[:, here]
        cols = columns(rows)
        bt_block, ct_block = bc_ref[:state, here], bc_ref[state:, here]
        b_block, c_block = bt_block.T, ct_block.T
        scores = product([b_block], [ct_block])
        entered = states_ref[sub]
        carry = carry_ref[...]
        entered_parts = split(entered, terms)
        carry_parts = split(carry, terms)
        carried = product([c_block], entered_parts)
        pulled = product([b_block], carry_parts)
        joint = jnp.sum(carry * after_ref[...], axis=0, keepdims=True)
        after_ref[...] = entered
        head_of = lax.broadcasted_iota(jnp.int32, (SUBLANES, span), 1) // half
        joint = jnp.sum(
            jnp.where(head_of == lax.broadcasted_iota(jnp.int32, (SUBLANES, span), 0), joint, 0.0),
            axis=1,
            keepdims=True,
        )
        weighted, grown_grad, grown = [], [], []
        grad_scores = jnp.zeros((CHUNK, CHUNK), F32)
        col_sums = jnp.zeros((CHUNK, LANES), F32)
        row_sums = []
        for pair in range(pairs):
            lanes = slice(pair * LANES, (pair + 1) * LANES)
            first, second = 2 * pair, 2 * pair + 1

            def pair_cols(offset):
                return lane_pair(
                    cols[:, offset + first : offset + first + 1],
                    cols[:, offset + second : offset + second + 1],
                    half,
                )

            conv = conv_ref[here, lanes]
            sigmoid = jax.nn.sigmoid(conv)
            x = conv * sigmoid
            grad = grad_ref[here, lanes]
            cum, size = pair_cols(SUBLANES), pair_cols(0)
            scaled = x * size
            last = cum[CHUNK - 1 : CHUNK]
            growth = jnp.exp(cum)
            tail = jnp.exp(last - cum)
            weighted.append(scaled * tail)
            grown_grad.append(grad * growth)
            grown.append(growth[CHUNK - 1 : CHUNK])
            grad_apart = split(apart(grad, half), terms)
            dots = product(split(scaled, terms), grad_apart, ROWS_OF_BOTH)
            kernels = []
            for k, head in enumerate((first, second)):
                gap = rows[SUBLANES + head : SUBLANES + head + 1] - cols[:, SUBLANES + head : SUBLANES + head + 1]
                decay = jnp.exp(jnp.where(causal, gap, -1e30))
                grad_score = decay * dots[:, k * CHUNK : (k + 1) * CHUNK]
                grad_scores = grad_scores + grad_score
                kernels.append(decay * scores)
                both = grad_score * scores
                row_sums.append(jnp.sum(both, axis=0, keepdims=True))
                col_sums = jnp.where(
                    lane == head, col_sums - jnp.sum(both, axis=1, keepdims=True), col_sums
                )
            pulled_pair = tail * pulled[:, lanes]
            force = product(split(jnp.concatenate(kernels, axis=1), terms), grad_apart) + pulled_pair
            grad_x = size * force + skip_ref[:, lanes] * grad
            flow = grown_grad[-1] * carried[:, lanes] - scaled * pulled_pair
            direct = x * force
            for head, flow_sum, direct_sum in zip(
                (first, second), head_sums(flow, half), head_sums(direct, half)
            ):
                col_sums = jnp.where(lane == head, col_sums + flow_sum, col_sums)
                col_sums = jnp.where(lane == SUBLANES + head, direct_sum, col_sums)
            small_ref[taps + 1 : taps + 2, lanes] += jnp.sum(grad * x, axis=0, keepdims=True)
            grad_conv = (grad_x * (sigmoid * (1.0 + conv * (1.0 - sigmoid)))).astype(BF).astype(F32)
            shift_ref[CHUNK : CHUNK + SUBLANES, lanes] = shift_ref[:SUBLANES, lanes]
            shift_ref[:CHUNK, lanes] = grad_conv
            conv_in = conv_in_ref[here, lanes].astype(F32)
            total = None
            for tap in range(taps):
                moved = shift_ref[taps - 1 - tap : taps - 1 - tap + CHUNK, lanes]
                term = weight_ref[tap : tap + 1, lanes] * moved
                total = term if total is None else total + term
                small_ref[tap : tap + 1, lanes] += jnp.sum(conv_in * moved, axis=0, keepdims=True)
            small_ref[taps : taps + 1, lanes] += jnp.sum(grad_conv, axis=0, keepdims=True)
            grad_x_ref[here, lanes] = total.astype(BF)
        grown_parts = split(jnp.concatenate(grown_grad, axis=1), terms)
        weighted_parts = split(jnp.concatenate(weighted, axis=1), terms)
        grad_b = product(carry_parts, weighted_parts, ROWS_OF_BOTH) + product(
            [ct_block], split(grad_scores.T, terms)
        )
        grad_c = product(entered_parts, grown_parts, ROWS_OF_BOTH) + product(
            [bt_block], split(grad_scores, terms)
        )
        middle = state // 2
        for k, part in enumerate((grad_b, grad_c)):
            place = slice(k * middle, (k + 1) * middle)
            kept_ref[place, here] = jnp.where(low == 0, part[:middle], part[middle:])
            sent_ref[place, here] = jnp.where(low == 0, part[middle:], part[:middle])
        carry_ref[...] = jnp.concatenate(grown, axis=1) * carry + product([ct_block], grown_parts)
        turned = col_sums.T
        row_sums.append(jnp.zeros((SUBLANES - 2 * pairs, CHUNK), F32))
        slots = lax.broadcasted_iota(jnp.int32, (SUBLANES, CHUNK), 1)
        grad_cum = (
            jnp.concatenate(row_sums, axis=0)
            + turned[:SUBLANES]
            + jnp.where(slots == CHUNK - 1, joint, 0.0)
        )
        grad_decay = product(split(grad_cum, 3), [(row >= lane).astype(BF)])
        grad_pre = (turned[SUBLANES : 2 * SUBLANES] + grad_decay * rate_ref[...]) * rows[2 * SUBLANES :]
        pre_ref[:, here] = grad_pre
        sums_ref[:SUBLANES] += grad_pre
        sums_ref[SUBLANES:] += grad_decay * rows[:SUBLANES]
    first_ref[...] = carry_ref[...]
    edge_ref[...] = shift_ref[:SUBLANES]


def backward_scan(
    low, grad, conv, conv_in, bc, rows, states, end, skip, weight, rate, back, halo, half,
    members,
):
    tokens, span = conv.shape
    state = bc.shape[0] // 2
    taps = weight.shape[0]
    block = tokens // members
    subs = block // CHUNK
    final = members - 1
    by_rows = lambda i, *_: (final - i, 0)
    by_lanes = lambda i, *_: (0, final - i)
    whole = lambda i, *_: (0, 0)
    return pl.pallas_call(
        functools.partial(backward_kernel, half, 2, taps),
        grid_spec=pltpu.PrefetchScalarGridSpec(
        num_scalar_prefetch=1,
        grid=(members,),
        in_specs=[
            pl.BlockSpec((block, span), by_rows),
            pl.BlockSpec((block, span), by_rows),
            pl.BlockSpec((block, span), by_rows),
            pl.BlockSpec((2 * state, block), by_lanes),
            pl.BlockSpec((3 * SUBLANES, block), by_lanes),
            pl.BlockSpec((subs, state, span), lambda i, *_: (final - i, 0, 0)),
            pl.BlockSpec((state, span), whole),
            pl.BlockSpec((1, span), whole),
            pl.BlockSpec((taps, span), whole),
            pl.BlockSpec((SUBLANES, 1), whole),
            pl.BlockSpec((state, span), whole),
            pl.BlockSpec((SUBLANES, span), whole),
        ],
        out_specs=[
            pl.BlockSpec((block, span), by_rows),
            pl.BlockSpec((state, block), by_lanes),
            pl.BlockSpec((state, block), by_lanes),
            pl.BlockSpec((state, span), whole),
            pl.BlockSpec((SUBLANES, span), whole),
            pl.BlockSpec((SUBLANES, span), whole),
            pl.BlockSpec((SUBLANES, block), by_lanes),
            pl.BlockSpec((2 * SUBLANES, LANES), whole),
        ],
        scratch_shapes=[
            pltpu.VMEM((state, span), F32),
            pltpu.VMEM((state, span), F32),
            pltpu.VMEM((CHUNK + SUBLANES, span), F32),
        ],
        ),
        out_shape=[
            jax.ShapeDtypeStruct((tokens, span), BF),
            jax.ShapeDtypeStruct((state, tokens), F32),
            jax.ShapeDtypeStruct((state, tokens), F32),
            jax.ShapeDtypeStruct((state, span), F32),
            jax.ShapeDtypeStruct((SUBLANES, span), F32),
            jax.ShapeDtypeStruct((SUBLANES, span), F32),
            jax.ShapeDtypeStruct((SUBLANES, tokens), F32),
            jax.ShapeDtypeStruct((2 * SUBLANES, LANES), F32),
        ],
        compiler_params=pltpu.CompilerParams(vmem_limit_bytes=VMEM_BYTES),
        cost_estimate=lasting(25),
    )(
        scalars(low), grad, conv, conv_in, bc, rows, states, end, skip, weight,
        jnp.pad(rate, ((0, SUBLANES - rate.shape[0]), (0, 0))), back, halo,
    )


def vmem(count):
    return [pl.BlockSpec(memory_space=pltpu.VMEM)] * count


def scalars(*values):
    return jnp.stack(values).astype(jnp.int32)


def stage(kernel, out_shape, operands, smem=0, micros=0.01):
    return pl.pallas_call(
        kernel,
        out_shape=out_shape,
        in_specs=[pl.BlockSpec(memory_space=pltpu.SMEM)] * smem + vmem(len(operands) - smem),
        out_specs=jax.tree.map(lambda _: pl.BlockSpec(memory_space=pltpu.VMEM), out_shape),
        compiler_params=pltpu.CompilerParams(vmem_limit_bytes=VMEM_BYTES),
        cost_estimate=lasting(micros),
    )(*operands)


def shaped(shape, dtype=F32):
    return jax.ShapeDtypeStruct(shape, dtype)


def add_kernel(a_ref, b_ref, out_ref):
    out_ref[...] = a_ref[...] + b_ref[...].astype(F32)


def added(a, b):
    return stage(add_kernel, shaped(a.shape), [a, b])


def split_kernel(axis, high_ref, kept_ref, come_ref, own_ref, sent_ref):
    high = high_ref[0]
    total = [
        kept_ref[(slice(None),) * axis + (k,)] + come_ref[(slice(None),) * axis + (k,)] for k in (0, 1)
    ]
    own_ref[...] = jnp.where(high == 0, total[0], total[1])
    sent_ref[...] = jnp.where(high == 0, total[1], total[0]).astype(BF)


def split_halves(kept, come, axis, high):
    shape = kept.shape[:axis] + kept.shape[axis + 1 :]
    return stage(
        functools.partial(split_kernel, axis),
        [shaped(shape), shaped(shape, BF)],
        [scalars(high), kept, come],
        smem=1,
    )


def rows_kernel(pieces, *refs):
    old_ref, sum_ref, mom_ref = refs[pieces], refs[-2], refs[-1]
    left = 0
    for ref in refs[:pieces]:
        cols = slice(left, left + ref.shape[2])
        left = cols.stop
        total = jnp.sum(ref[...].astype(F32), axis=0)
        sum_ref[:, cols] = total
        mom_ref[:, cols] = 0.5 * old_ref[:, cols] + total
    if mom_ref.shape[1] > left:
        mom_ref[:, left:] = refs[pieces + 1][...]


def rows_step(come, old, *others, micros=0.01):
    wide = old.shape[1] + sum(other.shape[1] for other in others)
    return stage(
        functools.partial(rows_kernel, len(come)),
        [shaped(old.shape), shaped((old.shape[0], wide))],
        [*come, old, *others],
        micros=micros,
    )


def weight_kernel(turned_ref, grad_ref, out_ref):
    out_ref[...] = jnp.dot(turned_ref[...], grad_ref[...], preferred_element_type=F32).astype(BF)


def weight_grad(turned, grad):
    return stage(weight_kernel, shaped((turned.shape[0], grad.shape[1]), BF), [turned, grad])


def side_kernel(taps, kept_ref, come_ref, conv_ref, conv_in_ref, weight_ref, halo_ref, pre_ref, turned_ref,
                x_ref, side_ref, small_ref, out_ref):
    tokens = kept_ref.shape[1]
    conv = conv_ref[...]
    sigmoid = jax.nn.sigmoid(conv)
    slope = sigmoid * (1.0 + conv * (1.0 - sigmoid))
    grad = ((kept_ref[...] + come_ref[...].astype(F32)) * slope).astype(BF).astype(F32)
    conv_in = conv_in_ref[...].astype(F32)
    wide = jnp.concatenate([grad, halo_ref[...]], axis=1)
    lane = lax.broadcasted_iota(jnp.int32, small_ref.shape, 1)
    small = jnp.where(lane == taps, jnp.sum(grad, axis=1, keepdims=True), 0.0)
    total = None
    for tap in range(taps):
        lead = taps - 1 - tap
        moved = pltpu.roll(wide, wide.shape[1] - lead, 1)[:, :tokens] if lead else grad
        term = weight_ref[:, tap : tap + 1] * moved
        total = term if total is None else total + term
        small = jnp.where(lane == tap, jnp.sum(moved * conv_in, axis=1, keepdims=True), small)
    small_ref[...] = small
    used = total.shape[0] + pre_ref.shape[0]
    spare = jnp.zeros((LANES - used, tokens), F32)
    side = jnp.concatenate([total, pre_ref[...], spare], axis=0).astype(BF).T
    side_ref[...] = side
    span = x_ref.shape[1]
    out_ref[:, :span] = x_ref[...]
    out_ref[:, span:] = jnp.dot(turned_ref[...], side, preferred_element_type=F32).astype(BF)


def lowered_kernel(
    low_ref, z_ref, x_ref, side_ref, weight_ref, data_ref, root_ref, kept_ref, sent_ref, gain_ref
):
    step = pl.program_id(0)
    span = z_ref.shape[1]
    total = jnp.dot(z_ref[...], weight_ref[:span], preferred_element_type=F32)
    total = total + jnp.dot(x_ref[...], weight_ref[span : 2 * span], preferred_element_type=F32)
    total = total + jnp.dot(side_ref[...], weight_ref[2 * span :], preferred_element_type=F32)
    normed = data_ref[...].astype(F32) * root_ref[...]

    @pl.when(step == 0)
    def _():
        gain_ref[...] = jnp.zeros_like(gain_ref)

    gain_ref[...] += jnp.sum(total * normed, axis=0, keepdims=True)
    parts = total.reshape((2, 2) + kept_ref.shape[2:])
    low = low_ref[0]
    kept_ref[0] = jnp.where(low == 0, parts[:, 0], parts[:, 1])
    sent_ref[0] = jnp.where(low == 0, parts[:, 1], parts[:, 0])


def lowered_grad(low, grad_z, grad_x, side, weight, data, root, members):
    tokens, width = data.shape
    block = tokens // members
    by_rows = lambda i, *_: (i, 0)
    whole = lambda i, *_: (0, 0)
    half = (1, 2, block // 4, width)
    return pl.pallas_call(
        lowered_kernel,
        grid_spec=pltpu.PrefetchScalarGridSpec(
            num_scalar_prefetch=1,
            grid=(members,),
            in_specs=[
                pl.BlockSpec((block, grad_z.shape[1]), by_rows),
                pl.BlockSpec((block, grad_x.shape[1]), by_rows),
                pl.BlockSpec((block, side.shape[1]), by_rows),
                pl.BlockSpec(weight.shape, whole),
                pl.BlockSpec((block, width), by_rows),
                pl.BlockSpec((block, 1), by_rows),
            ],
            out_specs=[
                pl.BlockSpec(half, lambda i, *_: (i, 0, 0, 0)),
                pl.BlockSpec(half, lambda i, *_: (i, 0, 0, 0)),
                pl.BlockSpec((1, width), whole),
            ],
        ),
        out_shape=[
            shaped((members,) + half[1:]),
            shaped((members,) + half[1:]),
            shaped((1, width)),
        ],
        compiler_params=pltpu.CompilerParams(vmem_limit_bytes=VMEM_BYTES),
        cost_estimate=lasting(0.01),
    )(scalars(low), grad_z, grad_x, side, weight, data, root)


def result_kernel(kept_ref, come_ref, data_ref, norm_ref, mask_ref, out_ref, squares_ref):
    result = kept_ref[...] + come_ref[...].astype(F32)
    result = mask_ref[...] * (data_ref[...].astype(F32) + norm_ref[...] * result)
    out_ref[...] = result.astype(BF)
    squares_ref[...] = jnp.sum(result * result, axis=(0, 1), keepdims=True)[0]


def input_kernel(kept_ref, come_ref, data_ref, cot_ref, root_ref, mask_ref, gain_ref, result_ref, out_ref):
    quarter = kept_ref.shape[1]
    grad = (kept_ref[...] + come_ref[...].astype(F32)) * gain_ref[...]
    normed = data_ref[...].astype(F32) * root_ref[...]
    shrink = jnp.mean(grad * normed, axis=-1, keepdims=True)
    back = mask_ref[...] * cot_ref[...].astype(F32)
    out_ref[:, :quarter] = result_ref[...]
    out_ref[:, quarter:] = (back + root_ref[...] * (grad - normed * shrink)).astype(BF)


def small_kernel(small_ref, bc_ref, sums_ref, gate_ref, gain_ref, squares_ref, out_ref):
    out_ref[...] = jnp.zeros_like(out_ref)
    row = 0
    for k in range(small_ref.shape[1] // LANES):
        out_ref[row : row + SUBLANES] = small_ref[:, k * LANES : (k + 1) * LANES]
        row += SUBLANES
    turned = bc_ref[...].T[:SUBLANES]
    out_ref[row : row + SUBLANES, : turned.shape[1]] = turned
    row += SUBLANES
    out_ref[row : row + 2 * SUBLANES] = sums_ref[...]
    row += 2 * SUBLANES
    for ref in (gate_ref, gain_ref, squares_ref):
        for k in range(ref.shape[1] // LANES):
            out_ref[row : row + 1] = ref[:, k * LANES : (k + 1) * LANES]
            row += 1


def order_kernel(place_ref, *refs):
    output_ref, grad_ref = refs[4:]
    quarter = refs[0].shape[1] // 2
    for distance, ref in enumerate(refs[:4]):
        start = pl.multiple_of((place_ref[0] ^ distance) * quarter, quarter)
        output_ref[0, pl.ds(start, quarter)] = ref[0, :quarter]
        grad_ref[0, pl.ds(start, quarter)] = ref[0, quarter:].astype(F32)


def in_order(place, pieces):
    members, both, width = pieces[0].shape
    rows = 2 * both
    block = lambda i, *_: (i, 0, 0)
    return pl.pallas_call(
        order_kernel,
        grid_spec=pltpu.PrefetchScalarGridSpec(
            num_scalar_prefetch=1,
            grid=(members,),
            in_specs=[pl.BlockSpec((1, both, width), block)] * 4,
            out_specs=[pl.BlockSpec((1, rows, width), block)] * 2,
        ),
        out_shape=[shaped((members, rows, width), BF), shaped((members, rows, width))],
        compiler_params=pltpu.CompilerParams(vmem_limit_bytes=VMEM_BYTES),
        cost_estimate=lasting(5),
    )(scalars(place), *pieces)


def norm_kernel(inner_all, mine_ref, come_ref, out_ref):
    total = mine_ref[...] + come_ref[...]
    row = lax.broadcasted_iota(jnp.int32, total.shape, 0)
    out_ref[...] = jnp.where(row == 0, lax.rsqrt(total / inner_all + EPSILON), total)


def enter_kernel(
    taps, heads, place_ref, own_ref, beside_ref, across_ref, corner_ref, gain_ref, side_weight_ref, weight_ref,
    halo_ref, params_ref, data_ref, lowered_ref, root_ref, bc_ref, conv_ref, conv_in_ref, rows_ref, carry_ref,
):
    quarter = own_ref.shape[1]
    block = data_ref.shape[0]
    channels = bc_ref.shape[0]
    for distance, ref in enumerate((own_ref, beside_ref, across_ref, corner_ref)):
        start = pl.multiple_of((place_ref[0] ^ distance) * quarter, quarter)
        data_ref[pl.ds(start, quarter)] = ref[0]
    data = data_ref[...].astype(F32)
    root = lax.rsqrt(jnp.mean(data * data, axis=1, keepdims=True) + EPSILON)
    root_ref[...] = root
    lowered = (data * root * gain_ref[...]).astype(BF)
    lowered_ref[...] = lowered
    side = lax.dot_general(
        side_weight_ref[...], lowered, (ROWS_OF_BOTH, ((), ())), preferred_element_type=F32
    )

    @pl.when(pl.program_id(0) == 0)
    def _():
        carry_ref[...] = halo_ref[...]

    conv_low = side[:channels].astype(BF)
    conv_in_ref[...] = conv_low
    conv_in = conv_low.astype(F32)
    wide = jnp.concatenate([carry_ref[...], conv_in], axis=1)
    carry_ref[...] = conv_in[:, block - LANES :]
    conv = weight_ref[:, taps : taps + 1] + weight_ref[:, taps - 1 : taps] * conv_in
    for tap in range(taps - 1):
        conv = conv + weight_ref[:, tap : tap + 1] * pltpu.roll(wide, taps - 1 - tap, 1)[:, LANES:]
    conv_ref[...] = conv
    bc_ref[...] = silu(conv).astype(BF)

    head = lax.broadcasted_iota(jnp.int32, (SUBLANES, block), 0)
    pre = side[channels : channels + SUBLANES] + params_ref[:, 0:1]
    size = jnp.where(head < heads, jax.nn.softplus(pre), 0.0)
    change = size * params_ref[:, 1:2]
    row = lax.broadcasted_iota(jnp.int32, (CHUNK, CHUNK), 0)
    upto = (row <= lax.broadcasted_iota(jnp.int32, (CHUNK, CHUNK), 1)).astype(BF)
    rows_ref[:SUBLANES] = size
    for sub in range(block // CHUNK):
        here = slice(sub * CHUNK, (sub + 1) * CHUNK)
        rows_ref[SUBLANES : 2 * SUBLANES, here] = product(split(change[:, here], 3), [upto])
    rows_ref[2 * SUBLANES :] = jnp.where(head < heads, jax.nn.sigmoid(pre), 0.0)


def enter(place, pieces, gain, side_weight, weight, halo, params, taps, heads, channels):
    members, quarter, width = pieces[0].shape
    block = 4 * quarter
    tokens = members * block
    by_rows = lambda i, *_: (i, 0)
    by_lanes = lambda i, *_: (0, i)
    whole = lambda i, *_: (0, 0)
    return pl.pallas_call(
        functools.partial(enter_kernel, taps, heads),
        grid_spec=pltpu.PrefetchScalarGridSpec(
            num_scalar_prefetch=1,
            grid=(members,),
            in_specs=[pl.BlockSpec((1, quarter, width), lambda i, *_: (i, 0, 0))] * 4
            + [
                pl.BlockSpec((1, width), whole),
                pl.BlockSpec(side_weight.shape, whole),
                pl.BlockSpec(weight.shape, whole),
                pl.BlockSpec(halo.shape, whole),
                pl.BlockSpec(params.shape, whole),
            ],
            out_specs=[
                pl.BlockSpec((block, width), by_rows),
                pl.BlockSpec((block, width), by_rows),
                pl.BlockSpec((block, 1), by_rows),
                pl.BlockSpec((channels, block), by_lanes),
                pl.BlockSpec((channels, block), by_lanes),
                pl.BlockSpec((channels, block), by_lanes),
                pl.BlockSpec((3 * SUBLANES, block), by_lanes),
            ],
            scratch_shapes=[pltpu.VMEM((channels, LANES), F32)],
        ),
        out_shape=[
            jax.ShapeDtypeStruct((tokens, width), BF),
            jax.ShapeDtypeStruct((tokens, width), BF),
            jax.ShapeDtypeStruct((tokens, 1), F32),
            jax.ShapeDtypeStruct((channels, tokens), BF),
            jax.ShapeDtypeStruct((channels, tokens), F32),
            jax.ShapeDtypeStruct((channels, tokens), BF),
            jax.ShapeDtypeStruct((3 * SUBLANES, tokens), F32),
        ],
        compiler_params=pltpu.CompilerParams(vmem_limit_bytes=VMEM_BYTES),
        cost_estimate=lasting(8),
    )(scalars(place), *pieces, gain, side_weight, weight, halo, params)


def columns_kernel(
    taps, lowered_ref, z_weight_ref, x_weight_ref, weight_ref, bias_ref, halo_ref, z_ref, x_in_ref, conv_ref,
    shift_ref,
):
    block = lowered_ref.shape[0]
    lowered = lowered_ref[...]
    z_ref[...] = jnp.dot(lowered, z_weight_ref[...], preferred_element_type=F32)
    conv_low = jnp.dot(lowered, x_weight_ref[...], preferred_element_type=F32).astype(BF)
    x_in_ref[...] = conv_low

    @pl.when(pl.program_id(0) == 0)
    def _():
        shift_ref[:SUBLANES] = halo_ref[...]

    shift_ref[SUBLANES:] = conv_low.astype(F32)
    conv = jnp.broadcast_to(bias_ref[...], conv_ref.shape)
    for tap in range(taps):
        first = SUBLANES - (taps - 1) + tap
        conv = conv + weight_ref[tap : tap + 1] * shift_ref[first : first + block]
    conv_ref[...] = conv
    shift_ref[:SUBLANES] = shift_ref[block:]


def z_and_x(lowered, proj, weight, bias, halo, members):
    tokens, width = lowered.shape
    span = weight.shape[1]
    block = tokens // members
    by_rows = lambda i: (i, 0)
    whole = lambda i: (0, 0)
    return pl.pallas_call(
        functools.partial(columns_kernel, weight.shape[0]),
        grid=(members,),
        in_specs=[
            pl.BlockSpec((block, width), by_rows),
            pl.BlockSpec((width, span), whole),
            pl.BlockSpec((width, span), lambda i: (0, 1)),
            pl.BlockSpec(weight.shape, whole),
            pl.BlockSpec((1, span), whole),
            pl.BlockSpec((SUBLANES, span), whole),
        ],
        out_specs=[pl.BlockSpec((block, span), by_rows)] * 3,
        out_shape=[
            jax.ShapeDtypeStruct((tokens, span), F32),
            jax.ShapeDtypeStruct((tokens, span), BF),
            jax.ShapeDtypeStruct((tokens, span), F32),
        ],
        scratch_shapes=[pltpu.VMEM((block + SUBLANES, span), F32)],
        compiler_params=pltpu.CompilerParams(vmem_limit_bytes=VMEM_BYTES),
        cost_estimate=lasting(8),
    )(lowered, proj, proj, weight, bias, halo)


TILE = 256


def tiles_of(width):
    starts = range(0, width, TILE)
    return [(i, j) for i in starts for j in starts if i <= j]


def at(start):
    return slice(start, start + TILE)


def put(pair, i, j, values):
    for row, col, tile in ((i, j, values), (j, i, values.T))[: 1 if i == j else 2]:
        high = tile.astype(BF)
        pair[0, at(row), at(col)] = high
        pair[1, at(row), at(col)] = (tile - high.astype(F32)).astype(BF)


def tile_of(left, right, i, j):
    high, low = left[0, at(i)], left[1, at(i)]
    total = jnp.dot(high, right[1, :, at(j)], preferred_element_type=F32)
    total = total + jnp.dot(low, right[0, :, at(j)], preferred_element_type=F32)
    return total + jnp.dot(high, right[0, :, at(j)], preferred_element_type=F32)


def eye(rows, cols):
    return lax.broadcasted_iota(jnp.int32, (rows, cols), 0) == lax.broadcasted_iota(
        jnp.int32, (rows, cols), 1
    )


def newton_kernel(opens, closes, steps, *refs):
    refs = list(refs)
    low_ref = refs.pop(0) if opens else None
    gram_in = refs.pop(0)
    other_in = refs.pop(0) if opens else None
    factor_in = None if opens else refs.pop(0)
    before = [refs.pop(0)] if closes and not opens else []
    picked_ref = refs.pop(0) if closes else None
    gram_out = refs.pop(0) if not closes else None
    rows_ref = refs.pop(0) if closes else None
    factor_out = refs.pop(0) if opens and not closes else None
    polys = refs.pop(0) if steps else None
    gram, first, second, third = refs
    width = gram.shape[0]
    tiles = tiles_of(width)
    if opens:
        low = low_ref[0]
        upper = jnp.where(low == 0, gram_in[:TILE], other_in[:TILE])
        lower = jnp.where(low == 0, other_in[:TILE], gram_in[:TILE])
        gram[at(0)] = upper
        gram[at(TILE), TILE:] = lower[:, : width - TILE]
        gram[at(2 * TILE), 2 * TILE :] = lower[:, width - TILE :]
        size = jnp.zeros((1, 1), F32)
        for i in range(0, width, TILE):
            size = size + jnp.sum(jnp.where(eye(TILE, TILE), gram[at(i), at(i)], 0.0), keepdims=True)
        factor = 1.0 / (jnp.sqrt(size) + 1e-07)
        if factor_out is not None:
            factor_out[...] = jnp.broadcast_to(factor, factor_out.shape)
    else:
        factor = factor_in[0:1, 0:1]
    for i, j in tiles:
        values = gram[at(i), at(j)] * (factor * factor) if opens else gram_in[at(i), at(j)]
        gram[at(i), at(j)] = values
        put(first, i, j, values)
    for step in range(steps):
        for i, j in tiles:
            square = tile_of(first, first, i, j)
            put(second, i, j, square)
            held = gram[at(i), at(j)]
            poly = COEF_B * held + COEF_C * square
            put(polys.at[step], i, j, jnp.where(eye(TILE, TILE), COEF_A, 0.0) + poly if i == j else poly)
            gram[at(i), at(j)] = COEF_A * held + COEF_B * square
        for i, j in tiles:
            put(third, i, j, gram[at(i), at(j)] + COEF_C * tile_of(second, first, i, j))
        for i, j in tiles:
            values = tile_of(third, polys.at[step], i, j)
            gram[at(i), at(j)] = values
            put(first, i, j, values)
    if not closes:
        for i, j in tiles:
            gram_out[at(i), at(j)] = gram[at(i), at(j)]
        return
    picked = picked_ref[...]
    held = [jnp.dot(picked, first[k], preferred_element_type=F32) for k in range(2)]
    rows = COEF_A * picked.astype(F32) + COEF_B * (held[0] + held[1])
    rows = rows + COEF_C * product([part.astype(BF) for part in held], [first[0], first[1]])
    chain = [(ref, k) for ref in before for k in range(ref.shape[0])]
    chain += [(polys, k) for k in range(steps)]
    for ref, k in reversed(chain):
        rows = product(split(rows, 2), [ref[k, 0], ref[k, 1]])
    rows_ref[...] = rows * factor


def newton_call(opens, closes, steps, micros, operands, picked, width):
    pair = pltpu.VMEM((2, width, width), BF)
    whole = pl.BlockSpec(memory_space=pltpu.VMEM)
    out_shape = []
    if closes:
        operands = operands + [picked]
        out_shape.append(jax.ShapeDtypeStruct(picked.shape, F32))
    else:
        out_shape.append(jax.ShapeDtypeStruct((width, width), F32))
        if opens:
            out_shape.append(jax.ShapeDtypeStruct((SUBLANES, LANES), F32))
        out_shape.append(jax.ShapeDtypeStruct((steps, 2, width, width), BF))
    kept = [pltpu.VMEM((steps, 2, width, width), BF)] if closes and steps else []
    return pl.pallas_call(
        functools.partial(newton_kernel, opens, closes, steps),
        out_shape=out_shape,
        in_specs=([pl.BlockSpec(memory_space=pltpu.SMEM)] if opens else [])
        + [whole] * (len(operands) - opens),
        out_specs=[whole] * len(out_shape),
        scratch_shapes=kept + [pltpu.VMEM((width, width), F32), pair, pair, pair],
        compiler_params=pltpu.CompilerParams(vmem_limit_bytes=VMEM_BYTES),
        cost_estimate=lasting(micros),
    )(*operands)


def newton_rows(pack, other, picked):
    low = scalars(lax.axis_index("head") % 2)
    return newton_call(True, True, NS_STEPS - 1, 30, [low, pack, other], picked, pack.shape[1])[0]


def newton_opening(pack, other):
    low = scalars(lax.axis_index("head") % 2)
    return newton_call(True, False, 2, 15, [low, pack, other], None, pack.shape[1])


def newton_closing(opening, picked):
    return newton_call(False, True, NS_STEPS - 3, 18, list(opening), picked, picked.shape[1])[0]


def gram_kernel(cols, low_ref, extras_ref, *refs):
    sent_ref, kept_ref = refs[-1], refs[-2]
    refs = refs[:-2]
    width = refs[0].shape[0]
    terms = []
    for (left, right), ref in zip(cols, refs):
        piece = ref[:, left : -(-right // LANES) * LANES]
        lane = lax.broadcasted_iota(jnp.int32, piece.shape, 1)
        terms.append(split(jnp.where(lane < right - left, piece, 0.0), 2))

    def strip(i):
        return sum(
            product([part[at(i)] for part in term], [part[i:] for part in term], ROWS_OF_BOTH)
            for term in terms
        )

    packs = (strip(0), jnp.concatenate([strip(TILE), strip(2 * TILE)], axis=1))
    low = low_ref[0]
    kept_ref[:TILE] = jnp.where(low == 0, packs[0], packs[1])
    sent_ref[:TILE] = jnp.where(low == 0, packs[1], packs[0])
    extras = extras_ref[...]
    if extras.shape[1] < width:
        rows = extras[-2 * (width // LANES) - 1 : -1].reshape(2, -1, LANES)
        rows = [jnp.concatenate([rows[k, j : j + 1] for j in range(width // LANES)], 1) for k in (0, 1)]
        extras = jnp.concatenate(rows + [jnp.zeros((SUBLANES - 2, width), F32)], axis=0)
    kept_ref[TILE:] = extras
    sent_ref[TILE:] = extras


def gram_packs(pieces, extras):
    width = pieces[0][0].shape[0]
    return stage(
        functools.partial(gram_kernel, [piece[1:] for piece in pieces]),
        [shaped((TILE + SUBLANES, width))] * 2,
        [scalars(lax.axis_index("head") % 2), extras] + [piece[0] for piece in pieces],
        smem=1,
    )


def per_device(
    inputs,
    lengths,
    norm_gain,
    in_proj,
    conv_weight,
    conv_bias,
    head_params,
    gate_gain,
    out_proj,
    cotangent,
    norm_gain_mom,
    in_proj_mom,
    conv_weight_mom,
    conv_bias_mom,
    head_params_mom,
    gate_gain_mom,
    out_proj_mom,
):
    members, extent, model_width = inputs.shape
    seq_count = lax.axis_size("seq")
    head_count = lax.axis_size("head")
    seq_place = lax.axis_index("seq")
    head_place = lax.axis_index("head")
    heads_here = head_params.shape[1]
    head_span = gate_gain.shape[0]
    head_size = head_span // heads_here
    channels = conv_bias.shape[0]
    state_size = (channels - head_span) * head_count // 2
    inner_all = head_span * head_count
    group_cols = in_proj.shape[1]
    proj_all = group_cols * head_count
    tap_count = conv_weight.shape[0]
    share = model_width // seq_count
    tokens = members * extent
    quarter = extent // head_count
    runs = seq_count // members

    def own_blocks(blocks):
        return lax.dynamic_slice_in_dim(blocks, head_place * quarter, quarter, 1)

    def own(per_token):
        return pick(per_token.reshape((members, head_count, quarter, -1)), head_place, 1)

    run_place = seq_place // members
    length = lengths[seq_place % members]
    first_slot = run_place * tokens
    place = scalars(length, first_slot, head_place)
    in_low = in_proj.astype(BF)
    out_low = out_proj.astype(BF)
    x_end = 2 * head_span
    bc_end = head_span + channels
    bc_count = channels - head_span
    halo = tap_count - 1
    side_cols = -(-(group_cols - x_end) // LANES) * LANES
    small_rows = SUBLANES * (head_span // LANES + 3) + head_span // LANES + 2 * (model_width // LANES) + 1
    data_piece = own_blocks(inputs)
    data_piece = spread(data_piece, members)
    cot_sent = cotangent.reshape(members, 2, 2, quarter, model_width)
    cot_sent = pick(cot_sent, head_place % 2, 2)
    decay_rate = -jnp.exp(head_params[1])[:, None]

    def from_run(edge, step):
        pairs = [(i, i + step) for i in range(seq_count) if 0 <= i + step < seq_count]
        return lax.ppermute(edge, "seq", pairs)

    side_weight = jnp.pad(in_low[:, x_end:], ((0, 0), (0, side_cols - (group_cols - x_end)))).T
    weight_cols = jnp.concatenate([conv_weight[:, head_span:], conv_bias[None, head_span:]], axis=0).T
    weight_cols = jnp.pad(weight_cols, ((0, 0), (0, LANES - tap_count - 1)))
    params = jnp.stack([head_params[0], decay_rate[:, 0]], axis=1)
    params = jnp.pad(params, ((0, SUBLANES - heads_here), (0, LANES - 2)))
    x_weight = conv_weight[:, :head_span]
    skip = jnp.repeat(head_params[2], head_size)[None]
    out_turned = out_low.T
    (
        data_piece, cot_sent, side_weight, weight_cols, params, in_low, out_low, out_turned, place, skip,
    ) = apart_from_here(
        data_piece, cot_sent, side_weight, weight_cols, params, in_low, out_low, out_turned, place, skip,
    )
    cot_mine = spread(cot_sent, members)
    across = flip(data_piece, "head", 2)
    corner = flip(across, "head", 1)
    beside = flip(data_piece, "head", 1)
    pieces = [data_piece, beside, across, corner]
    x_halo = jnp.zeros((SUBLANES, head_span), F32)
    bc_halo = jnp.zeros((bc_count, LANES), F32)
    if runs > 1:
        ends = gather_head(data_piece, 1).reshape(tokens, model_width)[tokens - SUBLANES :].astype(F32)
        ends = ends * lax.rsqrt(jnp.mean(ends * ends, axis=-1, keepdims=True) + EPSILON) * norm_gain
        ends = jnp.dot(ends.astype(BF), in_low[:, head_span:bc_end], preferred_element_type=F32)
        ends = from_run(ends.astype(BF), members).astype(F32)
        x_halo = ends[:, :head_span]
        bc_halo = jnp.pad(ends[:, head_span:].T, ((0, 0), (LANES - SUBLANES, 0)))
    data_low, lowered, root_scale, bc_own, bc_conv, bc_in, rows = enter(
        head_place, pieces, norm_gain[None], side_weight, weight_cols, bc_halo, params, tap_count, heads_here,
        bc_count,
    )
    bc_own, lowered = apart_from_here(bc_own, lowered)
    bc_across = flip(bc_own, "head", 2)
    bc_beside = flip(bc_own, "head", 1)
    z_part, x_in, x_conv = z_and_x(
        lowered, in_low, x_weight, conv_bias[None, :head_span], x_halo, members
    )
    bc_across, bc_beside, cot_mine, z_part = apart_from_here(bc_across, bc_beside, cot_mine, z_part)
    bc_corner = flip(bc_across, "head", 1)
    cot_pieces = [cot_mine, flip(cot_mine, "head", 1)]
    bc_pieces = [bc_own, bc_beside, bc_across, bc_corner]
    step_sizes = rows[:heads_here]
    growth = jnp.repeat(jnp.exp(jnp.sum(step_sizes * decay_rate, axis=1)), head_size)[None]
    gain = gate_gain[None]

    def scan_from(start):
        return forward_scan(
            place, x_conv, z_part, bc_pieces, rows, skip, gain, out_low, cot_pieces, start, head_size, members
        )

    start = jnp.zeros((state_size, head_span), F32)
    if runs > 1:
        start = entering(growth, scan_from(start)[2], members, False)
    mixed, states, state_end, gated_low, partial_kept, partial_sent, sums, bc_full, cot = scan_from(start)
    sums, partial_sent, cot_mine = apart_from_here(sums, partial_sent, cot_mine)
    cot_piece = pick(cot_mine, head_place // 2, 1)
    partial_come = flip(partial_sent, "head", 1)
    sums, lowered = apart_from_here(added(sums, flip(sums, "head", 1)), lowered)
    sums_come, turned_lowered = apart_from_here(flip(sums, "head", 2), lowered.T)
    norm_rows = stage(
        functools.partial(norm_kernel, inner_all), shaped(sums.shape), [sums, sums_come]
    )
    norm_scale = norm_rows[0]
    grad_mixed, grad_z, grad_summed, gate_gain_grad = gate_back(
        place, cot, norm_rows, z_part, mixed, gain, out_turned, inner_all, members
    )
    low, high = head_place % 2, head_place // 2


    def come_rows(blocks):
        return lax.all_to_all(blocks.reshape((seq_count, share, -1)), "seq", 0, 0, tiled=True)

    early_sent = jnp.concatenate(
        [
            jnp.dot(grad_summed.T, gated_low, preferred_element_type=F32),
            jnp.dot(turned_lowered, grad_z, preferred_element_type=F32),
        ],
        axis=1,
    ).astype(BF)
    slots = first_slot + lax.broadcasted_iota(jnp.int32, (tokens, 1), 0)
    valid_mask = own((slots < length).astype(F32))
    norm_piece = own(norm_scale)
    root_piece = own(root_scale)
    early_old = jnp.concatenate([out_proj_mom.T, in_proj_mom[:, :head_span]], axis=1)
    in_low_wide = jnp.pad(in_low, ((0, 0), (0, x_end + side_cols - group_cols))).T
    late_old = jnp.pad(in_proj_mom[:, head_span:], ((0, 0), (0, x_end + side_cols - group_cols)))
    (
        grad_mixed, early_sent, valid_mask, norm_piece, root_piece, early_old, weight_cols, in_low_wide, late_old,
        turned_lowered, root_scale,
    ) = apart_from_here(
        grad_mixed, early_sent, valid_mask, norm_piece, root_piece, early_old, weight_cols, in_low_wide, late_old,
        turned_lowered, root_scale,
    )
    early_come = come_rows(early_sent)

    def scan_back(back, edge):
        return backward_scan(
            low, grad_mixed, x_conv, x_in, bc_full, rows, states, state_end, skip, x_weight,
            decay_rate, back, edge, head_size, members,
        )

    back = jnp.zeros_like(state_end)
    edge = jnp.zeros((SUBLANES, head_span), F32)
    if runs > 1:
        back = entering(growth, scan_back(back, edge)[3], members, True)
        edge = from_run(scan_back(back, edge)[4], -members)
    grad_x_in, bc_kept, bc_sent, _, _, small, grad_pre, head_sums_out = scan_back(back, edge)

    bc_sent, grad_x_in, bc_kept, early_come = apart_from_here(
        bc_sent, grad_x_in, bc_kept, early_come
    )
    bc_come = flip(bc_sent, "head", 1)
    early_rows, early_mom = rows_step([early_come], early_old, micros=20)
    early_mom, bc_kept = apart_from_here(early_mom, bc_kept)
    full_early = whole_rows(early_mom)
    bc_shape = (2, bc_kept.shape[0] // 2, tokens)
    bc_kept, bc_sent = split_halves(bc_kept.reshape(bc_shape), bc_come.reshape(bc_shape), 0, high)
    bc_kept, bc_sent, grad_x_in = apart_from_here(bc_kept, bc_sent, grad_x_in)
    bc_come = flip(bc_sent, "head", 2)
    x_sent = weight_grad(turned_lowered, grad_x_in)
    x_sent, bc_kept = apart_from_here(x_sent, bc_kept)

    halo_cols = jnp.zeros((bc_in.shape[0], LANES), F32)
    if runs > 1:
        first = (bc_kept[:, :halo] + bc_come[:, :halo].astype(F32)) * silu_slope(bc_conv[:, :halo])
        first = from_run(first.astype(BF), -members).astype(F32)
        halo_cols = jnp.pad(first, ((0, 0), (0, LANES - halo)))
    grad_side, bc_small, late_sent = stage(
        functools.partial(side_kernel, tap_count),
        [
            shaped((tokens, side_cols), BF),
            shaped((bc_in.shape[0], LANES)),
            shaped((model_width, head_span + side_cols), BF),
        ],
        [bc_kept, bc_come, bc_conv, bc_in, weight_cols, halo_cols, grad_pre, turned_lowered, x_sent],
    )
    late_sent, grad_side, partial_kept, partial_come = apart_from_here(
        late_sent, grad_side, partial_kept, partial_come
    )
    late_come = come_rows(late_sent)

    summed_kept, summed_sent = split_halves(partial_kept, partial_come, 0, high)
    summed_kept, summed_sent, grad_side = apart_from_here(summed_kept, summed_sent, grad_side)
    summed_come = flip(summed_sent, "head", 2)
    lowered_kept, lowered_sent, norm_gain_grad = lowered_grad(
        low, grad_z, grad_x_in, grad_side, in_low_wide, data_low, root_scale, members
    )
    lowered_kept, lowered_sent, summed_kept = apart_from_here(lowered_kept, lowered_sent, summed_kept)
    lowered_come = flip(lowered_sent, "head", 1)
    lowered_kept, lowered_sent = split_halves(lowered_kept, lowered_come, 1, high)
    lowered_kept, lowered_sent, summed_kept = apart_from_here(lowered_kept, lowered_sent, summed_kept)
    lowered_come = flip(lowered_sent, "head", 2)
    result, result_squares = stage(
        result_kernel,
        [shaped(data_piece.shape, BF), shaped((1, model_width))],
        [summed_kept, summed_come, data_piece, norm_piece, valid_mask],
    )
    small_blocks = -(-small_rows // share)
    small_sums = stage(
        small_kernel,
        shaped((small_blocks * share, LANES)),
        [small, bc_small, head_sums_out, gate_gain_grad, norm_gain_grad, result_squares],
    )
    small_sums = jnp.moveaxis(small_sums.reshape(small_blocks, share, LANES), 0, 1).reshape(share, -1)
    late_come, small_sums, result, lowered_kept = apart_from_here(
        late_come, small_sums, result, lowered_kept
    )

    late_rows, late_mom = rows_step([late_come], late_old, small_sums)
    late_mom, lowered_kept = apart_from_here(late_mom, lowered_kept)
    full_late = whole_rows(late_mom)
    full_early, lowered_kept = apart_from_here(full_early, lowered_kept)

    no_extras = jnp.zeros((SUBLANES, model_width), F32)
    row_count = -(-share // (2 * SUBLANES)) * 2 * SUBLANES
    picked = seq_place * share + lax.broadcasted_iota(jnp.int32, (row_count, model_width), 0)
    picked = (picked == lax.broadcasted_iota(jnp.int32, picked.shape, 1)).astype(BF)
    pack, pack_sent = gram_packs([(full_early, 0, head_span)], no_extras)
    pieces = stage(
        input_kernel,
        shaped((members, 2 * quarter, model_width), BF),
        [
            lowered_kept, lowered_come, data_piece, cot_piece, root_piece, valid_mask, norm_gain[None, None],
            result,
        ],
    )
    pack, pack_sent, pieces = apart_from_here(pack, pack_sent, pieces)
    pack, picked = apart_from_here(added(pack, flip(pack_sent, "head", 1)), picked)
    pack_come = flip(pack, "head", 2)
    pack, pieces = apart_from_here(pack, pieces)
    pieces = spread(pieces, members)
    pack = added(pack, pack_come)
    opening = newton_opening(pack, flip(pack, "head", 1))
    full_late, opening = apart_from_here(full_late, opening)
    small_sums = full_late[:, full_late.shape[1] - small_blocks * LANES :]
    small_sums = jnp.sum(small_sums.reshape(seq_count, share, -1), axis=0)
    small_sums = jnp.moveaxis(small_sums.reshape(share, small_blocks, LANES), 1, 0)
    small_sums = small_sums.reshape(-1, LANES)[:small_rows]
    late_used = group_cols - head_span
    pack, pack_sent = gram_packs(
        [(full_early, head_span, 2 * head_span), (full_late, 0, late_used)], small_sums
    )
    pack, opening = apart_from_here(added(pack, flip(pack_sent, "head", 1)), opening)
    pack_come = flip(pack, "head", 2)
    turn_out = newton_closing(opening, picked)
    pack, turn_out, pieces = apart_from_here(pack, turn_out, pieces)
    pack, pieces = apart_from_here(added(pack, pack_come), pieces)
    beside, across = flip(pieces, "head", 1), flip(pieces, "head", 2)
    turn_in = newton_rows(pack, flip(pack, "head", 1), picked)
    turn_in, across, beside, small_sums = apart_from_here(turn_in, across, beside, small_sums)
    corner = flip(across, "head", 1)
    turn_in, turn_out = turn_in[:share], turn_out[:share]

    taps_rows = SUBLANES * (head_span // LANES)
    x_small = small_sums[:taps_rows].reshape(-1, SUBLANES, LANES)
    x_small = jnp.moveaxis(x_small, 0, 1).reshape(SUBLANES, head_span)
    bc_small = small_sums[taps_rows : taps_rows + SUBLANES, : channels - head_span]
    both_small = jnp.concatenate([x_small, bc_small], axis=1)
    conv_weight_grad, conv_bias_grad = both_small[:tap_count], both_small[tap_count]
    head_rows = jnp.sum(
        small_sums[taps_rows + SUBLANES : taps_rows + 3 * SUBLANES].reshape(2, SUBLANES, LANES), axis=2
    )[:, :heads_here]
    head_params_grad = jnp.stack(
        [
            head_rows[0],
            head_rows[1] * decay_rate[:, 0],
            jnp.sum(x_small[tap_count + 1].reshape(heads_here, head_size), axis=1),
        ]
    )
    gate_row = taps_rows + 3 * SUBLANES
    gate_gain_grad = small_sums[gate_row : gate_row + head_span // LANES].reshape(-1)
    norm_gain_grad, squares_all = pack[TILE], jnp.sum(pack[TILE + 1])

    out_grad_rows = early_rows[:, :head_span]
    out_rows_mom = early_mom[:, :head_span]
    in_proj_grad = jnp.concatenate(
        [early_rows[:, head_span:], late_rows[:, :late_used]], axis=1
    )
    in_proj_mom_new = jnp.concatenate([early_mom[:, head_span:], late_mom[:, :late_used]], axis=1)

    def turned(turn, matrix):
        return jnp.dot(turn, matrix, precision=lax.Precision.HIGH, preferred_element_type=F32)

    rows_early, rows_late = full_early, full_late[:, : x_end + side_cols - head_span]
    rows_out = turned(turn_out, rows_early[:, :head_span])
    rows_in = jnp.concatenate(
        [turned(turn_in, rows_early[:, head_span:]), turned(turn_in, rows_late)], axis=1
    )[:, :group_cols]
    output, input_grad = in_order(head_place, [pieces, beside, across, corner])
    rms = jnp.sqrt(squares_all / (jnp.sum(lengths).astype(F32) * model_width))
    in_old_rows = lax.dynamic_slice_in_dim(in_proj, seq_place * share, share, 0)
    in_proj_new = in_old_rows - MUON_RATE * 0.2 * math.sqrt(max(model_width, proj_all)) * rows_in
    out_old_cols = lax.dynamic_slice_in_dim(out_proj, seq_place * share, share, 1)
    out_proj_new = (
        out_old_cols - MUON_RATE * 0.2 * math.sqrt(max(inner_all, model_width)) * rows_out.T
    )
    divisor = math.sqrt(members * extent * seq_count)
    norm_gain_mom_new = 0.5 * norm_gain_mom + norm_gain_grad
    conv_weight_mom_new = 0.5 * conv_weight_mom + conv_weight_grad
    conv_bias_mom_new = 0.5 * conv_bias_mom + conv_bias_grad
    head_params_mom_new = 0.5 * head_params_mom + head_params_grad
    gate_gain_mom_new = 0.5 * gate_gain_mom + gate_gain_grad
    norm_gain_new = norm_gain - SMALL_RATE * norm_gain_mom_new / divisor
    conv_weight_new = conv_weight - SMALL_RATE * conv_weight_mom_new / divisor
    conv_bias_new = conv_bias - SMALL_RATE * conv_bias_mom_new / divisor
    head_params_new = head_params - SMALL_RATE * head_params_mom_new / divisor
    gate_gain_new = gate_gain - SMALL_RATE * gate_gain_mom_new / divisor
    return (
        output,
        input_grad,
        norm_gain_grad,
        in_proj_grad,
        conv_weight_grad,
        conv_bias_grad,
        head_params_grad,
        gate_gain_grad,
        out_grad_rows.T,
        norm_gain_mom_new,
        in_proj_mom_new,
        conv_weight_mom_new,
        conv_bias_mom_new,
        head_params_mom_new,
        gate_gain_mom_new,
        out_rows_mom.T,
        norm_gain_new,
        in_proj_new,
        conv_weight_new,
        conv_bias_new,
        head_params_new,
        gate_gain_new,
        out_proj_new,
        rms,
    )


def solution(mesh):
    return jax.shard_map(
        per_device,
        mesh=mesh,
        in_specs=(
            P(None, "seq", None),
            P(),
            P(),
            P(None, "head"),
            P(None, "head"),
            P("head"),
            P(None, "head"),
            P("head"),
            P("head", None),
            P(None, "seq", None),
            P(),
            P("seq", "head"),
            P(None, "head"),
            P("head"),
            P(None, "head"),
            P("head"),
            P("head", "seq"),
        ),
        out_specs=(
            P(None, "seq", None),
            P(None, "seq", None),
            P(),
            P("seq", "head"),
            P(None, "head"),
            P("head"),
            P(None, "head"),
            P("head"),
            P("head", "seq"),
            P(),
            P("seq", "head"),
            P(None, "head"),
            P("head"),
            P(None, "head"),
            P("head"),
            P("head", "seq"),
            P(),
            P("seq", "head"),
            P(None, "head"),
            P("head"),
            P(None, "head"),
            P("head"),
            P("head", "seq"),
            P(),
        ),
        check_vma=False,
    )
```
